32 devices in a mesh: dp: 16 (over z, y, core), fsdp: 2 (over x).
Axes of the slice: x: 2, y: 2, z: 4, core: 2. Of those that a mesh axis runs over, the one named last changes fastest.
Arguments:
- coarse_clips: bfloat16 [128, 8, 8, 1024], P(('dp', 'fsdp')), may hold values from -6 to 6
- medium_clips: bfloat16 [128, 12, 12, 1024], P(('dp', 'fsdp')), may hold values from -6 to 6
- fine_clips: bfloat16 [128, 14, 14, 1024], P(('dp', 'fsdp')), may hold values from -6 to 6
- clip_counts: int32 [32, 3], P(('dp', 'fsdp')), may hold values from 0 to 1, as said below
- frame_counts: int32 [32, 3], P(('dp', 'fsdp')), may hold values from 2 to 4, as said below
- reduce_one: float32 [1024, 512], P(('dp', 'fsdp')), may hold values from -0.1875 to 0.1875
- spatial_one: float32 [4608, 512], P(('dp', 'fsdp')), may hold values from -0.09375 to 0.09375
- expand_one: float32 [512, 2048], P(('dp', 'fsdp')), may hold values from -0.25 to 0.25
- shortcut_one: float32 [1024, 2048], P(('dp', 'fsdp')), may hold values from -0.1875 to 0.1875
- reduce_two: float32 [2048, 512], P(('dp', 'fsdp')), may hold values from -0.125 to 0.125
- excite_down: float32 [512, 32], P(('dp', 'fsdp')), may hold values from -0.25 to 0.25
- excite_up: float32 [32, 512], P(None, ('dp', 'fsdp')), may hold values from -4 to 4
- temporal_mix: float32 [27, 16384], P(None, ('dp', 'fsdp')), may hold values from -0.1875 to 0.1875
- expand_two: float32 [512, 2048], P(('dp', 'fsdp')), may hold values from -0.25 to 0.25
- norm_params: float32 [2, 8192], P(None, ('dp', 'fsdp')), may hold values from -1 to 1.5, as said below
- motion_kernel: float32 [9, 32], replicated, may hold values from -1.5 to 1.5
- coarse_cot: bfloat16 [128, 4, 4, 2048], P(('dp', 'fsdp')), may hold values from -6 to 6
- medium_cot: bfloat16 [128, 6, 6, 2048], P(('dp', 'fsdp')), may hold values from -6 to 6
- fine_cot: bfloat16 [128, 7, 7, 2048], P(('dp', 'fsdp')), may hold values from -6 to 6
Outputs:
- coarse_out: bfloat16 [128, 4, 4, 2048], P(('dp', 'fsdp'))
- medium_out: bfloat16 [128, 6, 6, 2048], P(('dp', 'fsdp'))
- fine_out: bfloat16 [128, 7, 7, 2048], P(('dp', 'fsdp'))
- coarse_input_grad: bfloat16 [128, 8, 8, 1024], P(('dp', 'fsdp'))
- medium_input_grad: bfloat16 [128, 12, 12, 1024], P(('dp', 'fsdp'))
- fine_input_grad: bfloat16 [128, 14, 14, 1024], P(('dp', 'fsdp'))
- reduce_one_grad: float32 [1024, 512], P(('dp', 'fsdp'))
- spatial_one_grad: float32 [4608, 512], P(('dp', 'fsdp'))
- expand_one_grad: float32 [512, 2048], P(('dp', 'fsdp'))
- shortcut_one_grad: float32 [1024, 2048], P(('dp', 'fsdp'))
- reduce_two_grad: float32 [2048, 512], P(('dp', 'fsdp'))
- excite_down_grad: float32 [512, 32], P(('dp', 'fsdp'))
- excite_up_grad: float32 [32, 512], P(None, ('dp', 'fsdp'))
- temporal_mix_grad: float32 [27, 16384], P(None, ('dp', 'fsdp'))
- expand_two_grad: float32 [512, 2048], P(('dp', 'fsdp'))
- norm_params_grad: float32 [2, 8192], P(None, ('dp', 'fsdp'))
- motion_kernel_grad: float32 [9, 32], replicated
The draws below stay inside these ranges and needn't reach their ends.
Inputs may be any that keep to these rules, and one draw needn't show every extreme that they name: `clip_counts`: in every group some device has 1 live clips. `frame_counts`: in every group some slot has 4 live frames. `norm_params`: row 0 gains, row 1 biases.
All inputs are finite; a program needn't handle non-finite values.
Results may differ from the reference program's by a relative error of at most 0.017.
The reference program's roundings to bfloat16 on the way count: a program that leaves them out, or rounds other values in their place, can miss the bound.
Values may be sent and summed in bfloat16 or wider, within the bound.
No kernel may reach another device: no remote copies, remote signals or barrier semaphores. Data moves between devices by JAX's collectives and lax.ppermute only.
A program may use at most 320 MiB of HBM per device.

```python
import jax
import jax.numpy as jnp
from jax import lax

C_IN = 1024
MID = 512
C_OUT = 2048
SQUEEZE = 32
FRAMES = 4
SIDE_A = 4
SIDE_B = 6
SIDE_C = 7
CLIPS = 1
GROUP = 128
SHIFT = 16
NORMS = 8192
SHARDS = 32
SLOTS = 32


def draw_clip_counts(key, part):
    key = jax.random.fold_in(key, 11)
    base_key, pick_key = jax.random.split(key)
    counts = jnp.minimum(jax.random.randint(base_key, (SHARDS, 3), 0, 2 * CLIPS + 1), CLIPS)
    chosen = jax.random.randint(pick_key, (1, 3), 0, SHARDS)
    rows = jnp.arange(SHARDS)[:, None]
    return jnp.where(rows == chosen, CLIPS, counts).astype(jnp.int32)


def draw_frame_counts(key, part):
    key = jax.random.fold_in(key, 23)
    base_key, pick_key = jax.random.split(key)
    counts = jax.random.randint(base_key, (SLOTS, 3), FRAMES // 2, FRAMES + 1)
    chosen = jax.random.randint(pick_key, (1, 3), 0, SLOTS)
    rows = jnp.arange(SLOTS)[:, None]
    return jnp.where(rows == chosen, FRAMES, counts).astype(jnp.int32)


def draw_norm_params(key, part):
    key = jax.random.fold_in(key, 37)
    gain_key, bias_key = jax.random.split(key)
    gain_row = jax.random.uniform(gain_key, (NORMS,), jnp.float32, 0.5, 1.5)
    biases = jnp.clip(0.3 * jax.random.normal(bias_key, (NORMS,), jnp.float32), -1.0, 1.0)
    return jnp.stack([gain_row, biases]).astype(jnp.float32)


def block_levels(own_key, extent, cuts, least, high):
    factor_of = 1.0
    for axis_at, parts in cuts:
        draws = jax.random.uniform(jax.random.fold_in(jax.random.fold_in(own_key, 6), axis_at), (parts,), jnp.float32, least / len(cuts), high / len(cuts))
        factor_of = factor_of * jnp.repeat(jnp.exp(draws), extent[axis_at] // parts).reshape((-1,) + (1,) * (len(extent) - 1 - axis_at))
    return factor_of


def gaussian(key, shape, width, limit, shards=(), kind=jnp.bfloat16):
    drawn = width * jax.random.normal(key, shape, jnp.float32)
    if shards:
        drawn = drawn * block_levels(key, shape, shards, -0.22, 0.18)
    return jnp.clip(drawn, -limit, limit).astype(kind)


def setup_inputs(seed: int = 0) -> dict:
    key_list = jax.random.split(jax.random.key(seed), 20)
    return {
        "coarse_clips": gaussian(key_list[0], (SLOTS * FRAMES, 2 * SIDE_A, 2 * SIDE_A, C_IN), 1.0, 6.0, ((0, 32),)),
        "medium_clips": gaussian(key_list[1], (SLOTS * FRAMES, 2 * SIDE_B, 2 * SIDE_B, C_IN), 1.0, 6.0, ((0, 32),)),
        "fine_clips": gaussian(key_list[2], (SLOTS * FRAMES, 2 * SIDE_C, 2 * SIDE_C, C_IN), 1.0, 6.0, ((0, 32),)),
        "clip_counts": draw_clip_counts(jax.random.fold_in(key_list[19], 71), 0),
        "frame_counts": draw_frame_counts(jax.random.fold_in(key_list[19], 71), 0),
        "reduce_one": gaussian(key_list[5], (C_IN, MID), C_IN ** -0.5, 0.1875, ((0, 32),), jnp.float32),
        "spatial_one": gaussian(key_list[6], (9 * MID, MID), (9 * MID) ** -0.5, 0.09375, ((0, 32),), jnp.float32),
        "expand_one": gaussian(key_list[7], (MID, C_OUT), MID ** -0.5, 0.25, ((0, 32),), jnp.float32),
        "shortcut_one": gaussian(key_list[8], (C_IN, C_OUT), C_IN ** -0.5, 0.1875, ((0, 32),), jnp.float32),
        "reduce_two": gaussian(key_list[9], (C_OUT, MID), C_OUT ** -0.5, 0.125, ((0, 32),), jnp.float32),
        "excite_down": gaussian(key_list[10], (MID, SQUEEZE), MID ** -0.5, 0.25, ((0, 32),), jnp.float32),
        "excite_up": gaussian(key_list[11], (SQUEEZE, MID), 2 ** -0.5, 4.0, ((1, 32),), jnp.float32),
        "temporal_mix": gaussian(key_list[12], (27, GROUP * GROUP), (9 * GROUP) ** -0.5, 0.1875, ((1, 32),), jnp.float32),
        "expand_two": gaussian(key_list[13], (MID, C_OUT), MID ** -0.5, 0.25, ((0, 32),), jnp.float32),
        "norm_params": draw_norm_params(jax.random.fold_in(key_list[19], 71), 0),
        "motion_kernel": gaussian(key_list[15], (9, SQUEEZE), 0.3, 1.5, (), jnp.float32),
        "coarse_cot": gaussian(key_list[16], (SLOTS * FRAMES, SIDE_A, SIDE_A, C_OUT), 1.0, 6.0, ((0, 32),)),
        "medium_cot": gaussian(key_list[17], (SLOTS * FRAMES, SIDE_B, SIDE_B, C_OUT), 1.0, 6.0, ((0, 32),)),
        "fine_cot": gaussian(key_list[18], (SLOTS * FRAMES, SIDE_C, SIDE_C, C_OUT), 1.0, 6.0, ((0, 32),)),
    }


@jax.custom_vjp
def low(v):
    return lax.optimization_barrier(v.astype(jnp.bfloat16)).astype(jnp.float32)

@jax.custom_vjp
def low_back(v):
    return v

def low_keep(v):
    return (low(v), None)

def low_pass(kept, grad):
    return (grad,)

def back_keep(v):
    return (v, None)

def back_low(kept, grad):
    return (low(grad),)
low.defvjp(low_keep, low_pass)
low_back.defvjp(back_keep, back_low)
epsilon = 1e-05
highest = lax.Precision.HIGHEST

def sigmoid_linear(values):
    return values * jax.nn.sigmoid(values)

def pointwise(inputs, weight):
    return jnp.einsum('bhwc,cd->bhwd', inputs, weight, precision=highest)

def conv_spatial(inputs, kernel, stride):
    return lax.conv_general_dilated(inputs, kernel, (stride, stride), ((1, 1), (1, 1)), dimension_numbers=('NHWC', 'HWIO', 'NHWC'), precision=highest)

def local_sums(values, masks):
    sum_first = jnp.zeros((values[0].shape[-1],), jnp.float32)
    sum_second = jnp.zeros((values[0].shape[-1],), jnp.float32)
    for tensor, live_mask in zip(values, masks):
        sum_first = sum_first + lax.optimization_barrier(jnp.sum(tensor * live_mask, axis=(0, 1, 2)))
        sum_second = sum_second + lax.optimization_barrier(jnp.sum(tensor * tensor * live_mask, axis=(0, 1, 2)))
    return (sum_first, sum_second)

def norm_apply(tensor, sum_first, sum_second, total_count, gain_row, biases):
    center = sum_first / total_count
    spread = sum_second / total_count - center * center
    return (tensor - center) * lax.rsqrt(spread + epsilon) * gain_row + biases

def norm_act(values, masks, total_count, gain_row, biases):
    sum_first, sum_second = local_sums(values, masks)
    return [live_mask * sigmoid_linear(norm_apply(tensor, sum_first, sum_second, total_count, gain_row, biases)) for tensor, live_mask in zip(values, masks)]

def shift_frames(values, frames, channels_moved):
    layout = values.shape
    blocks = values.reshape((-1, frames) + layout[1:])
    earlier = jnp.pad(blocks[:, :-1], ((0, 0), (1, 0), (0, 0), (0, 0), (0, 0)))
    later_frames = jnp.pad(blocks[:, 1:], ((0, 0), (0, 1), (0, 0), (0, 0), (0, 0)))
    joined = jnp.concatenate([earlier[..., :channels_moved], later_frames[..., channels_moved:2 * channels_moved], blocks[..., 2 * channels_moved:]], axis=-1)
    return joined.reshape(layout)

def next_frame(values, frames):
    layout = values.shape
    blocks = values.reshape((-1, frames) + layout[1:])
    later_frames = jnp.pad(blocks[:, 1:], ((0, 0), (0, 1), (0, 0), (0, 0), (0, 0)))
    return later_frames.reshape(layout)

def depthwise(values, kernel):
    padded = jnp.pad(values, ((0, 0), (1, 1), (1, 1), (0, 0)))
    rows_out = values.shape[1]
    cols_out = values.shape[2]
    summed = jnp.zeros(values.shape, jnp.float32)
    for tap_id in range(9):
        row_start, col_start = divmod(tap_id, 3)
        summed = summed + padded[:, row_start:row_start + rows_out, col_start:col_start + cols_out, :] * kernel[tap_id]
    return summed

def excite(features, squeezed, up_weight, kernel, next_masks, frames):
    gated_all = []
    for feature_one, squeezed_one, next_mask in zip(features, squeezed, next_masks):
        motion = next_mask * (depthwise(next_frame(squeezed_one, frames), kernel) - squeezed_one)
        pooled = lax.optimization_barrier(jnp.mean(motion, axis=(1, 2)))
        logits = jnp.dot(pooled, up_weight, precision=highest)
        gated_all.append(feature_one * (0.5 + jax.nn.sigmoid(logits))[:, None, None, :])
    return gated_all

def forward(clips, weights, kernel, masks, next_masks, count_in, count_out):
    reduce_one, spatial_one, expand_one, shortcut_one, reduce_two, excite_down, excite_up, temporal_mix, expand_two, norm_params = [low(weight) for weight in weights]
    bounds = [0, MID, 2 * MID, 2 * MID + C_OUT, 2 * MID + 2 * C_OUT, 3 * MID + 2 * C_OUT, 4 * MID + 2 * C_OUT, 4 * MID + 3 * C_OUT]
    gain_segs = [norm_params[0, bounds[seg_id]:bounds[seg_id + 1]] for seg_id in range(7)]
    bias_segs = [norm_params[1, bounds[seg_id]:bounds[seg_id + 1]] for seg_id in range(7)]
    spatial = spatial_one.reshape(3, 3, MID, MID)
    mixing = temporal_mix.reshape(3, 3, 3, GROUP, GROUP)
    inputs = [tensor * live_mask for tensor, live_mask in zip(clips, masks)]
    conv_first = [low_back(pointwise(tensor, reduce_one)) for tensor in inputs]
    hidden_one = [low(tensor) for tensor in norm_act(conv_first, masks, count_in, gain_segs[0], bias_segs[0])]
    conv_second = [low_back(conv_spatial(tensor, spatial, 2)) for tensor in hidden_one]
    hidden_two = [low(tensor) for tensor in norm_act(conv_second, masks, count_out, gain_segs[1], bias_segs[1])]
    conv_third = [low_back(pointwise(tensor, expand_one)) for tensor in hidden_two]
    conv_skip = [low_back(pointwise(tensor[:, ::2, ::2, :], shortcut_one)) for tensor in inputs]
    third_a, third_b = local_sums(conv_third, masks)
    skip_a, skip_b = local_sums(conv_skip, masks)
    block_one = [live_mask * sigmoid_linear(norm_apply(third, third_a, third_b, count_out, gain_segs[2], bias_segs[2]) + norm_apply(skipped, skip_a, skip_b, count_out, gain_segs[3], bias_segs[3])) for third, skipped, live_mask in zip(conv_third, conv_skip, masks)]
    conv_entry = [low_back(pointwise(low(tensor), reduce_two)) for tensor in block_one]
    features = norm_act(conv_entry, masks, count_out, gain_segs[4], bias_segs[4])
    squeezed = [low_back(pointwise(low(tensor), excite_down)) for tensor in features]
    gated_all = excite(features, squeezed, excite_up, kernel, next_masks, FRAMES)
    mixed_all = []
    for gated_one, live_mask in zip(gated_all, masks):
        pieces = jnp.split(gated_one, 4, axis=-1)
        outputs = [pieces[0]]
        for branch_id in range(1, 4):
            shifted = low(shift_frames(pieces[branch_id] + outputs[-1], FRAMES, SHIFT))
            outputs.append(live_mask * low_back(conv_spatial(shifted, mixing[branch_id - 1], 1)))
        mixed_all.append(jnp.concatenate(outputs, axis=-1))
    activated = [low(tensor) for tensor in norm_act(mixed_all, masks, count_out, gain_segs[5], bias_segs[5])]
    conv_last = [low_back(pointwise(tensor, expand_two)) for tensor in activated]
    last_a, last_b = local_sums(conv_last, masks)
    return [live_mask * sigmoid_linear(norm_apply(tensor, last_a, last_b, count_out, gain_segs[6], bias_segs[6]) + skipped) for tensor, skipped, live_mask in zip(conv_last, block_one, masks)]

def reference(coarse_clips, medium_clips, fine_clips, clip_counts, frame_counts, reduce_one, spatial_one, expand_one, shortcut_one, reduce_two, excite_down, excite_up, temporal_mix, expand_two, norm_params, motion_kernel, coarse_cot, medium_cot, fine_cot):
    slot_ids = jnp.arange(SLOTS, dtype=jnp.int32)
    frame_ids = jnp.arange(FRAMES, dtype=jnp.int32)
    sides = (SIDE_A, SIDE_B, SIDE_C)
    masks = []
    next_masks = []
    count_in = jnp.zeros((), jnp.float32)
    count_out = jnp.zeros((), jnp.float32)
    for group_id in range(3):
        clip_alive = slot_ids % CLIPS < clip_counts[slot_ids // CLIPS, group_id]
        frame_alive = frame_ids[None, :] < frame_counts[:, group_id][:, None]
        alive_now = (clip_alive[:, None] & frame_alive).astype(jnp.float32)
        later_alive = jnp.pad(alive_now[:, 1:], ((0, 0), (0, 1)))
        masks.append(alive_now.reshape(-1, 1, 1, 1))
        next_masks.append(later_alive.reshape(-1, 1, 1, 1))
        count_in = count_in + jnp.sum(alive_now) * (4 * sides[group_id] * sides[group_id])
        count_out = count_out + jnp.sum(alive_now) * (sides[group_id] * sides[group_id])
    clips = [tensor.astype(jnp.float32) for tensor in (coarse_clips, medium_clips, fine_clips)]
    weights = (reduce_one, spatial_one, expand_one, shortcut_one, reduce_two, excite_down, excite_up, temporal_mix, expand_two, norm_params)

    def run_layers(clip_vals, weight_vals, kernel_vals):
        return forward(clip_vals, weight_vals, kernel_vals, masks, next_masks, count_in, count_out)
    outputs, pull_back = jax.vjp(run_layers, clips, weights, motion_kernel)
    cotangents = [tensor.astype(jnp.float32) for tensor in (coarse_cot, medium_cot, fine_cot)]
    input_grads, weight_grads, kernel_grad = pull_back(cotangents)
    return (outputs[0].astype(jnp.bfloat16), outputs[1].astype(jnp.bfloat16), outputs[2].astype(jnp.bfloat16), input_grads[0].astype(jnp.bfloat16), input_grads[1].astype(jnp.bfloat16), input_grads[2].astype(jnp.bfloat16), weight_grads[0], weight_grads[1], weight_grads[2], weight_grads[3], weight_grads[4], weight_grads[5], weight_grads[6], weight_grads[7], weight_grads[8], weight_grads[9], kernel_grad)
```

```python
from functools import partial

import jax
import jax.numpy as jnp
from jax import lax
from jax.experimental import pallas as pl
from jax.experimental.pallas import tpu as pltpu
from jax.sharding import PartitionSpec as P
import numpy as np

MID = 512
C_OUT = 2048
FRAMES = 4
GROUP = 128
SHIFT = 16
SQUEEZE = 32
SIDES = (4, 6, 7)
AXES = ("dp", "fsdp")
EPS = 1e-05
HIGHEST = lax.Precision.HIGHEST
F32 = jnp.float32
BF16 = jnp.bfloat16

ROWS = (64, 192, 224)
CUTS = (0, 64, 256, 480)
R = 480


def row_tables():
    frame = np.zeros(R, np.int32)
    row = np.zeros(R, np.int32)
    col = np.zeros(R, np.int32)
    group = np.zeros(R, np.int32)
    at = 0
    for a in range(2):
        for i in range(4):
            for p in range(2):
                for j in range(4):
                    frame[at], row[at], col[at], group[at] = 2 * a + p, i, j, 0
                    at += 1
    for g in (1, 2):
        for f in range(4):
            for i in range(SIDES[g]):
                for j in range(8):
                    frame[at], row[at], col[at], group[at] = f, i, j, g
                    at += 1
    side = np.array(SIDES)[group]
    return group, frame, row, col, (col < side), side


GROUP_OF, FRAME_OF, ROW_OF, COL_OF, VALID, SIDE_OF = row_tables()
SLOT_OF = GROUP_OF * FRAMES + FRAME_OF


def window_table():
    table = np.zeros((12, 9, R), np.float32)
    for r in range(R):
        if not VALID[r]:
            continue
        for t in range(9):
            dy, dx = t // 3 - 1, t % 3 - 1
            i, j = ROW_OF[r] - dy, COL_OF[r] - dx
            if 0 <= i < SIDE_OF[r] and 0 <= j < SIDE_OF[r]:
                table[SLOT_OF[r], t, r] = 1.0
    return table.reshape(108, R)


WINDOWS = window_table()
SPREAD = ((SLOT_OF[:, None] == np.arange(12)[None]) & VALID[:, None]).astype(np.float32)
NPIX = np.repeat(np.array([s * s for s in SIDES], np.float32), FRAMES)


def split(v):
    c = v.shape[-1]
    return (
        v[0:64].reshape(2, 4, 8, c),
        v[64:256].reshape(4, 6, 8, c),
        v[256:480].reshape(4, 7, 8, c),
    )


def join(parts):
    return jnp.concatenate([p.reshape(-1, p.shape[-1]) for p in parts], axis=0)


def shift_rows(v, dy):
    if dy == 0:
        return v
    out = []
    for p in split(v):
        zero = jnp.zeros_like(p[:, :1])
        out.append(
            jnp.concatenate([p[:, 1:], zero] if dy > 0 else [zero, p[:, :-1]], axis=1)
        )
    return join(out)


def shift_cols(v, dx):
    if dx == 0:
        return v
    c = v.shape[-1]
    rolled = jnp.roll(v.reshape(R // 8, 8, c), -dx, axis=1).reshape(R, c)
    edge = COL_OF == (0 if dx < 0 else 3)
    keep = ~((GROUP_OF == 0) & edge)
    return jnp.where(keep[:, None], rolled, jnp.zeros_like(rolled))


def shift(v, dy, dx):
    return shift_rows(shift_cols(v, dx), dy)


def shift_frame(v, df):
    c = v.shape[-1]
    pc, pm, pf = split(v)
    half = jnp.roll(pc.reshape(8, 8, c), 4, axis=1).reshape(2, 4, 8, c)
    zero = jnp.zeros_like(half[:1])
    first = (np.arange(8) < 4)[None, None, :, None]
    if df < 0:
        other = jnp.concatenate([zero, half[:-1]], axis=0)
        oc = jnp.where(first, other, half)
    else:
        other = jnp.concatenate([half[1:], zero], axis=0)
        oc = jnp.where(first, half, other)
    out = [oc]
    for p in (pm, pf):
        zero = jnp.zeros_like(p[:1])
        out.append(jnp.concatenate([p[1:], zero] if df > 0 else [zero, p[:-1]], axis=0))
    return join(out)


def time_shift(v, back):
    a = shift_frame(v, 1 if back else -1)
    b = shift_frame(v, -1 if back else 1)
    return jnp.concatenate(
        [a[:, :SHIFT], b[:, SHIFT : 2 * SHIFT], v[:, 2 * SHIFT :]], axis=-1
    )


def dot(a, b):
    return jnp.dot(a, b, preferred_element_type=F32)


def dot_nt(a, b):
    return lax.dot_general(a, b, (((1,), (1,)), ((), ())), preferred_element_type=F32)


def dot_tn(a, b):
    return lax.dot_general(a, b, (((0,), (0,)), ((), ())), preferred_element_type=F32)


def sums_of(a):
    return jnp.stack([jnp.sum(a, axis=0), jnp.sum(a * a, axis=0)])


def allsum(vectors, n):
    flat = jnp.concatenate([v.reshape(-1) for v in vectors])
    size = flat.shape[0]
    padded = -(-size // 1024) * 1024
    flat = jnp.pad(flat, (0, padded - size)).reshape(padded // 128, 128)
    spread = jnp.broadcast_to(flat[None], (n,) + flat.shape)
    got = lax.all_to_all(spread, AXES, 0, 0, tiled=True)
    flat = jnp.sum(got, axis=0).reshape(-1)
    out = []
    at = 0
    for v in vectors:
        out.append(flat[at : at + v.size].reshape(v.shape))
        at += v.size
    return out


def norm_rows(sums, count, gb):
    mean = sums[0] / count
    var = sums[1] / count - mean * mean
    rstd = lax.rsqrt(var + EPS)
    return mean, rstd, gb[0], gb[1]


def normalize(a, st):
    mean, rstd, gain, bias = st
    xhat = (a - mean) * rstd
    return xhat, xhat * gain + bias


def silu(u):
    return u * jax.nn.sigmoid(u)


def silu_grad(u):
    s = jax.nn.sigmoid(u)
    return s * (1.0 + u * (1.0 - s))


def back_sums(g, xhat):
    return jnp.stack([jnp.sum(g * xhat, axis=0), jnp.sum(g, axis=0)])


def norm_back(g, xhat, mask, st, tot, count):
    mean, rstd, gain, bias = st
    return gain * rstd * (g - mask * (tot[1] + xhat * tot[0]) / count)


def to_rows(groups, phase):
    out = []
    for x, side in zip(groups, SIDES):
        c = x.shape[-1]
        if phase is not None:
            x = x.reshape(FRAMES, side, 2, side, 2, c)[:, :, phase // 2, :, phase % 2]
        if side == 4:
            x = x.reshape(2, 2, 4, 4, c).transpose(0, 2, 1, 3, 4).reshape(64, c)
        else:
            x = jnp.pad(x, ((0, 0), (0, 0), (0, 8 - side), (0, 0))).reshape(-1, c)
        out.append(x)
    return jnp.concatenate(out, axis=0)


def from_rows(v):
    c = v.shape[-1]
    pc, pm, pf = split(v)
    coarse = pc.reshape(2, 4, 2, 4, c).transpose(0, 2, 1, 3, 4).reshape(4, 4, 4, c)
    return [coarse, pm[:, :, :6], pf[:, :, :7]]


TAPS2 = []
for kh in range(3):
    for kw in range(3):
        pr, dy = (1, -1) if kh == 0 else ((0, 0) if kh == 1 else (1, 0))
        pc, dx = (1, -1) if kw == 0 else ((0, 0) if kw == 1 else (1, 0))
        TAPS2.append((pr * 2 + pc, dy, dx, kh * 3 + kw))


VMEM = pl.BlockSpec(memory_space=pltpu.VMEM)
SMEM = pl.BlockSpec(memory_space=pltpu.SMEM)


def call(kernel, outs, n_in, scratch=(), scalars=1, flops=0, moved=0):
    return pl.pallas_call(
        kernel,
        out_shape=outs,
        in_specs=[SMEM] * scalars + [VMEM] * n_in,
        out_specs=[VMEM] * len(outs),
        scratch_shapes=list(scratch),
        compiler_params=pltpu.CompilerParams(vmem_limit_bytes=56 * 1024 * 1024),
        cost_estimate=pl.CostEstimate(flops=flops, bytes_accessed=moved, transcendentals=0),
    )


def like(shape, dtype=F32):
    return jax.ShapeDtypeStruct(shape, dtype)


def kshift_cols(v, dx):
    if dx == 0:
        return v
    c = v.shape[-1]
    rolled = pltpu.roll(v.reshape(R // 8, 8, c), 1 if dx < 0 else 7, 1).reshape(R, c)
    top = rolled[:64]
    place = lax.broadcasted_iota(jnp.int32, (64, c), 0) & 3
    top = jnp.where(place == (0 if dx < 0 else 3), 0.0, top)
    return jnp.concatenate([top, rolled[64:]], axis=0)


def kshift_frame(v, df):
    c = v.shape[-1]
    pc, pm, pf = split(v)
    half = pltpu.roll(pc.reshape(8, 8, c), 4, 1).reshape(2, 4, 8, c)
    zero = jnp.zeros_like(half[:1])
    first = lax.broadcasted_iota(jnp.int32, (2, 4, 8, c), 2) < 4
    if df < 0:
        oc = jnp.where(first, jnp.concatenate([zero, half[:-1]], axis=0), half)
    else:
        oc = jnp.where(first, half, jnp.concatenate([half[1:], zero], axis=0))
    out = [oc]
    for p in (pm, pf):
        zero = jnp.zeros_like(p[:1])
        out.append(jnp.concatenate([p[1:], zero] if df > 0 else [zero, p[:-1]], axis=0))
    return join(out)


def ktime_shift(v, back):
    lane = lax.broadcasted_iota(jnp.int32, v.shape, 1)
    a = kshift_frame(v, 1 if back else -1)
    b = kshift_frame(v, -1 if back else 1)
    return jnp.where(lane < SHIFT, a, jnp.where(lane < 2 * SHIFT, b, v))


def kstats(sums, count, gb):
    mean = sums[0:1] / count
    var = sums[1:2] / count - mean * mean
    return mean, lax.rsqrt(var + EPS), gb[0:1], gb[1:2]


def ksums(a, b):
    return jnp.concatenate(
        [jnp.sum(a, axis=0, keepdims=True), jnp.sum(b, axis=0, keepdims=True)], axis=0
    )


def cols(st, c, w=128):
    return tuple(v[:, c * w : (c + 1) * w] for v in st)


def three(v):
    a = v.astype(BF16)
    rest = v - a.astype(F32)
    b = rest.astype(BF16)
    c = (rest - b.astype(F32)).astype(BF16)
    return a, b, c


def exact_dot(table, v):
    return sum(dot(table, part) for part in three(v))


def frame_sums(v):
    pc, pm, pf = split(v)
    first = lax.broadcasted_iota(jnp.int32, (2, 4, 8, v.shape[-1]), 2) < 4
    even = jnp.sum(jnp.where(first, pc, 0.0), axis=(1, 2))
    odd = jnp.sum(jnp.where(first, 0.0, pc), axis=(1, 2))
    pm = jnp.sum(pm, axis=(1, 2))
    pf = jnp.sum(pf, axis=(1, 2))
    rows = [even[0:1], odd[0:1], even[1:2], odd[1:2]]
    rows += [pm[f : f + 1] for f in range(4)] + [pf[f : f + 1] for f in range(4)]
    return jnp.concatenate(rows + [jnp.zeros((4, v.shape[-1]), F32)], axis=0)


def mix_forward(cnt, b1, s4, gb4, mask, wdown, wup, wmix, kern, scale, table, spread,
                z_ref, zl_ref, mixed_ref, im_ref, sig_ref, pooled_ref, wnext_ref, sums_ref):
    m = mask[...]
    st = kstats(s4[...], cnt[0], gb4[...])
    for c in range(4):
        sl = slice(c * 128, (c + 1) * 128)
        z = m * silu(normalize(b1[:, sl], cols(st, c))[1])
        z_ref[:, sl] = z
        zl_ref[:, sl] = z.astype(BF16)
    r = dot(zl_ref[...], wdown[...])
    ws = exact_dot(table[...], r)
    wnext_ref[...] = ws[:144]
    pooled = -ws[144:160]
    for t in range(9):
        pooled = pooled + kern[t : t + 1, :] * ws[t * 16 : (t + 1) * 16]
    pooled = scale[...] * pooled
    pooled_ref[...] = pooled
    sig = jax.nn.sigmoid(jnp.dot(pooled, wup[...], precision=HIGHEST))
    sig_ref[...] = sig
    gates = jnp.concatenate(three(0.5 + sig), axis=0)
    prev = None
    for c in range(4):
        sl = slice(c * 128, (c + 1) * 128)
        v = z_ref[:, sl] * dot(spread[...], gates[:, sl])
        if c > 0:
            low = ktime_shift(v + prev, False).astype(BF16).astype(F32)
            for dx in (-1, 0, 1):
                moved = kshift_cols(low, dx)
                for dy in (-1, 0, 1):
                    t = (dy + 1) * 3 + dx + 1
                    im_ref[c - 1, :, t * 128 : (t + 1) * 128] = shift_rows(moved, dy).astype(BF16)
            v = m * dot(im_ref[c - 1], wmix[c - 1])
        prev = v
        mixed_ref[:, sl] = v
        sums_ref[:, sl] = ksums(v, v * v)


def mix_backward(cnt, g5, t5, mixed, s5, gb5, mask, imt, wmix_t, z_ref, sig, pooled, wnext,
                 wup, kern, scale, table_t, spread, zl, wdown, b1, s4, gb4,
                 g4_ref, sums_ref, gkern_ref, gmix_ref, gdown_ref, gup_ref, gim, gzg):
    m = mask[...]
    count = cnt[0]
    st = kstats(s5[...], count, gb5[...])
    tot = t5[...]
    carried = None
    gsig = []
    for c in (3, 2, 1, 0):
        sl = slice(c * 128, (c + 1) * 128)
        stc = cols(st, c)
        x, _ = normalize(mixed[:, sl], stc)
        gm = norm_back(g5[:, sl], x, m, stc, (tot[0:1, sl], tot[1:2, sl]), count)
        if carried is not None:
            gm = gm + carried
        if c > 0:
            low = (m * gm).astype(BF16)
            gmix_ref[c - 1] = dot_tn(imt[c - 1], low).astype(BF16)
            low = low.astype(F32)
            for dx in (-1, 0, 1):
                moved = kshift_cols(low, -dx)
                for dy in (-1, 0, 1):
                    t = (dy + 1) * 3 + dx + 1
                    gim[:, t * 128 : (t + 1) * 128] = shift_rows(moved, -dy).astype(BF16)
            gm = ktime_shift(dot(gim[...], wmix_t[c - 1]), True)
            carried = gm
        gzg[:, sl] = gm
        gsig.insert(0, frame_sums(gm * z_ref[:, sl]))
    sg = sig[...]
    ge = jnp.concatenate(gsig, axis=1) * sg * (1.0 - sg)
    gup_ref[...] = lax.dot_general(
        pooled[...], ge, (((0,), (0,)), ((), ())), precision=HIGHEST, preferred_element_type=F32
    )
    q = scale[...] * lax.dot_general(
        ge, wup[...], (((1,), (1,)), ((), ())), precision=HIGHEST, preferred_element_type=F32
    )
    coef = []
    gk = []
    for t in range(9):
        gk.append(jnp.sum(q * wnext[t * 16 : (t + 1) * 16], axis=0, keepdims=True))
        coef.append(kern[t : t + 1, :] * q)
    gkern_ref[...] = jnp.concatenate(gk + [jnp.zeros((7, SQUEEZE), F32)], axis=0)
    coef = jnp.concatenate(coef + [-q], axis=0)
    gr = exact_dot(table_t[...], coef).astype(BF16)
    gdown_ref[...] = dot_tn(zl[...], gr)
    gates = jnp.concatenate(three(0.5 + sg), axis=0)
    st = kstats(s4[...], count, gb4[...])
    for c in range(4):
        sl = slice(c * 128, (c + 1) * 128)
        gz = gzg[:, sl] * dot(spread[...], gates[:, sl]) + dot_nt(gr, wdown[sl, :])
        x, u = normalize(b1[:, sl], cols(st, c))
        g = gz * m * silu_grad(u)
        g4_ref[:, sl] = g
        sums_ref[:, sl] = ksums(g * x, g)


def conv_forward(cnt, a1, s0, gb0, mask, valid, w, im_ref, a2_ref, sums_ref):
    m = mask[...]
    st = kstats(s0[...], 4.0 * cnt[0], gb0[...])
    for c in range(4):
        sl = slice(c * 128, (c + 1) * 128)
        stc = cols(st, c)
        for ph in range(4):
            h = m * silu(normalize(a1[ph, :, sl], stc)[1])
            h = h.astype(BF16).astype(F32)
            for dx in (0, -1):
                if dx and not ph & 1:
                    continue
                moved = kshift_cols(h, dx)
                for p, dy, dx2, t in TAPS2:
                    if p == ph and dx2 == dx:
                        at = t * MID + c * 128
                        im_ref[:, at : at + 128] = shift_rows(moved, dy).astype(BF16)
    a2 = dot(im_ref[...], w[...]) * valid[...]
    a2_ref[...] = a2
    sums_ref[...] = ksums(a2, a2 * a2)


def conv_backward(cnt, g1, t1, a2, s1, gb1, mask, w, a1, s0, gb0,
                  d1_ref, g0_ref, sums_ref, moved_ref):
    m = mask[...]
    count = cnt[0]
    st = kstats(s1[...], count, gb1[...])
    tot = t1[...]
    for c in range(4):
        sl = slice(c * 128, (c + 1) * 128)
        stc = cols(st, c)
        x, _ = normalize(a2[:, sl], stc)
        d = norm_back(g1[:, sl], x, m, stc, (tot[0:1, sl], tot[1:2, sl]), count).astype(BF16)
        d1_ref[:, sl] = d
        d = d.astype(F32)
        for dx in (0, 1):
            moved = kshift_cols(d, dx)
            for dy in (0, 1):
                moved_ref[dy * 2 + dx, :, sl] = shift_rows(moved, dy).astype(BF16)
    st = kstats(s0[...], 4.0 * count, gb0[...])
    sums = jnp.zeros((2, MID), F32)
    for ph in range(4):
        gh = None
        for p, dy, dx, t in TAPS2:
            if p == ph:
                part = dot_nt(moved_ref[-dy * 2 - dx], w[t * MID : (t + 1) * MID, :])
                gh = part if gh is None else gh + part
        halves = []
        for c in range(4):
            sl = slice(c * 128, (c + 1) * 128)
            x, u = normalize(a1[ph, :, sl], cols(st, c))
            g = gh[:, sl] * m * silu_grad(u)
            g0_ref[ph, :, sl] = g
            halves.append(ksums(g * x, g))
        sums = sums + jnp.concatenate(halves, axis=1)
    sums_ref[...] = sums


def window_tables():
    pixel = WINDOWS.reshape(12, 9, R)
    table = np.zeros((160, R), np.float32)
    for slot in range(12):
        if slot % 4 < 3:
            for t in range(9):
                table[t * 16 + slot] = pixel[slot + 1, t]
        table[144 + slot] = pixel[slot, 4]
    spread = np.zeros((R, 16), np.float32)
    spread[:, :12] = SPREAD
    return table, np.concatenate([spread] * 3, axis=1)


TABLE, SPREAD3 = window_tables()


def scatter_sum(grads, n, mesh_bits):
    sizes = [g.shape[1] for g in grads]
    x = jnp.concatenate([g.astype(BF16) for g in grads], axis=1)
    x = jnp.pad(x, ((0, 0), (0, -x.shape[1] % 1024)))
    x = x.reshape((2,) * (n.bit_length() - 1) + (-1, 128))
    me = lax.axis_index(AXES)
    bits = n.bit_length() - 1
    left = list(range(bits))
    for b in mesh_bits:
        axis = left.index(bits - 1 - b)
        mine = (me >> b) & 1
        keep = lax.dynamic_index_in_dim(x, mine, axis, keepdims=False)
        send = lax.dynamic_index_in_dim(x, 1 - mine, axis, keepdims=False)
        got = lax.ppermute(send, AXES, [(i, i ^ (1 << b)) for i in range(n)])
        total = keep.astype(F32) + got.astype(F32)
        left.pop(axis)
        x = total if b == mesh_bits[-1] else total.astype(BF16)
    flat = x.reshape(-1)
    out = []
    at = 0
    for s in sizes:
        out.append(flat[at : at + s])
        at += s
    return out


def body(n, fsdp, *args):
    (coarse, medium, fine, clip_counts, frame_counts, reduce_one, spatial_one, expand_one,
     shortcut_one, reduce_two, excite_down, excite_up, temporal_mix, expand_two, norm_params,
     motion_kernel, cot_c, cot_m, cot_f) = args
    bits = n.bit_length() - 1
    core = fsdp.bit_length() - 1
    order = [core] + [b for b in range(bits) if b != core]

    def gather(w):
        return lax.all_gather(w.astype(BF16), AXES, axis=0, tiled=True)

    def pack(ws):
        flat = jnp.concatenate([w.astype(BF16).reshape(-1) for w in ws])
        return jnp.pad(flat, (0, -flat.size % 1024)).reshape(-1, 128)

    def unpack(got, ws):
        flat = got.reshape(n, -1)
        out = []
        at = 0
        for w in ws:
            out.append(flat[:, at : at + w.size].reshape((n,) + w.shape))
            at += w.size
        return out

    early = (reduce_one, norm_params)
    packed = pack(early)
    got = lax.all_to_all(
        jnp.broadcast_to(packed[None], (n,) + packed.shape), AXES, 0, 0, tiled=True
    )
    w1, norms = unpack(got, early)
    w1 = w1.reshape(-1, MID)
    norms = norms.transpose(1, 0, 2).reshape(2, -1).astype(F32)
    wsp = gather(spatial_one)
    wsk = gather(shortcut_one)
    we1 = gather(expand_one)
    w2 = gather(reduce_two)
    narrow = (excite_down, excite_up, temporal_mix)
    wdown, wup, wmix = unpack(gather(pack(narrow)), narrow)
    wdown = wdown.reshape(MID, SQUEEZE)
    wup = wup.transpose(1, 0, 2).reshape(SQUEEZE, MID).astype(F32)
    wmix = wmix.transpose(1, 0, 2).reshape(3, 9 * GROUP, GROUP)
    we2 = gather(expand_two)
    edges = [0, 512, 1024, 3072, 5120, 5632, 6144, 8192]
    gb = [norms[:, edges[k] : edges[k + 1]] for k in range(7)]

    alive = (jnp.arange(4)[None, :] < frame_counts[0][:, None]) & (clip_counts[0][:, None] > 0)
    alive = alive.astype(F32)
    later = jnp.pad(alive[:, 1:], ((0, 0), (0, 1)))
    alive_slots = alive.reshape(12)
    later_slots = later.reshape(12)
    mask = (jnp.asarray(SPREAD) @ alive_slots)[:, None]
    per_group = jnp.sum(alive, axis=1)
    local_out = jnp.sum(per_group * jnp.array([16.0, 36.0, 49.0], F32))

    clips = [
        x * alive[g].astype(BF16)[:, None, None, None]
        for g, x in enumerate((coarse, medium, fine))
    ]
    xph = [to_rows(clips, ph) for ph in range(4)]
    cot = to_rows((cot_c, cot_m, cot_f), None).astype(F32)

    a1 = [dot(x, w1) for x in xph]
    s0 = sum(sums_of(a) for a in a1)
    ap = dot(xph[0], wsk)
    s3 = sums_of(ap)
    s0, count_out = allsum((s0, local_out.reshape(1)), n)
    count_out = count_out[0]
    count_in = 4.0 * count_out
    st0 = norm_rows(s0, count_in, gb[0])
    cnt = count_out.reshape(1)
    m128 = jnp.broadcast_to(mask, (R, 128))
    valid = jnp.asarray(np.broadcast_to(VALID[:, None], (R, MID)).astype(np.float32))
    a1 = jnp.stack(a1)
    im, a2, p1 = call(
        conv_forward,
        [like((R, 9 * MID), BF16), like((R, MID)), like((2, MID))],
        6,
    )(cnt, a1, s0, gb[0], m128, valid, wsp)
    s1, = allsum((p1,), n)
    st1 = norm_rows(s1, count_out, gb[1])
    h2 = (mask * silu(normalize(a2, st1)[1])).astype(BF16)
    a3 = dot(h2, we1)
    s2, s3 = allsum((sums_of(a3), s3), n)
    st2 = norm_rows(s2, count_out, gb[2])
    st3 = norm_rows(s3, count_out, gb[3])
    y1 = mask * silu(normalize(a3, st2)[1] + normalize(ap, st3)[1])
    y1_low = y1.astype(BF16)
    b1 = dot(y1_low, w2)
    s4, = allsum((sums_of(b1),), n)
    st4 = norm_rows(s4, count_out, gb[4])
    scale = later_slots / jnp.asarray(NPIX)
    scale = jnp.broadcast_to(jnp.pad(scale, (0, 4))[:, None], (16, SQUEEZE))
    table = jnp.asarray(TABLE, BF16)
    spread = jnp.asarray(SPREAD3, BF16)
    z, z_low, mixed, mix_im, sig, pooled, wnext, p5 = call(
        mix_forward,
        [like((R, MID)), like((R, MID), BF16), like((R, MID)), like((3, R, 9 * GROUP), BF16),
         like((16, MID)), like((16, SQUEEZE)), like((144, SQUEEZE)), like((2, MID))],
        11,
    )(cnt, b1, s4, gb[4], m128, wdown, wup, wmix, motion_kernel, scale, table, spread)
    s5, = allsum((p5,), n)
    st5 = norm_rows(s5, count_out, gb[5])
    w = (mask * silu(normalize(mixed, st5)[1])).astype(BF16)
    b3 = dot(w, we2)
    s6, = allsum((sums_of(b3),), n)
    st6 = norm_rows(s6, count_out, gb[6])
    x6, u6 = normalize(b3, st6)
    u6 = u6 + y1
    out = (mask * silu(u6)).astype(BF16)

    g6 = cot * mask * silu_grad(u6)
    t6, = allsum((back_sums(g6, x6),), n)
    d6 = norm_back(g6, x6, mask, st6, t6, count_out).astype(BF16)
    ge2 = dot_tn(w, d6)
    x5, u5 = normalize(mixed, st5)
    g5 = dot_nt(d6, we2) * mask * silu_grad(u5)
    t5, = allsum((back_sums(g5, x5),), n)
    wmix_t = wmix.reshape(3, 9, GROUP, GROUP).transpose(0, 1, 3, 2).reshape(3, 9 * GROUP, GROUP)
    g4, p4, gkernel, gmix, gdown, gup = call(
        mix_backward,
        [like((R, MID)), like((2, MID)), like((16, SQUEEZE)), like((3, 9 * GROUP, GROUP), BF16),
         like((MID, SQUEEZE)), like((SQUEEZE, MID))],
        22,
        [pltpu.VMEM((R, 9 * GROUP), BF16), pltpu.VMEM((R, MID), F32)],
    )(cnt, g5, t5, mixed, s5, gb[5], m128, mix_im, wmix_t, z, sig, pooled, wnext,
      wup, motion_kernel, scale, table.T, spread, z_low, wdown, b1, s4, gb[4])
    t4, gkernel = allsum((p4, gkernel), n)
    gkernel = gkernel[:9]
    x4, u4 = normalize(b1, st4)
    d4 = norm_back(g4, x4, mask, st4, t4, count_out).astype(BF16)
    gr2 = dot_tn(y1_low, d4)
    gy1 = g6 + dot_nt(d4, w2)
    x2, u2 = normalize(a3, st2)
    x3, u3 = normalize(ap, st3)
    gj = gy1 * mask * silu_grad(u2 + u3)
    tj, = allsum((jnp.stack([jnp.sum(gj * x2, 0), jnp.sum(gj * x3, 0), jnp.sum(gj, 0)]),), n)
    d2 = norm_back(gj, x2, mask, st2, tj[jnp.array([0, 2])], count_out).astype(BF16)
    d3 = norm_back(gj, x3, mask, st3, tj[1:], count_out).astype(BF16)
    ge1 = dot_tn(h2, d2)
    gsk = dot_tn(xph[0], d3)
    x1, u1 = normalize(a2, st1)
    g1 = dot_nt(d2, we1) * mask * silu_grad(u1)
    t1, = allsum((back_sums(g1, x1),), n)
    d1, g0, p0 = call(
        conv_backward,
        [like((R, MID), BF16), like((4, R, MID)), like((2, MID))],
        10,
        [pltpu.VMEM((4, R, MID), BF16)],
    )(cnt, g1, t1, a2, s1, gb[1], m128, wsp, a1, s0, gb[0])
    gsp = dot_tn(im, d1)
    t0, = allsum((p0,), n)
    d0 = [
        norm_back(g0[k], normalize(a1[k], st0)[0], mask, st0, t0, count_in).astype(BF16)
        for k in range(4)
    ]
    gr1 = sum(dot_tn(x, d) for x, d in zip(xph, d0))
    gx = [dot_nt(d, w1) for d in d0]
    gx[0] = gx[0] + dot_nt(d3, wsk)
    gx = [(mask * v).astype(BF16) for v in gx]
    phases = [from_rows(v) for v in gx]
    gin = []
    for g, side in enumerate(SIDES):
        st = jnp.stack([phases[k][g] for k in range(4)]).reshape(2, 2, 4, side, side, -1)
        gin.append(st.transpose(2, 3, 0, 4, 1, 5).reshape(4, 2 * side, 2 * side, -1))

    def shards(v):
        return v.reshape(n, -1)

    gmix = gmix.reshape(27, n, GROUP * GROUP // n).transpose(1, 0, 2)
    gup = gup.reshape(SQUEEZE, n, MID // n).transpose(1, 0, 2)
    second = scatter_sum(
        [shards(ge2), shards(gr2), shards(gmix), shards(gdown), shards(gup)], n, order
    )
    first = scatter_sum([shards(ge1), shards(gsk)], n, order)
    last = scatter_sum([shards(gsp), shards(gr1)], n, order)

    gain = jnp.concatenate([t0[0], t1[0], tj[0], tj[1], t4[0], t5[0], t6[0]])
    bias = jnp.concatenate([t0[1], t1[1], tj[2], tj[2], t4[1], t5[1], t6[1]])
    me = lax.axis_index(AXES)
    gnorm = lax.dynamic_slice_in_dim(jnp.stack([gain, bias]), me * (8192 // n), 8192 // n, 1)
    o = from_rows(out)
    return (
        o[0], o[1], o[2], gin[0], gin[1], gin[2],
        last[1].reshape(reduce_one.shape),
        last[0].reshape(spatial_one.shape),
        first[0].reshape(expand_one.shape),
        first[1].reshape(shortcut_one.shape),
        second[1].reshape(reduce_two.shape),
        second[3].reshape(excite_down.shape),
        second[4].reshape(excite_up.shape),
        second[2].reshape(temporal_mix.shape),
        second[0].reshape(expand_two.shape),
        gnorm,
        gkernel,
    )


def solution(mesh):
    n = mesh.shape["dp"] * mesh.shape["fsdp"]
    rows = P(AXES, None)
    cols = P(None, AXES)
    image = P(AXES, None, None, None)
    return jax.shard_map(
        partial(body, n, mesh.shape["fsdp"]),
        mesh=mesh,
        in_specs=(image, image, image, rows, rows, rows, rows, rows, rows, rows, rows, cols, cols,
                  rows, cols, P(), image, image, image),
        out_specs=(image, image, image, image, image, image, rows, rows, rows, rows, rows, rows,
                   cols, cols, rows, cols, P()),
        check_vma=False,
    )
```

```python
from functools import partial

import jax
import jax.numpy as jnp
from jax import lax
from jax.experimental import pallas as pl
from jax.experimental.pallas import tpu as pltpu
from jax.sharding import PartitionSpec as P
import numpy as np

MID = 512
C_OUT = 2048
FRAMES = 4
GROUP = 128
SHIFT = 16
SQUEEZE = 32
SIDES = (4, 6, 7)
AXES = ("dp", "fsdp")
EPS = 1e-05
HIGHEST = lax.Precision.HIGHEST
F32 = jnp.float32
BF16 = jnp.bfloat16

ROWS = (64, 192, 224)
CUTS = (0, 64, 256, 480)
R = 480


def row_tables():
    frame = np.zeros(R, np.int32)
    row = np.zeros(R, np.int32)
    col = np.zeros(R, np.int32)
    group = np.zeros(R, np.int32)
    at = 0
    for a in range(2):
        for i in range(4):
            for p in range(2):
                for j in range(4):
                    frame[at], row[at], col[at], group[at] = 2 * a + p, i, j, 0
                    at += 1
    for g in (1, 2):
        for f in range(4):
            for i in range(SIDES[g]):
                for j in range(8):
                    frame[at], row[at], col[at], group[at] = f, i, j, g
                    at += 1
    side = np.array(SIDES)[group]
    return group, frame, row, col, (col < side), side


GROUP_OF, FRAME_OF, ROW_OF, COL_OF, VALID, SIDE_OF = row_tables()
SLOT_OF = GROUP_OF * FRAMES + FRAME_OF


def window_table():
    table = np.zeros((12, 9, R), np.float32)
    for r in range(R):
        if not VALID[r]:
            continue
        for t in range(9):
            dy, dx = t // 3 - 1, t % 3 - 1
            i, j = ROW_OF[r] - dy, COL_OF[r] - dx
            if 0 <= i < SIDE_OF[r] and 0 <= j < SIDE_OF[r]:
                table[SLOT_OF[r], t, r] = 1.0
    return table.reshape(108, R)


WINDOWS = window_table()
SPREAD = ((SLOT_OF[:, None] == np.arange(12)[None]) & VALID[:, None]).astype(np.float32)
NPIX = np.repeat(np.array([s * s for s in SIDES], np.float32), FRAMES)


def split(v):
    c = v.shape[-1]
    return (
        v[0:64].reshape(2, 4, 8, c),
        v[64:256].reshape(4, 6, 8, c),
        v[256:480].reshape(4, 7, 8, c),
    )


def join(parts):
    return jnp.concatenate([p.reshape(-1, p.shape[-1]) for p in parts], axis=0)


def shift_rows(v, dy):
    if dy == 0:
        return v
    out = []
    for p in split(v):
        zero = jnp.zeros_like(p[:, :1])
        out.append(
            jnp.concatenate([p[:, 1:], zero] if dy > 0 else [zero, p[:, :-1]], axis=1)
        )
    return join(out)


def shift_cols(v, dx):
    if dx == 0:
        return v
    c = v.shape[-1]
    rolled = jnp.roll(v.reshape(R // 8, 8, c), -dx, axis=1).reshape(R, c)
    edge = COL_OF == (0 if dx < 0 else 3)
    keep = ~((GROUP_OF == 0) & edge)
    return jnp.where(keep[:, None], rolled, jnp.zeros_like(rolled))


def shift(v, dy, dx):
    return shift_rows(shift_cols(v, dx), dy)


def shift_frame(v, df):
    c = v.shape[-1]
    pc, pm, pf = split(v)
    half = jnp.roll(pc.reshape(8, 8, c), 4, axis=1).reshape(2, 4, 8, c)
    zero = jnp.zeros_like(half[:1])
    first = (np.arange(8) < 4)[None, None, :, None]
    if df < 0:
        other = jnp.concatenate([zero, half[:-1]], axis=0)
        oc = jnp.where(first, other, half)
    else:
        other = jnp.concatenate([half[1:], zero], axis=0)
        oc = jnp.where(first, half, other)
    out = [oc]
    for p in (pm, pf):
        zero = jnp.zeros_like(p[:1])
        out.append(jnp.concatenate([p[1:], zero] if df > 0 else [zero, p[:-1]], axis=0))
    return join(out)


def time_shift(v, back):
    a = shift_frame(v, 1 if back else -1)
    b = shift_frame(v, -1 if back else 1)
    return jnp.concatenate(
        [a[:, :SHIFT], b[:, SHIFT : 2 * SHIFT], v[:, 2 * SHIFT :]], axis=-1
    )


def dot(a, b):
    return jnp.dot(a, b, preferred_element_type=F32)


def dot_nt(a, b):
    return lax.dot_general(a, b, (((1,), (1,)), ((), ())), preferred_element_type=F32)


def dot_tn(a, b):
    return lax.dot_general(a, b, (((0,), (0,)), ((), ())), preferred_element_type=F32)


def sums_of(a):
    return jnp.stack([jnp.sum(a, axis=0), jnp.sum(a * a, axis=0)])


def allsum(vectors, n):
    flat = jnp.concatenate([v.reshape(-1) for v in vectors])
    size = flat.shape[0]
    padded = -(-size // 1024) * 1024
    flat = jnp.pad(flat, (0, padded - size)).reshape(padded // 128, 128)
    spread = jnp.broadcast_to(flat[None], (n,) + flat.shape)
    got = lax.all_to_all(spread, AXES, 0, 0, tiled=True)
    flat = jnp.sum(got, axis=0).reshape(-1)
    out = []
    at = 0
    for v in vectors:
        out.append(flat[at : at + v.size].reshape(v.shape))
        at += v.size
    return out


def norm_rows(sums, count, gb):
    mean = sums[0] / count
    var = sums[1] / count - mean * mean
    rstd = lax.rsqrt(var + EPS)
    return mean, rstd, gb[0], gb[1]


def normalize(a, st):
    mean, rstd, gain, bias = st
    xhat = (a - mean) * rstd
    return xhat, xhat * gain + bias


def silu(u):
    return u * jax.nn.sigmoid(u)


def silu_grad(u):
    s = jax.nn.sigmoid(u)
    return s * (1.0 + u * (1.0 - s))


def back_sums(g, xhat):
    return jnp.stack([jnp.sum(g * xhat, axis=0), jnp.sum(g, axis=0)])


def norm_back(g, xhat, mask, st, tot, count):
    mean, rstd, gain, bias = st
    return gain * rstd * (g - mask * (tot[1] + xhat * tot[0]) / count)


def to_rows(groups, phase):
    out = []
    for x, side in zip(groups, SIDES):
        c = x.shape[-1]
        if phase is not None:
            x = x.reshape(FRAMES, side, 2, side, 2, c)[:, :, phase // 2, :, phase % 2]
        if side == 4:
            x = x.reshape(2, 2, 4, 4, c).transpose(0, 2, 1, 3, 4).reshape(64, c)
        else:
            x = jnp.pad(x, ((0, 0), (0, 0), (0, 8 - side), (0, 0))).reshape(-1, c)
        out.append(x)
    return jnp.concatenate(out, axis=0)


def from_rows(v):
    c = v.shape[-1]
    pc, pm, pf = split(v)
    coarse = pc.reshape(2, 4, 2, 4, c).transpose(0, 2, 1, 3, 4).reshape(4, 4, 4, c)
    return [coarse, pm[:, :, :6], pf[:, :, :7]]


TAPS2 = []
for kh in range(3):
    for kw in range(3):
        pr, dy = (1, -1) if kh == 0 else ((0, 0) if kh == 1 else (1, 0))
        pc, dx = (1, -1) if kw == 0 else ((0, 0) if kw == 1 else (1, 0))
        TAPS2.append((pr * 2 + pc, dy, dx, kh * 3 + kw))


FREE = pl.CostEstimate(flops=0, bytes_accessed=0, transcendentals=0)
VMEM = pl.BlockSpec(memory_space=pltpu.VMEM)
SMEM = pl.BlockSpec(memory_space=pltpu.SMEM)


def call(kernel, outs, n_in, scratch=(), scalars=1):
    return pl.pallas_call(
        kernel,
        out_shape=outs,
        in_specs=[SMEM] * scalars + [VMEM] * n_in,
        out_specs=[VMEM] * len(outs),
        scratch_shapes=list(scratch),
        compiler_params=pltpu.CompilerParams(vmem_limit_bytes=56 * 1024 * 1024),
        cost_estimate=FREE,
    )


def like(shape, dtype=F32):
    return jax.ShapeDtypeStruct(shape, dtype)


def kshift_cols(v, dx):
    if dx == 0:
        return v
    c = v.shape[-1]
    rolled = pltpu.roll(v.reshape(R // 8, 8, c), 1 if dx < 0 else 7, 1).reshape(R, c)
    top = rolled[:64]
    place = lax.broadcasted_iota(jnp.int32, (64, c), 0) & 3
    top = jnp.where(place == (0 if dx < 0 else 3), 0.0, top)
    return jnp.concatenate([top, rolled[64:]], axis=0)


def kshift_frame(v, df):
    c = v.shape[-1]
    pc, pm, pf = split(v)
    half = pltpu.roll(pc.reshape(8, 8, c), 4, 1).reshape(2, 4, 8, c)
    zero = jnp.zeros_like(half[:1])
    first = lax.broadcasted_iota(jnp.int32, (2, 4, 8, c), 2) < 4
    if df < 0:
        oc = jnp.where(first, jnp.concatenate([zero, half[:-1]], axis=0), half)
    else:
        oc = jnp.where(first, half, jnp.concatenate([half[1:], zero], axis=0))
    out = [oc]
    for p in (pm, pf):
        zero = jnp.zeros_like(p[:1])
        out.append(jnp.concatenate([p[1:], zero] if df > 0 else [zero, p[:-1]], axis=0))
    return join(out)


def ktime_shift(v, back):
    lane = lax.broadcasted_iota(jnp.int32, v.shape, 1)
    a = kshift_frame(v, 1 if back else -1)
    b = kshift_frame(v, -1 if back else 1)
    return jnp.where(lane < SHIFT, a, jnp.where(lane < 2 * SHIFT, b, v))


def kstats(sums, count, gb):
    mean = sums[0:1] / count
    var = sums[1:2] / count - mean * mean
    return mean, lax.rsqrt(var + EPS), gb[0:1], gb[1:2]


def ksums(a, b):
    return jnp.concatenate(
        [jnp.sum(a, axis=0, keepdims=True), jnp.sum(b, axis=0, keepdims=True)], axis=0
    )


def cols(st, c, w=128):
    return tuple(v[:, c * w : (c + 1) * w] for v in st)


def three(v):
    a = v.astype(BF16)
    rest = v - a.astype(F32)
    b = rest.astype(BF16)
    c = (rest - b.astype(F32)).astype(BF16)
    return a, b, c


def exact_dot(table, v):
    return sum(dot(table, part) for part in three(v))


def frame_sums(v):
    pc, pm, pf = split(v)
    first = lax.broadcasted_iota(jnp.int32, (2, 4, 8, v.shape[-1]), 2) < 4
    even = jnp.sum(jnp.where(first, pc, 0.0), axis=(1, 2))
    odd = jnp.sum(jnp.where(first, 0.0, pc), axis=(1, 2))
    pm = jnp.sum(pm, axis=(1, 2))
    pf = jnp.sum(pf, axis=(1, 2))
    rows = [even[0:1], odd[0:1], even[1:2], odd[1:2]]
    rows += [pm[f : f + 1] for f in range(4)] + [pf[f : f + 1] for f in range(4)]
    return jnp.concatenate(rows + [jnp.zeros((4, v.shape[-1]), F32)], axis=0)


def mix_forward(cnt, b1, s4, gb4, mask, wdown, wup, wmix, kern, scale, table, spread,
                z_ref, zl_ref, mixed_ref, im_ref, sig_ref, pooled_ref, wnext_ref, sums_ref):
    m = mask[...]
    st = kstats(s4[...], cnt[0], gb4[...])
    for c in range(4):
        sl = slice(c * 128, (c + 1) * 128)
        z = m * silu(normalize(b1[:, sl], cols(st, c))[1])
        z_ref[:, sl] = z
        zl_ref[:, sl] = z.astype(BF16)
    r = dot(zl_ref[...], wdown[...])
    ws = exact_dot(table[...], r)
    wnext_ref[...] = ws[:144]
    pooled = -ws[144:160]
    for t in range(9):
        pooled = pooled + kern[t : t + 1, :] * ws[t * 16 : (t + 1) * 16]
    pooled = scale[...] * pooled
    pooled_ref[...] = pooled
    sig = jax.nn.sigmoid(jnp.dot(pooled, wup[...], precision=HIGHEST))
    sig_ref[...] = sig
    gates = jnp.concatenate(three(0.5 + sig), axis=0)
    prev = None
    for c in range(4):
        sl = slice(c * 128, (c + 1) * 128)
        v = z_ref[:, sl] * dot(spread[...], gates[:, sl])
        if c > 0:
            low = ktime_shift(v + prev, False).astype(BF16).astype(F32)
            for dx in (-1, 0, 1):
                moved = kshift_cols(low, dx)
                for dy in (-1, 0, 1):
                    t = (dy + 1) * 3 + dx + 1
                    im_ref[c - 1, :, t * 128 : (t + 1) * 128] = shift_rows(moved, dy).astype(BF16)
            v = m * dot(im_ref[c - 1], wmix[c - 1])
        prev = v
        mixed_ref[:, sl] = v
        sums_ref[:, sl] = ksums(v, v * v)


def mix_backward(cnt, g5, t5, mixed, s5, gb5, mask, imt, wmix_t, z_ref, sig, pooled, wnext,
                 wup, kern, scale, table_t, spread, zl, wdown, b1, s4, gb4,
                 g4_ref, sums_ref, gkern_ref, gmix_ref, gdown_ref, gup_ref, gim, gzg):
    m = mask[...]
    count = cnt[0]
    st = kstats(s5[...], count, gb5[...])
    tot = t5[...]
    carried = None
    gsig = []
    for c in (3, 2, 1, 0):
        sl = slice(c * 128, (c + 1) * 128)
        stc = cols(st, c)
        x, _ = normalize(mixed[:, sl], stc)
        gm = norm_back(g5[:, sl], x, m, stc, (tot[0:1, sl], tot[1:2, sl]), count)
        if carried is not None:
            gm = gm + carried
        if c > 0:
            low = (m * gm).astype(BF16)
            gmix_ref[c - 1] = dot_tn(imt[c - 1], low).astype(BF16)
            low = low.astype(F32)
            for dx in (-1, 0, 1):
                moved = kshift_cols(low, -dx)
                for dy in (-1, 0, 1):
                    t = (dy + 1) * 3 + dx + 1
                    gim[:, t * 128 : (t + 1) * 128] = shift_rows(moved, -dy).astype(BF16)
            gm = ktime_shift(dot(gim[...], wmix_t[c - 1]), True)
            carried = gm
        gzg[:, sl] = gm
        gsig.insert(0, frame_sums(gm * z_ref[:, sl]))
    sg = sig[...]
    ge = jnp.concatenate(gsig, axis=1) * sg * (1.0 - sg)
    gup_ref[...] = lax.dot_general(
        pooled[...], ge, (((0,), (0,)), ((), ())), precision=HIGHEST, preferred_element_type=F32
    )
    q = scale[...] * lax.dot_general(
        ge, wup[...], (((1,), (1,)), ((), ())), precision=HIGHEST, preferred_element_type=F32
    )
    coef = []
    gk = []
    for t in range(9):
        gk.append(jnp.sum(q * wnext[t * 16 : (t + 1) * 16], axis=0, keepdims=True))
        coef.append(kern[t : t + 1, :] * q)
    gkern_ref[...] = jnp.concatenate(gk + [jnp.zeros((7, SQUEEZE), F32)], axis=0)
    coef = jnp.concatenate(coef + [-q], axis=0)
    gr = exact_dot(table_t[...], coef).astype(BF16)
    gdown_ref[...] = dot_tn(zl[...], gr)
    gates = jnp.concatenate(three(0.5 + sg), axis=0)
    st = kstats(s4[...], count, gb4[...])
    for c in range(4):
        sl = slice(c * 128, (c + 1) * 128)
        gz = gzg[:, sl] * dot(spread[...], gates[:, sl]) + dot_nt(gr, wdown[sl, :])
        x, u = normalize(b1[:, sl], cols(st, c))
        g = gz * m * silu_grad(u)
        g4_ref[:, sl] = g
        sums_ref[:, sl] = ksums(g * x, g)


def conv_forward(cnt, a1, s0, gb0, mask, valid, w, im_ref, a2_ref, sums_ref):
    m = mask[...]
    st = kstats(s0[...], 4.0 * cnt[0], gb0[...])
    for c in range(4):
        sl = slice(c * 128, (c + 1) * 128)
        stc = cols(st, c)
        for ph in range(4):
            h = m * silu(normalize(a1[ph, :, sl], stc)[1])
            h = h.astype(BF16).astype(F32)
            for dx in (0, -1):
                if dx and not ph & 1:
                    continue
                moved = kshift_cols(h, dx)
                for p, dy, dx2, t in TAPS2:
                    if p == ph and dx2 == dx:
                        at = t * MID + c * 128
                        im_ref[:, at : at + 128] = shift_rows(moved, dy).astype(BF16)
    a2 = dot(im_ref[...], w[...]) * valid[...]
    a2_ref[...] = a2
    sums_ref[...] = ksums(a2, a2 * a2)


def window_tables():
    pixel = WINDOWS.reshape(12, 9, R)
    table = np.zeros((160, R), np.float32)
    for slot in range(12):
        if slot % 4 < 3:
            for t in range(9):
                table[t * 16 + slot] = pixel[slot + 1, t]
        table[144 + slot] = pixel[slot, 4]
    spread = np.zeros((R, 16), np.float32)
    spread[:, :12] = SPREAD
    return table, np.concatenate([spread] * 3, axis=1)


TABLE, SPREAD3 = window_tables()


def phase_tables():
    out = []
    for side, pairs in zip(SIDES, (2, 1, 1)):
        high = 2 * side
        wide = 4 if side == 4 else 8
        count = side * wide * pairs
        t = np.zeros((4 * count, pairs * high * 16), np.float32)
        for ph in range(4):
            for p in range(pairs):
                for i in range(side):
                    for j in range(side):
                        row = ph * count + (i * pairs + p) * wide + j
                        at = (p * high + 2 * i + ph // 2) * 16 + 2 * j + ph % 2
                        t[row, at] = 1.0
        out.append(t)
    return out


PHASES = phase_tables()


def split_phases(alive, xc, xm, xf, tc, tm, tf, out_ref, bc, bm, bf):
    @pl.when(pl.program_id(0) == 0)
    def _():
        for b in (bc, bm, bf):
            b[...] = jnp.zeros_like(b)

    pieces = [[], [], [], []]
    lanes = out_ref.shape[-1]
    for g, (x, table, buf) in enumerate(((xc, tc, bc), (xm, tm, bm), (xf, tf, bf))):
        pairs = buf.shape[0]
        side = 2 * SIDES[g]
        for f in range(0, FRAMES, pairs):
            for p in range(pairs):
                live = alive[g * FRAMES + f + p] > 0.0
                buf[p, :, 0:side, :] = jnp.where(live, x[f + p], jnp.zeros_like(x[f + p]))
            y = dot(table[...], buf[...].reshape(-1, lanes))
            step = y.shape[0] // 4
            for ph in range(4):
                pieces[ph].append(y[ph * step : (ph + 1) * step])
    for ph in range(4):
        out_ref[ph] = jnp.concatenate(pieces[ph], axis=0).astype(BF16)


def clip_blocks(lanes):
    return [
        pl.BlockSpec((FRAMES, 2 * s, 2 * s, lanes), lambda c: (0, 0, 0, c)) for s in SIDES
    ]


def image_blocks(lanes):
    return [pl.BlockSpec((FRAMES, s, s, lanes), lambda c: (0, 0, 0, c)) for s in SIDES]


def whole(v):
    return pl.BlockSpec(v.shape, lambda c: (0,) * v.ndim)


def column(rows, lanes):
    return pl.BlockSpec((rows, lanes), lambda c: (0, c))


LIMIT = pltpu.CompilerParams(vmem_limit_bytes=56 * 1024 * 1024)


def run_split(alive, clips, tables):
    lanes = 256
    c_in = clips[0].shape[-1]
    return pl.pallas_call(
        split_phases,
        grid=(c_in // lanes,),
        out_shape=like((4, R, c_in), BF16),
        in_specs=[SMEM] + clip_blocks(lanes) + [whole(t) for t in tables],
        out_specs=pl.BlockSpec((4, R, lanes), lambda c: (0, 0, c)),
        scratch_shapes=[
            pltpu.VMEM((2 if s == 4 else 1, 2 * s, 16, lanes), BF16) for s in SIDES
        ],
        compiler_params=LIMIT,
        cost_estimate=FREE,
    )(alive, *clips, *tables)


def input_grads(d0, d3, w1, wsk, mask, tc, tm, tf, oc, om, of):
    lanes = oc.shape[-1]
    m = mask[...]
    m = jnp.concatenate([m] * (lanes // 128), axis=1)
    groups = []
    for ph in range(4):
        v = dot_nt(d0[ph], w1[...])
        if ph == 0:
            v = v + dot_nt(d3[...], wsk[...])
        groups.append(m * v)
    for g, (out, table) in enumerate(((oc, tc), (om, tm), (of, tf))):
        pairs = 2 if g == 0 else 1
        side = 2 * SIDES[g]
        step = ROWS[g] // (FRAMES // pairs)
        for f in range(0, FRAMES, pairs):
            at = CUTS[g] + (f // pairs) * step
            rows = jnp.concatenate([v[at : at + step] for v in groups], axis=0).astype(BF16)
            y = dot(table[...], rows).reshape(pairs, side, 16, lanes)
            for p in range(pairs):
                out[f + p] = y[p, :, 0:side, :].astype(BF16)


def run_input_grads(d0, d3, w1, wsk, mask, tables):
    lanes = 256
    c_in = w1.shape[0]
    return pl.pallas_call(
        input_grads,
        grid=(c_in // lanes,),
        out_shape=[like((FRAMES, 2 * s, 2 * s, c_in), BF16) for s in SIDES],
        in_specs=[
            whole(d0), whole(d3),
            pl.BlockSpec((lanes, MID), lambda c: (c, 0)),
            pl.BlockSpec((lanes, C_OUT), lambda c: (c, 0)),
            whole(mask),
        ] + [whole(t) for t in tables],
        out_specs=clip_blocks(lanes),
        compiler_params=LIMIT,
        cost_estimate=FREE,
    )(d0, d3, w1, wsk, mask, *tables)


def first_grads(cnt, g0, t0, a1, s0, gb0, mask, xph, d0_ref, gr1_ref):
    m = mask[...]
    count = 4.0 * cnt[0]
    st = kstats(s0[...], count, gb0[...])
    tot = t0[...]
    for ph in range(4):
        for c in range(4):
            sl = slice(c * 128, (c + 1) * 128)
            stc = cols(st, c)
            x, _ = normalize(a1[ph, :, sl], stc)
            d = norm_back(g0[ph, :, sl], x, m, stc, (tot[0:1, sl], tot[1:2, sl]), count)
            d0_ref[ph, :, sl] = d.astype(BF16)
    c_in = xph.shape[-1]
    gr1_ref[...] = dot_tn(
        xph[...].reshape(4 * R, c_in), d0_ref[...].reshape(4 * R, MID)
    ).astype(BF16)


def last_norm(cnt, b3, y1, s6, gb6, mask, cc, cm, cf, oc, om, of, g6_ref, sums_ref, bc, bm, bf):
    @pl.when(pl.program_id(0) == 0)
    def _():
        for b in (bc, bm, bf):
            b[...] = jnp.zeros_like(b)

    lanes = g6_ref.shape[-1]
    for f in range(FRAMES):
        p = f % 2
        bc[f // 2, :, p * 4 : p * 4 + 4, :] = cc[f].astype(F32)
    bm[:, :, 0:6, :] = cm[...].astype(F32)
    bf[:, :, 0:7, :] = cf[...].astype(F32)
    cot = join((bc[...], bm[...], bf[...]))
    m = mask[...]
    m = jnp.concatenate([m] * (lanes // 128), axis=1)
    x, u = normalize(b3[...], kstats(s6[...], cnt[0], gb6[...]))
    u = u + y1[...]
    s = jax.nn.sigmoid(u)
    pc, pm, pf = split(m * u * s)
    for f in range(FRAMES):
        p = f % 2
        oc[f] = pc[f // 2, :, p * 4 : p * 4 + 4, :].astype(BF16)
    om[...] = pm[:, :, 0:6, :].astype(BF16)
    of[...] = pf[:, :, 0:7, :].astype(BF16)
    g = cot * m * (s * (1.0 + u * (1.0 - s)))
    g6_ref[...] = g
    sums_ref[...] = ksums(g * x, g)


def run_last_norm(cnt, b3, y1, s6, gb6, mask, cots):
    lanes = 256
    return pl.pallas_call(
        last_norm,
        grid=(C_OUT // lanes,),
        out_shape=[like((FRAMES, s, s, C_OUT), BF16) for s in SIDES]
        + [like((R, C_OUT)), like((2, C_OUT))],
        in_specs=[SMEM, column(R, lanes), column(R, lanes), column(2, lanes), column(2, lanes),
                  whole(mask)] + image_blocks(lanes),
        out_specs=image_blocks(lanes) + [column(R, lanes), column(2, lanes)],
        scratch_shapes=[
            pltpu.VMEM((2 if s == 4 else 4, s, 8, lanes), F32) for s in SIDES
        ],
        compiler_params=LIMIT,
        cost_estimate=FREE,
    )(cnt, b3, y1, s6, gb6, mask, *cots)


def joint_norm(cnt, a3, ap, s2, s3, gb2, gb3, mask, w2, y1_ref, yl_ref, b1_ref, sums_ref):
    lanes = y1_ref.shape[-1]
    m = mask[...]
    m = jnp.concatenate([m] * (lanes // 128), axis=1)
    _, u2 = normalize(a3[...], kstats(s2[...], cnt[0], gb2[...]))
    _, u3 = normalize(ap[...], kstats(s3[...], cnt[0], gb3[...]))
    y = m * silu(u2 + u3)
    y1_ref[...] = y
    low = y.astype(BF16)
    yl_ref[...] = low
    part = dot(low, w2[...])
    step = pl.program_id(0)

    @pl.when(step == 0)
    def _():
        b1_ref[...] = part

    @pl.when(step > 0)
    def _():
        b1_ref[...] = b1_ref[...] + part

    @pl.when(step == pl.num_programs(0) - 1)
    def _():
        b = b1_ref[...]
        sums_ref[...] = ksums(b, b * b)


def run_joint_norm(cnt, a3, ap, s2, s3, gb2, gb3, mask, w2):
    lanes = 512
    wide = column(R, lanes)
    pair = column(2, lanes)
    return pl.pallas_call(
        joint_norm,
        grid=(C_OUT // lanes,),
        out_shape=[like((R, C_OUT)), like((R, C_OUT), BF16), like((R, MID)), like((2, MID))],
        in_specs=[SMEM, wide, wide, pair, pair, pair, pair, whole(mask),
                  pl.BlockSpec((lanes, MID), lambda c: (c, 0))],
        out_specs=[wide, wide, pl.BlockSpec((R, MID), lambda c: (0, 0)),
                   pl.BlockSpec((2, MID), lambda c: (0, 0))],
        compiler_params=LIMIT,
        cost_estimate=FREE,
    )(cnt, a3, ap, s2, s3, gb2, gb3, mask, w2)


def wide_grid(kernel, outs, out_specs, ins, in_specs, scratch=(), steps=4):
    return pl.pallas_call(
        kernel,
        grid=(steps,),
        out_shape=outs,
        in_specs=in_specs,
        out_specs=out_specs,
        scratch_shapes=list(scratch),
        compiler_params=LIMIT,
        cost_estimate=FREE,
    )(*ins)


def fixed(shape):
    return pl.BlockSpec(shape, lambda c: (0,) * len(shape))


def row_block(rows, width):
    return pl.BlockSpec((rows, width), lambda c: (c, 0))


def first_step(fn):
    pl.when(pl.program_id(0) == 0)(fn)


def last_step(fn):
    pl.when(pl.program_id(0) == pl.num_programs(0) - 1)(fn)


def accumulate(ref, part):
    first = pl.program_id(0) == 0

    @pl.when(first)
    def _():
        ref[...] = part

    @pl.when(jnp.logical_not(first))
    def _():
        ref[...] = ref[...] + part


def tiled(m, lanes):
    return jnp.concatenate([m] * (lanes // 128), axis=1)


def enter(x, w, a1_ref, sums_ref):
    a = dot(x[0], w[...])
    a1_ref[0] = a
    accumulate(sums_ref, ksums(a, a * a))


def run_enter(xph, w1):
    c_in = xph.shape[-1]
    return wide_grid(
        enter,
        [like((4, R, MID)), like((2, MID))],
        [pl.BlockSpec((1, R, MID), lambda c: (c, 0, 0)), fixed((2, MID))],
        (xph, w1),
        [pl.BlockSpec((1, R, c_in), lambda c: (c, 0, 0)), fixed((c_in, MID))],
    )


def expand_pair(cnt, a2, s1, gb1, mask, w, x, wsk, h_ref, a3_ref, ap_ref, s2_ref, s3_ref):
    @first_step
    def _():
        m = tiled(mask[...], MID)
        h = m * silu(normalize(a2[...], kstats(s1[...], cnt[0], gb1[...]))[1])
        h_ref[...] = h.astype(BF16)

    a = dot(h_ref[...], w[...])
    a3_ref[...] = a
    s2_ref[...] = ksums(a, a * a)
    a = dot(x[0], wsk[...])
    ap_ref[...] = a
    s3_ref[...] = ksums(a, a * a)


def run_expand_pair(cnt, a2, s1, gb1, mask, we1, xph, wsk):
    c_in = xph.shape[-1]
    wide, pair = column(R, MID), column(2, MID)
    return wide_grid(
        expand_pair,
        [like((R, MID), BF16), like((R, C_OUT)), like((R, C_OUT)), like((2, C_OUT)), like((2, C_OUT))],
        [fixed((R, MID)), wide, wide, pair, pair],
        (cnt, a2, s1, gb1, mask, we1, xph, wsk),
        [SMEM, fixed((R, MID)), fixed((2, MID)), fixed((2, MID)), fixed((R, 128)), column(MID, MID),
         pl.BlockSpec((1, R, c_in), lambda c: (0, 0, 0)), column(c_in, MID)],
    )


def expand_last(cnt, mixed, s5, gb5, mask, w, h_ref, b3_ref, s6_ref):
    @first_step
    def _():
        m = tiled(mask[...], MID)
        h = m * silu(normalize(mixed[...], kstats(s5[...], cnt[0], gb5[...]))[1])
        h_ref[...] = h.astype(BF16)

    a = dot(h_ref[...], w[...])
    b3_ref[...] = a
    s6_ref[...] = ksums(a, a * a)


def run_expand_last(cnt, mixed, s5, gb5, mask, we2):
    wide, pair = column(R, MID), column(2, MID)
    return wide_grid(
        expand_last,
        [like((R, MID), BF16), like((R, C_OUT)), like((2, C_OUT))],
        [fixed((R, MID)), wide, pair],
        (cnt, mixed, s5, gb5, mask, we2),
        [SMEM, fixed((R, MID)), fixed((2, MID)), fixed((2, MID)), fixed((R, 128)), column(MID, MID)],
    )


def last_back(cnt, g6, b3, t6, s6, gb6, mask, w, we2, mixed, s5, gb5, ge2_ref, g5_ref, p5_ref):
    m = tiled(mask[...], MID)
    st = kstats(s6[...], cnt[0], gb6[...])
    x, _ = normalize(b3[...], st)
    tot = t6[...]
    d = norm_back(g6[...], x, m, st, (tot[0:1], tot[1:2]), cnt[0]).astype(BF16)
    ge2_ref[...] = dot_tn(w[...], d).astype(BF16)
    accumulate(g5_ref, dot_nt(d, we2[...]))

    @last_step
    def _():
        x5, u5 = normalize(mixed[...], kstats(s5[...], cnt[0], gb5[...]))
        g = g5_ref[...] * m * silu_grad(u5)
        g5_ref[...] = g
        p5_ref[...] = ksums(g * x5, g)


def run_last_back(cnt, g6, b3, t6, s6, gb6, mask, w, we2, mixed, s5, gb5):
    wide, pair = column(R, MID), column(2, MID)
    one, two = fixed((R, MID)), fixed((2, MID))
    return wide_grid(
        last_back,
        [like((MID, C_OUT), BF16), like((R, MID)), like((2, MID))],
        [column(MID, MID), one, two],
        (cnt, g6, b3, t6, s6, gb6, mask, w, we2, mixed, s5, gb5),
        [SMEM, wide, wide, pair, pair, pair, fixed((R, 128)), one, column(MID, MID), one, two, two],
    )


def joint_back(cnt, g4, t4, b1, s4, gb4, mask, yl, w2, g6, a3, ap, s2, s3, gb2, gb3,
               gr2_ref, gj_ref, pj_ref, d4_ref):
    m = tiled(mask[...], MID)

    @first_step
    def _():
        st = kstats(s4[...], cnt[0], gb4[...])
        x, _ = normalize(b1[...], st)
        tot = t4[...]
        d4_ref[...] = norm_back(g4[...], x, m, st, (tot[0:1], tot[1:2]), cnt[0]).astype(BF16)

    d = d4_ref[...]
    gr2_ref[...] = dot_tn(yl[...], d).astype(BF16)
    gy = g6[...] + dot_nt(d, w2[...])
    x2, u2 = normalize(a3[...], kstats(s2[...], cnt[0], gb2[...]))
    x3, u3 = normalize(ap[...], kstats(s3[...], cnt[0], gb3[...]))
    g = gy * m * silu_grad(u2 + u3)
    gj_ref[...] = g
    pj_ref[...] = jnp.concatenate(
        [jnp.sum(v, axis=0, keepdims=True) for v in (g * x2, g * x3, g)], axis=0
    )


def run_joint_back(cnt, g4, t4, b1, s4, gb4, mask, yl, w2, g6, a3, ap, s2, s3, gb2, gb3):
    wide, pair = column(R, MID), column(2, MID)
    one, two = fixed((R, MID)), fixed((2, MID))
    return wide_grid(
        joint_back,
        [like((C_OUT, MID), BF16), like((R, C_OUT)), like((3, C_OUT))],
        [row_block(MID, MID), wide, column(3, MID)],
        (cnt, g4, t4, b1, s4, gb4, mask, yl, w2, g6, a3, ap, s2, s3, gb2, gb3),
        [SMEM, one, two, one, two, two, fixed((R, 128)), wide, row_block(MID, MID), wide, wide, wide,
         pair, pair, pair, pair],
        [pltpu.VMEM((R, MID), BF16)],
    )


def expand_back(cnt, gj, tj, a3, ap, s2, s3, gb2, gb3, mask, h2, xph, we1, a2, s1, gb1,
                ge1_ref, gsk_ref, d3_ref, g1_ref, p1_ref):
    m = tiled(mask[...], MID)
    g = gj[...]
    tot = tj[...]
    st = kstats(s2[...], cnt[0], gb2[...])
    x, _ = normalize(a3[...], st)
    d = norm_back(g, x, m, st, (tot[0:1], tot[2:3]), cnt[0]).astype(BF16)
    ge1_ref[...] = dot_tn(h2[...], d).astype(BF16)
    accumulate(g1_ref, dot_nt(d, we1[...]))
    st = kstats(s3[...], cnt[0], gb3[...])
    x, _ = normalize(ap[...], st)
    d = norm_back(g, x, m, st, (tot[1:2], tot[2:3]), cnt[0]).astype(BF16)
    d3_ref[...] = d
    gsk_ref[...] = dot_tn(xph[0], d).astype(BF16)

    @last_step
    def _():
        x1, u1 = normalize(a2[...], kstats(s1[...], cnt[0], gb1[...]))
        g = g1_ref[...] * m * silu_grad(u1)
        g1_ref[...] = g
        p1_ref[...] = ksums(g * x1, g)


def run_expand_back(cnt, gj, tj, a3, ap, s2, s3, gb2, gb3, mask, h2, xph, we1, a2, s1, gb1):
    wide, pair = column(R, MID), column(2, MID)
    one, two = fixed((R, MID)), fixed((2, MID))
    c_in = xph.shape[-1]
    return wide_grid(
        expand_back,
        [like((MID, C_OUT), BF16), like((c_in, C_OUT), BF16), like((R, C_OUT), BF16), like((R, MID)),
         like((2, MID))],
        [column(MID, MID), column(c_in, MID), wide, one, two],
        (cnt, gj, tj, a3, ap, s2, s3, gb2, gb3, mask, h2, xph, we1, a2, s1, gb1),
        [SMEM, wide, column(3, MID), wide, wide, pair, pair, pair, pair, fixed((R, 128)), one,
         pl.BlockSpec((1, R, c_in), lambda c: (0, 0, 0)), column(MID, MID), one, two, two],
    )


def spatial_grad(cnt, g1, t1, a2, s1, gb1, mask, im, d1_ref, gsp_ref):
    @first_step
    def _():
        m = tiled(mask[...], MID)
        st = kstats(s1[...], cnt[0], gb1[...])
        x, _ = normalize(a2[...], st)
        tot = t1[...]
        d1_ref[...] = norm_back(g1[...], x, m, st, (tot[0:1], tot[1:2]), cnt[0]).astype(BF16)

    gsp_ref[...] = dot_tn(im[...], d1_ref[...]).astype(BF16)


def run_spatial_grad(cnt, g1, t1, a2, s1, gb1, mask, im):
    one, two = fixed((R, MID)), fixed((2, MID))
    return wide_grid(
        spatial_grad,
        [like((R, MID), BF16), like((9 * MID, MID), BF16)],
        [one, row_block(MID, MID)],
        (cnt, g1, t1, a2, s1, gb1, mask, im),
        [SMEM, one, two, one, two, two, fixed((R, 128)), column(R, MID)],
        steps=9,
    )


def conv_back(cnt, d1, mask, w, a1, s0, gb0, g0_ref, sums_ref, moved_ref):
    m = mask[...]
    for c in range(4):
        sl = slice(c * 128, (c + 1) * 128)
        d = d1[:, sl].astype(F32)
        for dx in (0, 1):
            moved = kshift_cols(d, dx)
            for dy in (0, 1):
                moved_ref[dy * 2 + dx, :, sl] = shift_rows(moved, dy).astype(BF16)
    st = kstats(s0[...], 4.0 * cnt[0], gb0[...])
    sums = jnp.zeros((2, MID), F32)
    for ph in range(4):
        gh = None
        for p, dy, dx, t in TAPS2:
            if p == ph:
                part = dot_nt(moved_ref[-dy * 2 - dx], w[t * MID : (t + 1) * MID, :])
                gh = part if gh is None else gh + part
        halves = []
        for c in range(4):
            sl = slice(c * 128, (c + 1) * 128)
            x, u = normalize(a1[ph, :, sl], cols(st, c))
            g = gh[:, sl] * m * silu_grad(u)
            g0_ref[ph, :, sl] = g
            halves.append(ksums(g * x, g))
        sums = sums + jnp.concatenate(halves, axis=1)
    sums_ref[...] = sums


def tie(*arrays):
    return lax.optimization_barrier(arrays)


def axes_bits(n, fsdp):
    bits = n.bit_length() - 1
    core = fsdp.bit_length() - 1
    return list(range(core)), core, core + 1, list(range(core + 2, bits))


def swap(v, d, n):
    return lax.ppermute(v, AXES, [(i, i ^ d) for i in range(n)])


def allsum_wide(vectors, n, fsdp):
    near, core, mid, far = axes_bits(n, fsdp)
    flat = jnp.concatenate([v.reshape(-1) for v in vectors])
    size = flat.shape[0]
    flat = jnp.pad(flat, (0, -size % 1024)).reshape(-1, 128)
    bits = near + [mid] + far
    rounds = [[core]] + [bits[i : i + 2] for i in range(0, len(bits), 2)]
    for r in rounds:
        got = [
            swap(flat, sum(1 << b for j, b in enumerate(r) if m >> j & 1), n)
            for m in range(1, 1 << len(r))
        ]
        flat = sum(got, flat)
    flat = flat.reshape(-1)
    out = []
    at = 0
    for v in vectors:
        out.append(flat[at : at + v.size].reshape(v.shape))
        at += v.size
    return out


def rows16(v):
    return jnp.pad(v, ((0, 0),) * (v.ndim - 2) + ((0, -v.shape[-2] % 16), (0, 0)))


def place_blocks(n, orders, core, heights, width):
    part = width // len(orders)

    def kernel(me_ref, *refs):
        srcs = refs[: 2 * len(orders)]
        outs = refs[2 * len(orders) : -1]
        sem = refs[-1]
        me = me_ref[0]
        for rel in range(n):
            for k, order in enumerate(orders):
                at = sum((rel >> b & 1) << j for j, b in enumerate(order))
                src = srcs[2 * k + (rel >> core & 1)]
                row = 0
                for i, (h, out) in enumerate(zip(heights, outs)):
                    pltpu.make_async_copy(
                        src.at[at, pl.ds(row, h)],
                        out.at[me ^ rel, :, pl.ds(k * part, part)],
                        sem.at[i],
                    ).start()
                    row += h
        for i, out in enumerate(outs):
            pltpu.make_async_copy(out, out, sem.at[i]).wait()

    return pl.pallas_call(
        kernel,
        out_shape=[jax.ShapeDtypeStruct((n, h, width), BF16) for h in heights],
        in_specs=[SMEM] + [pl.BlockSpec(memory_space=pl.ANY)] * (2 * len(orders)),
        out_specs=[VMEM] * len(heights),
        scratch_shapes=[pltpu.SemaphoreType.DMA((len(heights),))],
        compiler_params=LIMIT,
        cost_estimate=FREE,
    )


class Gather:
    def __init__(self, shards, n, fsdp):
        self.n = n
        self.near, self.core, self.mid, self.far = axes_bits(n, fsdp)
        self.shards = shards
        padded = [rows16(v.astype(BF16)) for v in shards]
        self.heights = [v.shape[0] for v in padded]
        self.x = jnp.concatenate(padded, axis=0) if len(padded) > 1 else padded[0]

    def first(self):
        got = []
        for m in range(1, 1 << len(self.far)):
            got.append(swap(self.x, sum(1 << b for j, b in enumerate(self.far) if m >> j & 1), self.n))
        self.hops = [self.x] + got

    def second(self):
        n = self.n
        bits = self.near + [self.mid]
        v = jnp.stack(self.hops)
        got = [v]
        for m in range(1, 1 << len(bits)):
            got.append(swap(v, sum(1 << b for j, b in enumerate(bits) if m >> j & 1), n))
        self.planes = [jnp.concatenate(got, axis=0)]
        self.orders = [self.far + bits]

    def split(self):
        width = self.x.shape[1]
        bits = self.near + [self.mid]
        self.paths = [bits, bits[::-1]]
        self.orders = [self.far + path for path in self.paths]
        v = jnp.stack(self.hops)
        self.planes = [v[..., : width // 2], v[..., width // 2 :]]

    def hop(self, k):
        self.got = [swap(v, 1 << p[k], self.n) for v, p in zip(self.planes, self.paths)]

    def land(self):
        self.planes = [jnp.concatenate([v, g], axis=0) for v, g in zip(self.planes, self.got)]

    def third(self):
        self.other = [swap(v, 1 << self.core, self.n) for v in self.planes]

    def finish(self, me):
        width = self.x.shape[1]
        planes = [v for pair in zip(self.planes, self.other) for v in pair]
        outs = place_blocks(self.n, self.orders, self.core, self.heights, width)(me, *planes)
        return [
            o.reshape(self.n * h, width)
            if h == v.shape[0]
            else o[:, : v.shape[0]].reshape(-1, width)
            for o, h, v in zip(outs, self.heights, self.shards)
        ]


def order_blocks(n, orders, pieces, width, arrays):
    heights = [arrays[i].shape[1] for i, _ in pieces]
    total = sum(heights)
    half = width // 2

    def kernel(me_ref, *refs):
        srcs = refs[: len(arrays)]
        outs = refs[len(arrays) : len(arrays) + 2]
        sem = refs[-1]
        me = me_ref[0]
        for rel in range(n):
            for k, order in enumerate(orders):
                at = 0
                for b in order:
                    at = at * 2 + (rel >> b & 1)
                side = at * 2 // n
                row = 0
                for (i, col), h in zip(pieces, heights):
                    pltpu.make_async_copy(
                        srcs[i].at[me ^ rel, :, pl.ds(col + k * half, half)],
                        outs[side].at[k, at % (n // 2), pl.ds(row, h)],
                        sem.at[side],
                    ).start()
                    row += h
        for k, out in enumerate(outs):
            pltpu.make_async_copy(out, out, sem.at[k]).wait()

    return pl.pallas_call(
        kernel,
        out_shape=[jax.ShapeDtypeStruct((2, n // 2, total, half), BF16)] * 2,
        in_specs=[SMEM] + [pl.BlockSpec(memory_space=pl.ANY)] * len(arrays),
        out_specs=[VMEM] * 2,
        scratch_shapes=[pltpu.SemaphoreType.DMA((2,))],
        compiler_params=LIMIT,
        cost_estimate=FREE,
    )


def add_blocks(keep, got, joined):
    m, rows, half = keep[0].shape[-3:]
    k_in = len(keep)

    def kernel(*refs):
        ins, outs = refs[: 2 * k_in], refs[2 * k_in :]

        def total(k, i):
            if k_in == 1:
                return ins[0][k, i].astype(F32) + ins[1][k, i].astype(F32)
            return ins[k][i].astype(F32) + ins[2 + k][i].astype(F32)

        if m == 1:
            for k in range(2):
                outs[0][:, k * half : (k + 1) * half] = total(k, 0)
            return

        @pl.loop(0, m // 2)
        def _(i):
            for k in range(2):
                for side in range(2):
                    v = total(k, i + side * (m // 2)).astype(BF16)
                    if joined:
                        outs[side][k, i] = v
                    else:
                        outs[2 * side + k][i] = v

    if m == 1:
        outs = [like((rows, 2 * half))]
    elif joined:
        outs = [like((2, m // 2, rows, half), BF16)] * 2
    else:
        outs = [like((m // 2, rows, half), BF16)] * 4
    return call(kernel, outs, 2 * k_in, scalars=0)(*keep, *got)


class Scatter:
    def __init__(self, me, arrays, pieces, width, n, fsdp):
        self.n = n
        near, core, mid, self.far = axes_bits(n, fsdp)
        bits = near + [mid]
        self.paths = [bits, bits[::-1]]
        self.heights = [arrays[i].shape[1] for i, _ in pieces]
        orders = [[core] + path + self.far for path in self.paths]
        send, keep = order_blocks(n, orders, pieces, width, arrays)(me, *arrays)[::-1]
        self.send, self.keep = [send], [keep]
        self.hops = [[core]] + list(zip(*self.paths)) + [[b] for b in self.far]
        self.at = 0

    def start(self):
        self.got = [swap(v, 1 << b, self.n) for v, b in zip(self.send, self.hops[self.at])]
        self.at += 1

    def add(self):
        after = self.hops[self.at : self.at + 1]
        got = add_blocks(self.keep, self.got, bool(after) and len(after[0]) == 1)
        if not after:
            self.total = got[0]
        else:
            k = len(got) // 2
            self.keep, self.send = got[:k], got[k:]

    def end(self, x):
        x, *self.got = tie(x, *self.got)
        return x

    def ready(self, x):
        x, *self.send = tie(x, *self.send)
        self.start()
        return x

    def rest(self):
        self.add()
        while self.at < len(self.hops):
            self.start()
            self.add()
        out = []
        at = 0
        for h in self.heights:
            out.append(self.total[at : at + h])
            at += h
        return out


def body(n, fsdp, *args):
    (coarse, medium, fine, clip_counts, frame_counts, reduce_one, spatial_one, expand_one,
     shortcut_one, reduce_two, excite_down, excite_up, temporal_mix, expand_two, norm_params,
     motion_kernel, cot_c, cot_m, cot_f) = args
    near, core, mid, far = axes_bits(n, fsdp)

    def gather(w):
        return lax.all_gather(w.astype(BF16), AXES, axis=0, tiled=True)

    def flat(w):
        v = w.reshape(-1)
        return jnp.pad(v, (0, -v.size % MID)).reshape(-1, MID)

    def flat_back(got, w):
        return got.reshape(n, -1)[:, : w.size].reshape((n,) + w.shape)

    alive = (jnp.arange(4)[None, :] < frame_counts[0][:, None]) & (clip_counts[0][:, None] > 0)
    alive = alive.astype(F32)
    later = jnp.pad(alive[:, 1:], ((0, 0), (0, 1)))
    alive_slots = alive.reshape(12)
    later_slots = later.reshape(12)
    mask = (jnp.asarray(SPREAD) @ alive_slots)[:, None]
    per_group = jnp.sum(alive, axis=1)
    local_out = jnp.sum(per_group * jnp.array([16.0, 36.0, 49.0], F32))

    tables = [jnp.asarray(t, BF16) for t in PHASES]
    tables_t = [jnp.asarray(t.T, BF16) for t in PHASES]
    clips = [coarse, medium, fine]

    m128 = jnp.broadcast_to(mask, (R, 128))
    valid = jnp.asarray(np.broadcast_to(VALID[:, None], (R, MID)).astype(np.float32))
    scale = later_slots / jnp.asarray(NPIX)
    scale = jnp.broadcast_to(jnp.pad(scale, (0, 4))[:, None], (16, SQUEEZE))
    table = jnp.asarray(TABLE, BF16)
    table_t = jnp.asarray(TABLE.T, BF16)
    spread = jnp.asarray(SPREAD3, BF16)
    me = lax.axis_index(AXES).astype(jnp.int32).reshape(1)
    ga = Gather([reduce_one, flat(norm_params)], n, fsdp)
    gb_ = Gather([spatial_one], n, fsdp)
    gc_ = Gather([shortcut_one, expand_one], n, fsdp)
    narrow = [reduce_two, flat(excite_down), flat(excite_up), flat(temporal_mix)]
    rows = [v.shape[0] for v in narrow]
    narrow = jnp.concatenate(narrow, axis=0)
    got = gather(jnp.pad(narrow, ((0, -narrow.shape[0] % 16), (0, 0))))
    we2 = gather(expand_two)
    ga.first()
    *ga.hops, gb_.x, clips[0], clips[1], clips[2] = tie(*ga.hops, gb_.x, *clips)
    ga.second()
    gb_.first()
    xph = run_split(alive_slots, clips, tables)
    ga.planes[0], xph = tie(ga.planes[0], xph)
    ga.third()
    w1, norms = ga.finish(me)
    norms = flat_back(norms, norm_params).transpose(1, 0, 2).reshape(2, -1).astype(F32)
    edges = [0, 512, 1024, 3072, 5120, 5632, 6144, 8192]
    gb = [norms[:, edges[k] : edges[k + 1]] for k in range(7)]

    w1, gc_.x, *gb_.hops = tie(w1, gc_.x, *gb_.hops)
    gb_.split()
    w1, *gb_.planes = tie(w1, *gb_.planes)
    gb_.hop(0)
    gc_.first()
    a1, p0 = run_enter(xph, w1)
    for k in range(1, len(gb_.paths[0])):
        p0, *gb_.got = tie(p0, *gb_.got)
        gb_.land()
        p0, *gb_.planes = tie(p0, *gb_.planes)
        gb_.hop(k)
    s0, count_out = allsum((p0, local_out.reshape(1)), n)
    cnt = count_out.reshape(1)
    s0, *rest = tie(s0, *gb_.got, *gc_.hops)
    gb_.got, gc_.hops = rest[:2], rest[2:]
    gb_.land()
    gb_.third()
    gc_.split()
    gc_.hop(0)
    wsp, = gb_.finish(me)
    im, a2, p1 = call(
        conv_forward,
        [like((R, 9 * MID), BF16), like((R, MID)), like((2, MID))],
        6,
    )(cnt, a1, s0, gb[0], m128, valid, wsp)
    for k in range(1, len(gc_.paths[0])):
        p1, *gc_.got = tie(p1, *gc_.got)
        gc_.land()
        p1, *gc_.planes = tie(p1, *gc_.planes)
        gc_.hop(k)
    s1, = allsum((p1,), n)
    s1, *gc_.got = tie(s1, *gc_.got)
    gc_.land()
    gc_.third()
    wsk, we1 = gc_.finish(me)
    got = got.reshape(n, -1, MID)
    w2 = got[:, : rows[0]].reshape(C_OUT, MID)
    at = rows[0]
    wdown = flat_back(got[:, at : at + rows[1]], excite_down).reshape(MID, SQUEEZE)
    at += rows[1]
    wup = flat_back(got[:, at : at + rows[2]], excite_up)
    wup = wup.transpose(1, 0, 2).reshape(SQUEEZE, MID).astype(F32)
    at += rows[2]
    wmix = flat_back(got[:, at : at + rows[3]], temporal_mix)
    wmix = wmix.transpose(1, 0, 2).reshape(3, 9 * GROUP, GROUP)
    wmix_t = wmix.reshape(3, 9, GROUP, GROUP).transpose(0, 1, 3, 2).reshape(3, 9 * GROUP, GROUP)
    h2, a3, ap, p2, p3 = run_expand_pair(cnt, a2, s1, gb[1], m128, we1, xph, wsk)
    s2, s3 = allsum_wide((p2, p3), n, fsdp)
    y1, y1_low, b1, p4 = run_joint_norm(cnt, a3, ap, s2, s3, gb[2], gb[3], m128, w2)
    s4, = allsum((p4,), n)
    z, z_low, mixed, mix_im, sig, pooled, wnext, p5 = call(
        mix_forward,
        [like((R, MID)), like((R, MID), BF16), like((R, MID)), like((3, R, 9 * GROUP), BF16),
         like((16, MID)), like((16, SQUEEZE)), like((144, SQUEEZE)), like((2, MID))],
        11,
    )(cnt, b1, s4, gb[4], m128, wdown, wup, wmix, motion_kernel, scale, table, spread)
    s5, = allsum((p5,), n)
    w, b3, p6 = run_expand_last(cnt, mixed, s5, gb[5], m128, we2)
    s6, = allsum((p6,), n)
    o_c, o_m, o_f, g6, p6 = run_last_norm(cnt, b3, y1, s6, gb[6], m128, (cot_c, cot_m, cot_f))

    t6, = allsum((p6,), n)
    ge2, g5, p5 = run_last_back(cnt, g6, b3, t6, s6, gb[6], m128, w, we2, mixed, s5, gb[5])
    t5, = allsum((p5,), n)
    g4, p4, gkernel, gmix, gdown, gup = call(
        mix_backward,
        [like((R, MID)), like((2, MID)), like((16, SQUEEZE)), like((3, 9 * GROUP, GROUP), BF16),
         like((MID, SQUEEZE)), like((SQUEEZE, MID))],
        22,
        [pltpu.VMEM((R, 9 * GROUP), BF16), pltpu.VMEM((R, MID), F32)],
    )(cnt, g5, t5, mixed, s5, gb[5], m128, mix_im, wmix_t, z, sig, pooled, wnext,
      wup, motion_kernel, scale, table_t, spread, z_low, wdown, b1, s4, gb[4])
    t4, gkernel = allsum((p4, gkernel), n)
    gkernel = gkernel[:9]
    gr2, gj, pj = run_joint_back(cnt, g4, t4, b1, s4, gb[4], m128, y1_low, w2, g6, a3, ap, s2, s3,
                                 gb[2], gb[3])

    gmix = gmix.reshape(27, n, GROUP * GROUP // n).transpose(1, 0, 2).reshape(n, -1)
    gup = gup.reshape(SQUEEZE, n, MID // n).transpose(1, 0, 2).reshape(n, -1)
    thin = jnp.concatenate([gmix, gdown.reshape(n, -1).astype(BF16), gup.astype(BF16)], axis=1)
    thin = jnp.pad(thin, ((0, 0), (0, -thin.shape[1] % (16 * MID)))).reshape(n, -1, MID)

    def blocks(v):
        return rows16(v.reshape(n, -1, v.shape[-1]))

    starts = list(range(0, C_OUT, MID))
    ra = Scatter(
        me, [blocks(gr2), thin, blocks(ge2)], [(0, 0), (1, 0)] + [(2, c) for c in starts], MID,
        n, fsdp,
    )
    pj = ra.ready(pj)
    tj, = allsum_wide((pj,), n, fsdp)
    tj = ra.end(tj)
    ra.add()
    tj = ra.ready(tj)
    ge1, gsk, d3, g1, p1 = run_expand_back(cnt, gj, tj, a3, ap, s2, s3, gb[2], gb[3], m128, h2, xph,
                                           we1, a2, s1, gb[1])
    p1 = ra.end(p1)
    t1, = allsum((p1,), n)
    ra.add()
    rb = Scatter(
        me, [blocks(ge1), blocks(gsk)], [(i, c) for i in range(2) for c in starts], MID, n, fsdp
    )
    t1 = rb.ready(ra.ready(t1))
    d1, gsp = run_spatial_grad(cnt, g1, t1, a2, s1, gb[1], m128, im)
    d1 = rb.end(ra.end(d1))
    rb.add()
    ra.add()
    d1 = ra.ready(rb.ready(d1))
    gsp, d1 = tie(gsp, d1)
    rc = Scatter(me, [blocks(gsp)], [(0, 0)], MID, n, fsdp)
    d1 = rc.ready(d1)
    g0, p0 = call(
        conv_back, [like((4, R, MID)), like((2, MID))], 6, [pltpu.VMEM((4, R, MID), BF16)]
    )(cnt, d1, m128, wsp, a1, s0, gb[0])
    p0 = rc.end(rb.end(ra.end(p0)))
    t0, = allsum((p0,), n)
    rc.add()
    rb.add()
    ra.add()
    t0 = ra.ready(rb.ready(rc.ready(t0)))
    d0, gr1 = call(
        first_grads,
        [like((4, R, MID), BF16), like((xph.shape[-1], MID), BF16)],
        7,
    )(cnt, g0, t0, a1, s0, gb[0], m128, xph)
    gr1 = blocks(gr1)
    d0 = rc.end(rb.end(d0))
    rc.add()
    rb.add()
    d0 = rb.ready(rc.ready(d0))
    d0, gr1 = tie(d0, gr1)
    got = lax.all_to_all(gr1, AXES, 0, 0, tiled=True)
    gin = run_input_grads(d0, d3, w1, wsk, m128, tables_t)
    gin = list(gin)
    gin[0] = rc.end(rb.end(gin[0]))
    gr1 = jnp.sum(got.astype(F32), axis=0)[: reduce_one.shape[0]]
    second = ra.rest()
    first = rb.rest()
    gsp = rc.rest()[0][: spatial_one.shape[0]]

    def wide_back(parts, like_):
        return jnp.concatenate([p[: like_.shape[0]] for p in parts], axis=1)

    thin = second[1].reshape(-1)
    s1_ = temporal_mix.size
    s2_ = s1_ + excite_down.size
    s3_ = s2_ + excite_up.size

    gain = jnp.concatenate([t0[0], t1[0], tj[0], tj[1], t4[0], t5[0], t6[0]])
    bias = jnp.concatenate([t0[1], t1[1], tj[2], tj[2], t4[1], t5[1], t6[1]])
    gnorm = lax.dynamic_slice_in_dim(jnp.stack([gain, bias]), me[0] * (8192 // n), 8192 // n, 1)
    return (
        o_c, o_m, o_f, gin[0], gin[1], gin[2],
        gr1,
        gsp,
        wide_back(first[:4], expand_one),
        wide_back(first[4:], shortcut_one),
        second[0][: reduce_two.shape[0]],
        thin[s1_:s2_].reshape(excite_down.shape),
        thin[s2_:s3_].reshape(excite_up.shape),
        thin[:s1_].reshape(temporal_mix.shape),
        wide_back(second[2:], expand_two),
        gnorm,
        gkernel,
    )


def solution(mesh):
    n = mesh.shape["dp"] * mesh.shape["fsdp"]
    rows = P(AXES, None)
    cols = P(None, AXES)
    image = P(AXES, None, None, None)
    return jax.shard_map(
        partial(body, n, mesh.shape["fsdp"]),
        mesh=mesh,
        in_specs=(image, image, image, rows, rows, rows, rows, rows, rows, rows, rows, cols, cols,
                  rows, cols, P(), image, image, image),
        out_specs=(image, image, image, image, image, image, rows, rows, rows, rows, rows, rows,
                   cols, cols, rows, cols, P()),
        check_vma=False,
    )
```

```python
from functools import partial

import jax
import jax.numpy as jnp
from jax import lax
from jax.experimental import pallas as pl
from jax.experimental.pallas import tpu as pltpu
from jax.sharding import PartitionSpec as P
import numpy as np

MID = 512
C_OUT = 2048
FRAMES = 4
GROUP = 128
SHIFT = 16
SQUEEZE = 32
SIDES = (4, 6, 7)
AXES = ("dp", "fsdp")
EPS = 1e-05
HIGHEST = lax.Precision.HIGHEST
F32 = jnp.float32
BF16 = jnp.bfloat16

ROWS = (64, 192, 224)
CUTS = (0, 64, 256, 480)
R = 480


def row_tables():
    frame = np.zeros(R, np.int32)
    row = np.zeros(R, np.int32)
    col = np.zeros(R, np.int32)
    group = np.zeros(R, np.int32)
    at = 0
    for a in range(2):
        for i in range(4):
            for p in range(2):
                for j in range(4):
                    frame[at], row[at], col[at], group[at] = 2 * a + p, i, j, 0
                    at += 1
    for g in (1, 2):
        for f in range(4):
            for i in range(SIDES[g]):
                for j in range(8):
                    frame[at], row[at], col[at], group[at] = f, i, j, g
                    at += 1
    side = np.array(SIDES)[group]
    return group, frame, row, col, (col < side), side


GROUP_OF, FRAME_OF, ROW_OF, COL_OF, VALID, SIDE_OF = row_tables()
SLOT_OF = GROUP_OF * FRAMES + FRAME_OF


def window_table():
    table = np.zeros((12, 9, R), np.float32)
    for r in range(R):
        if not VALID[r]:
            continue
        for t in range(9):
            dy, dx = t // 3 - 1, t % 3 - 1
            i, j = ROW_OF[r] - dy, COL_OF[r] - dx
            if 0 <= i < SIDE_OF[r] and 0 <= j < SIDE_OF[r]:
                table[SLOT_OF[r], t, r] = 1.0
    return table.reshape(108, R)


WINDOWS = window_table()
SPREAD = ((SLOT_OF[:, None] == np.arange(12)[None]) & VALID[:, None]).astype(np.float32)
NPIX = np.repeat(np.array([s * s for s in SIDES], np.float32), FRAMES)


def split(v):
    c = v.shape[-1]
    return (
        v[0:64].reshape(2, 4, 8, c),
        v[64:256].reshape(4, 6, 8, c),
        v[256:480].reshape(4, 7, 8, c),
    )


def join(parts):
    return jnp.concatenate([p.reshape(-1, p.shape[-1]) for p in parts], axis=0)


def shift_rows(v, dy):
    if dy == 0:
        return v
    out = []
    for p in split(v):
        zero = jnp.zeros_like(p[:, :1])
        out.append(
            jnp.concatenate([p[:, 1:], zero] if dy > 0 else [zero, p[:, :-1]], axis=1)
        )
    return join(out)


def dot(a, b):
    return jnp.dot(a, b, preferred_element_type=F32)


def dot_nt(a, b):
    return lax.dot_general(a, b, (((1,), (1,)), ((), ())), preferred_element_type=F32)


def dot_tn(a, b):
    return lax.dot_general(a, b, (((0,), (0,)), ((), ())), preferred_element_type=F32)


def normalize(a, st):
    mean, rstd, gain, bias = st
    xhat = (a - mean) * rstd
    return xhat, xhat * gain + bias


def silu(u):
    return u * jax.nn.sigmoid(u)


def silu_grad(u):
    s = jax.nn.sigmoid(u)
    return s * (1.0 + u * (1.0 - s))


def norm_back(g, xhat, mask, st, tot, count):
    mean, rstd, gain, bias = st
    return gain * rstd * (g - mask * (tot[1] + xhat * tot[0]) / count)


TAPS2 = []
for kh in range(3):
    for kw in range(3):
        pr, dy = (1, -1) if kh == 0 else ((0, 0) if kh == 1 else (1, 0))
        pc, dx = (1, -1) if kw == 0 else ((0, 0) if kw == 1 else (1, 0))
        TAPS2.append((pr * 2 + pc, dy, dx, kh * 3 + kw))


FREE = pl.CostEstimate(flops=0, bytes_accessed=0, transcendentals=0)
LONG = pl.CostEstimate(flops=20 * 10**9, bytes_accessed=60 * 10**6, transcendentals=0)
VMEM = pl.BlockSpec(memory_space=pltpu.VMEM)
SMEM = pl.BlockSpec(memory_space=pltpu.SMEM)


def call(kernel, outs, n_in, scratch=(), scalars=1):
    return pl.pallas_call(
        kernel,
        out_shape=outs,
        in_specs=[SMEM] * scalars + [VMEM] * n_in,
        out_specs=[VMEM] * len(outs),
        scratch_shapes=list(scratch),
        compiler_params=LIMIT,
        cost_estimate=FREE,
    )


def like(shape, dtype=F32):
    return jax.ShapeDtypeStruct(shape, dtype)


def kshift_cols(v, dx):
    if dx == 0:
        return v
    c = v.shape[-1]
    rolled = pltpu.roll(v.reshape(R // 8, 8, c), 1 if dx < 0 else 7, 1).reshape(R, c)
    top = rolled[:64]
    place = lax.broadcasted_iota(jnp.int32, (64, c), 0) & 3
    top = jnp.where(place == (0 if dx < 0 else 3), 0.0, top)
    return jnp.concatenate([top, rolled[64:]], axis=0)


def kshift_frame(v, df):
    c = v.shape[-1]
    pc, pm, pf = split(v)
    half = pltpu.roll(pc.reshape(8, 8, c), 4, 1).reshape(2, 4, 8, c)
    zero = jnp.zeros_like(half[:1])
    first = lax.broadcasted_iota(jnp.int32, (2, 4, 8, c), 2) < 4
    if df < 0:
        oc = jnp.where(first, jnp.concatenate([zero, half[:-1]], axis=0), half)
    else:
        oc = jnp.where(first, half, jnp.concatenate([half[1:], zero], axis=0))
    out = [oc]
    for p in (pm, pf):
        zero = jnp.zeros_like(p[:1])
        out.append(jnp.concatenate([p[1:], zero] if df > 0 else [zero, p[:-1]], axis=0))
    return join(out)


def ktime_shift(v, back):
    lane = lax.broadcasted_iota(jnp.int32, v.shape, 1)
    a = kshift_frame(v, 1 if back else -1)
    b = kshift_frame(v, -1 if back else 1)
    return jnp.where(lane < SHIFT, a, jnp.where(lane < 2 * SHIFT, b, v))


def cols(st, c, w=128):
    return tuple(v[:, c * w : (c + 1) * w] for v in st)


def three(v):
    a = v.astype(BF16)
    rest = v - a.astype(F32)
    b = rest.astype(BF16)
    c = (rest - b.astype(F32)).astype(BF16)
    return a, b, c


def exact_dot(table, v):
    return sum(dot(table, part) for part in three(v))


def frame_sums(v):
    pc, pm, pf = split(v)
    first = lax.broadcasted_iota(jnp.int32, (2, 4, 8, v.shape[-1]), 2) < 4
    even = jnp.sum(jnp.where(first, pc, 0.0), axis=(1, 2))
    odd = jnp.sum(jnp.where(first, 0.0, pc), axis=(1, 2))
    pm = jnp.sum(pm, axis=(1, 2))
    pf = jnp.sum(pf, axis=(1, 2))
    rows = [even[0:1], odd[0:1], even[1:2], odd[1:2]]
    rows += [pm[f : f + 1] for f in range(4)] + [pf[f : f + 1] for f in range(4)]
    return jnp.concatenate(rows + [jnp.zeros((4, v.shape[-1]), F32)], axis=0)


def window_tables():
    pixel = WINDOWS.reshape(12, 9, R)
    table = np.zeros((160, R), np.float32)
    for slot in range(12):
        if slot % 4 < 3:
            for t in range(9):
                table[t * 16 + slot] = pixel[slot + 1, t]
        table[144 + slot] = pixel[slot, 4]
    spread = np.zeros((R, 16), np.float32)
    spread[:, :12] = SPREAD
    return table, np.concatenate([spread] * 3, axis=1)


TABLE, SPREAD3 = window_tables()


def phase_tables():
    out = []
    for side, pairs in zip(SIDES, (2, 1, 1)):
        high = 2 * side
        wide = 4 if side == 4 else 8
        count = side * wide * pairs
        t = np.zeros((4 * count, pairs * high * 16), np.float32)
        for ph in range(4):
            for p in range(pairs):
                for i in range(side):
                    for j in range(side):
                        row = ph * count + (i * pairs + p) * wide + j
                        at = (p * high + 2 * i + ph // 2) * 16 + 2 * j + ph % 2
                        t[row, at] = 1.0
        out.append(t)
    return out


PHASES = phase_tables()


def split_phases(alive, xc, xm, xf, tc, tm, tf, out_ref, bc, bm, bf):
    @pl.when(pl.program_id(0) == 0)
    def _():
        for b in (bc, bm, bf):
            b[...] = jnp.zeros_like(b)

    pieces = [[], [], [], []]
    lanes = out_ref.shape[-1]
    for g, (x, table, buf) in enumerate(((xc, tc, bc), (xm, tm, bm), (xf, tf, bf))):
        pairs = buf.shape[0]
        side = 2 * SIDES[g]
        for f in range(0, FRAMES, pairs):
            for p in range(pairs):
                live = alive[g * FRAMES + f + p] > 0.0
                buf[p, :, 0:side, :] = jnp.where(live, x[f + p], jnp.zeros_like(x[f + p]))
            y = dot(table[...], buf[...].reshape(-1, lanes))
            step = y.shape[0] // 4
            for ph in range(4):
                pieces[ph].append(y[ph * step : (ph + 1) * step])
    for ph in range(4):
        out_ref[ph] = jnp.concatenate(pieces[ph], axis=0).astype(BF16)


def clip_blocks(lanes):
    return [
        pl.BlockSpec((FRAMES, 2 * s, 2 * s, lanes), lambda c: (0, 0, 0, c)) for s in SIDES
    ]


def whole(v):
    return pl.BlockSpec(v.shape, lambda c: (0,) * v.ndim)


LIMIT = pltpu.CompilerParams(vmem_limit_bytes=60 * 2**20)


def run_split(alive, clips, tables):
    lanes = 256
    c_in = clips[0].shape[-1]
    return pl.pallas_call(
        split_phases,
        grid=(c_in // lanes,),
        out_shape=like((4, R, c_in), BF16),
        in_specs=[SMEM] + clip_blocks(lanes) + [whole(t) for t in tables],
        out_specs=pl.BlockSpec((4, R, lanes), lambda c: (0, 0, c)),
        scratch_shapes=[
            pltpu.VMEM((2 if s == 4 else 1, 2 * s, 16, lanes), BF16) for s in SIDES
        ],
        compiler_params=LIMIT,
        cost_estimate=FREE,
    )(alive, *clips, *tables)


def tiled(m, lanes):
    return jnp.concatenate([m] * (lanes // 128), axis=1)


class Flow:
    def __init__(self, far, near, sem, parts, axis, out):
        self.far, self.v, self.sem = far, near, sem
        self.parts, self.axis, self.out = parts, axis, out

    def copy(self, c):
        size = self.v.shape[self.axis] // self.parts
        at = [slice(None)] * len(self.v.shape)
        at[self.axis] = pl.ds(c * size, size)
        a, b = self.far.at[tuple(at)], self.v.at[tuple(at)]
        return pltpu.make_async_copy(*((b, a) if self.out else (a, b)), self.sem.at[c])

    def get(self, c=0):
        self.copy(c).wait()

    def put(self, c=0):
        self.copy(c).start()


class Plain:
    def __init__(self, ref):
        self.v = ref

    def get(self, c=0):
        pass

    def put(self, c=0):
        pass


def plain_call(body, scalars, small, ins, outs, small_outs=(), scratch=(), only=()):
    n_s, n_m, n_i, n_o, n_p = len(scalars), len(small), len(ins), len(outs), len(small_outs)

    def kernel(*refs):
        at = 0

        def take(k):
            nonlocal at
            at += k
            return refs[at - k : at]

        s, m, fi, fo, so = take(n_s), take(n_m), take(n_i), take(n_o), take(n_p)
        body(s, m, [Plain(r) for r in fi], [Plain(r) for r in fo], so, take(len(scratch)))

    return pl.pallas_call(
        kernel,
        out_shape=[like(o[0], o[1]) for o in outs] + list(small_outs),
        in_specs=[SMEM] * n_s + [VMEM] * (n_m + n_i),
        out_specs=[VMEM] * (n_o + n_p),
        scratch_shapes=list(scratch),
        compiler_params=LIMIT,
        cost_estimate=FREE,
    )(*scalars, *small, *[v for v, _, _ in ins])


def flow_call(body, scalars, small, ins, outs, small_outs=(), scratch=(), only=(), cost=FREE):
    n_s, n_m, n_i, n_o, n_p = len(scalars), len(small), len(ins), len(outs), len(small_outs)

    def kernel(*refs):
        at = 0

        def take(k):
            nonlocal at
            at += k
            return refs[at - k : at]

        s, m, far_in, far_out, so = take(n_s), take(n_m), take(n_i), take(n_o), take(n_p)
        near_in, near_out, extra = take(n_i), take(n_o), take(len(scratch))
        sem_in, sem_out = take(n_i), take(n_o)
        fi = [
            Flow(f, v, q, p, a, False)
            for f, v, q, (_, p, a) in zip(far_in, near_in, sem_in, ins)
        ]
        fo = [
            Flow(f, v, q, p, a, True)
            for f, v, q, (_, _, p, a) in zip(far_out, near_out, sem_out, outs)
        ]
        for c in range(max([f.parts for f in fi])):
            for i, f in enumerate(fi):
                if c < f.parts and (c == 0 or i not in only):
                    f.put(c)
        body(s, m, fi, fo, so, extra)
        for f in fo:
            for c in range(f.parts):
                f.get(c)

    any_space = pl.BlockSpec(memory_space=pl.ANY)
    return pl.pallas_call(
        kernel,
        out_shape=[like(o[0], o[1]) for o in outs] + list(small_outs),
        in_specs=[SMEM] * n_s + [VMEM] * n_m + [any_space] * n_i,
        out_specs=[any_space] * n_o + [VMEM] * n_p,
        scratch_shapes=[pltpu.VMEM(v.shape, v.dtype) for v, _, _ in ins]
        + [pltpu.VMEM(o[0], o[1]) for o in outs]
        + list(scratch)
        + [pltpu.SemaphoreType.DMA((p,)) for _, p, _ in ins]
        + [pltpu.SemaphoreType.DMA((o[2],)) for o in outs],
        compiler_params=LIMIT,
        cost_estimate=cost,
    )(*scalars, *small, *[v for v, _, _ in ins])


def put_rows(ref, row, vec):
    for j in range(vec.shape[1] // 128):
        ref[row + j : row + j + 1, :] = vec[:, j * 128 : (j + 1) * 128]


def get_rows(t, row, width):
    return jnp.concatenate([t[row + j : row + j + 1, :] for j in range(width // 128)], axis=1)


def spread_rows(ref, rows):
    @pl.loop(0, ref.shape[0])
    def _(i):
        ref[i] = rows


def pack_sums(a, b):
    out = []
    for v in (a, b):
        v = jnp.sum(v, axis=0, keepdims=True)
        out += [v[:, j * 128 : (j + 1) * 128] for j in range(v.shape[1] // 128)]
    return jnp.concatenate(out, axis=0)


def stats_of(got, count, gb, row=0, second=4, width=MID, lane=0):
    mean = get_rows(got, row, width) / count
    var = get_rows(got, second, width) / count - mean * mean
    sl = slice(lane, lane + width)
    return mean, lax.rsqrt(var + EPS), gb[0:1, sl], gb[1:2, sl]


def total_of(ref):
    return jnp.sum(ref[...], axis=0) if len(ref.shape) == 3 else ref[...]


def wide_stats(got, count, gb, c, base=0):
    return stats_of(got, count, gb, base + 4 * c, base + 16 + 4 * c, MID, c * MID)


def enter(s, m, ins, outs, so, extra):
    (x, w), (a1,) = ins, outs
    w.get()
    total = jnp.zeros((8, 128), F32)
    for ph in range(4):
        x.get(ph)
        a = dot(x.v[ph], w.v[...])
        a1.v[ph] = a
        a1.put(ph)
        total = total + pack_sums(a, a * a)
    spread_rows(so[0], total)


def run_enter(n, xph, w1):
    return flow_call(
        enter, (), (), [(w1, 1, 0), (xph, 4, 0)][::-1], [((4, R, MID), F32, 4, 0)],
        [like((n, 8, 128))],
    )


def conv_forward(s, m, ins, outs, so, extra):
    (cnt,), (s0, gb0, mask), (a1, w), (im, a2) = s, m, ins, outs
    live = mask[...]
    st = stats_of(total_of(s0), 4.0 * cnt[0], gb0[...])
    acc = None
    for ph in range(4):
        a1.get(ph)
        taps = [q for q in TAPS2 if q[0] == ph]
        for c in range(4):
            sl = slice(c * 128, (c + 1) * 128)
            stc = cols(st, c)
            h = live * silu(normalize(a1.v[ph, :, sl], stc)[1])
            h = h.astype(BF16).astype(F32)
            for dx in (0, -1):
                if dx and not ph & 1:
                    continue
                moved = kshift_cols(h, dx)
                for _, dy, dx2, t in taps:
                    if dx2 == dx:
                        at = t * MID + c * 128
                        im.v[:, at : at + 128] = shift_rows(moved, dy).astype(BF16)
        for _, _, _, t in taps:
            im.put(t)
        if ph == 0:
            w.get()
        for _, _, _, t in taps:
            sl = slice(t * MID, (t + 1) * MID)
            part = dot(im.v[:, sl], w.v[sl, :])
            acc = part if acc is None else acc + part
    acc = acc * tiled(live, MID)
    a2.v[...] = acc
    a2.put()
    spread_rows(so[0], pack_sums(acc, acc * acc))


def run_conv_forward(n, cnt, s0, gb0, mask, a1, w):
    return flow_call(
        conv_forward, (cnt,), (s0, gb0, mask), [(a1, 4, 0), (w, 1, 0)],
        [((R, 9 * MID), BF16, 9, 1), ((R, MID), F32, 1, 0)], [like((n, 8, 128))],
    )


def joint_norm(s, m, ins, outs, so, extra):
    (cnt,), (s23, gb2, gb3, mask), (a3, ap, w2), (y1, yl, b1) = s, m, ins, outs
    live = tiled(mask[...], MID)
    got = s23[...]
    acc = None
    for c in range(4):
        sl = slice(c * MID, (c + 1) * MID)
        a3.get(c)
        ap.get(c)
        gbs = [b[:, sl] for b in (gb2, gb3)]
        _, u2 = normalize(a3.v[:, sl], stats_of(got[c], cnt[0], gbs[0]))
        _, u3 = normalize(ap.v[:, sl], stats_of(got[c], cnt[0], gbs[1], 8, 12))
        y = live * silu(u2 + u3)
        y1.v[:, sl] = y
        y1.put(c)
        low = y.astype(BF16)
        yl.v[:, sl] = low
        yl.put(c)
        w2.get(c)
        part = dot(low, w2.v[sl, :])
        acc = part if acc is None else acc + part
    b1.v[...] = acc
    b1.put()
    spread_rows(so[0], pack_sums(acc, acc * acc))


def run_joint_norm(n, cnt, s23, gb2, gb3, mask, a3, ap, w2):
    return flow_call(
        joint_norm, (cnt,), (s23, gb2, gb3, mask), [(a3, 4, 1), (ap, 4, 1), (w2, 4, 0)],
        [((R, C_OUT), F32, 4, 1), ((R, C_OUT), BF16, 4, 1), ((R, MID), F32, 1, 0)],
        [like((n, 8, 128))],
    )


def mix_forward(s, m, ins, outs, so, extra):
    (cnt,) = s
    s4, gb4, mask, wdown, wup, kern, scale, table, spread = m
    (b1, wmix), (z, zl, mixed, im) = ins, outs
    sig_ref, pooled_ref, wnext_ref, sums_ref = so
    live = mask[...]
    st = stats_of(total_of(s4), cnt[0], gb4[...])
    b1.get()
    for c in range(4):
        sl = slice(c * 128, (c + 1) * 128)
        v = live * silu(normalize(b1.v[:, sl], cols(st, c))[1])
        z.v[:, sl] = v
        zl.v[:, sl] = v.astype(BF16)
    z.put()
    zl.put()
    r = dot(zl.v[...], wdown[...])
    ws = exact_dot(table[...], r)
    wnext_ref[...] = ws[:144]
    pooled = -ws[144:160]
    for t in range(9):
        pooled = pooled + kern[t : t + 1, :] * ws[t * 16 : (t + 1) * 16]
    pooled = scale[...] * pooled
    pooled_ref[...] = pooled
    sig = jax.nn.sigmoid(jnp.dot(pooled, wup[...], precision=HIGHEST))
    sig_ref[...] = sig
    gates = jnp.concatenate(three(0.5 + sig), axis=0)
    prev = None
    sums = []
    for c in range(4):
        sl = slice(c * 128, (c + 1) * 128)
        v = z.v[:, sl] * dot(spread[...], gates[:, sl])
        if c > 0:
            low = ktime_shift(v + prev, False).astype(BF16).astype(F32)
            for dx in (-1, 0, 1):
                moved = kshift_cols(low, dx)
                for dy in (-1, 0, 1):
                    t = (dy + 1) * 3 + dx + 1
                    im.v[c - 1, :, t * 128 : (t + 1) * 128] = shift_rows(moved, dy).astype(BF16)
            im.put(c - 1)
            if c == 1:
                wmix.get()
            v = live * dot(im.v[c - 1], wmix.v[c - 1])
        prev = v
        mixed.v[:, sl] = v
        sums.append((jnp.sum(v, axis=0, keepdims=True), jnp.sum(v * v, axis=0, keepdims=True)))
    mixed.put()
    spread_rows(sums_ref, jnp.concatenate([q[0] for q in sums] + [q[1] for q in sums], axis=0))


def run_mix_forward(n, cnt, s4, gb4, mask, wdown, wup, kern, scale, table, spread, b1, wmix):
    return flow_call(
        mix_forward, (cnt,), (s4, gb4, mask, wdown, wup, kern, scale, table, spread),
        [(b1, 1, 0), (wmix, 1, 0)],
        [((R, MID), F32, 1, 0), ((R, MID), BF16, 1, 0), ((R, MID), F32, 1, 0),
         ((3, R, 9 * GROUP), BF16, 3, 0)],
        [like((16, MID)), like((16, SQUEEZE)), like((144, SQUEEZE)), like((n, 8, 128))],
    )


def expand_last(s, m, ins, outs, so, extra):
    (cnt,), (s5, gb5, mask), (mixed, we2), (w, b3), (rows,) = s, m, ins, outs, extra
    live = tiled(mask[...], MID)
    mixed.get()
    h = live * silu(normalize(mixed.v[...], stats_of(total_of(s5), cnt[0], gb5[...]))[1])
    w.v[...] = h.astype(BF16)
    w.put()
    for c in range(4):
        sl = slice(c * MID, (c + 1) * MID)
        we2.get(c)
        a = dot(w.v[...], we2.v[:, sl])
        b3.v[:, sl] = a
        b3.put(c)
        put_rows(rows, 4 * c, jnp.sum(a, axis=0, keepdims=True))
        put_rows(rows, 16 + 4 * c, jnp.sum(a * a, axis=0, keepdims=True))
    so[0][...] = rows[...]


def run_expand_last(cnt, s5, gb5, mask, mixed, we2):
    return plain_call(
        expand_last, (cnt,), (s5, gb5, mask), [(mixed, 1, 0), (we2, 4, 1)],
        [((R, MID), BF16, 1, 0), ((R, C_OUT), F32, 4, 1)], [like((32, 128))],
        [pltpu.VMEM((32, 128), F32)],
    )


def last_norm(s, m, ins, outs, so, extra):
    (cnt,), (s6, gb6, mask), (b3, y1, cc, cm, cf), (oc, om, of, g6) = s, m, ins, outs
    bc, bm, bf, rows = extra
    for b in (bc, bm, bf):
        b[...] = jnp.zeros_like(b)
    live = tiled(mask[...], MID)
    got = total_of(s6)
    for c in range(4):
        sl = slice(c * MID, (c + 1) * MID)
        for f in ins:
            f.get(c)
        for f in range(FRAMES):
            p = f % 2
            bc[f // 2, :, p * 4 : p * 4 + 4, :] = cc.v[f, :, :, sl].astype(F32)
        bm[:, :, 0:6, :] = cm.v[..., sl].astype(F32)
        bf[:, :, 0:7, :] = cf.v[..., sl].astype(F32)
        cot = join((bc[...], bm[...], bf[...]))
        x, u = normalize(b3.v[:, sl], wide_stats(got, cnt[0], gb6[...], c))
        u = u + y1.v[:, sl]
        sg = jax.nn.sigmoid(u)
        pc, pm, pf = split(live * u * sg)
        for f in range(FRAMES):
            p = f % 2
            oc.v[f, :, :, sl] = pc[f // 2, :, p * 4 : p * 4 + 4, :].astype(BF16)
        om.v[..., sl] = pm[:, :, 0:6, :].astype(BF16)
        of.v[..., sl] = pf[:, :, 0:7, :].astype(BF16)
        g = cot * live * (sg * (1.0 + u * (1.0 - sg)))
        g6.v[:, sl] = g
        for f in outs:
            f.put(c)
        put_rows(rows, 4 * c, jnp.sum(g * x, axis=0, keepdims=True))
        put_rows(rows, 16 + 4 * c, jnp.sum(g, axis=0, keepdims=True))
    so[0][...] = rows[...]


def run_last_norm(cnt, s6, gb6, mask, b3, y1, cots):
    return flow_call(
        last_norm, (cnt,), (s6, gb6, mask), [(b3, 4, 1), (y1, 4, 1)] + [(v, 4, 3) for v in cots],
        [((FRAMES, q, q, C_OUT), BF16, 4, 3) for q in SIDES] + [((R, C_OUT), F32, 4, 1)],
        [like((32, 128))],
        [pltpu.VMEM((2 if q == 4 else 4, q, 8, MID), F32) for q in SIDES]
        + [pltpu.VMEM((32, 128), F32)],
    )


def back_rows(tot, c=None):
    if c is None:
        return get_rows(tot, 0, MID), get_rows(tot, 4, MID)
    return get_rows(tot, 4 * c, MID), get_rows(tot, 16 + 4 * c, MID)


def last_back(s, m, ins, outs, so, extra):
    (cnt,), (t6, s6, gb6, mask, s5, gb5), (g6, b3, w, we2, mixed), (ge2, g5) = s, m, ins, outs
    live = tiled(mask[...], MID)
    tot, got = total_of(t6), total_of(s6)
    w.get()
    acc = None
    for c in range(4):
        sl = slice(c * MID, (c + 1) * MID)
        g6.get(c)
        b3.get(c)
        st = wide_stats(got, cnt[0], gb6[...], c)
        x, _ = normalize(b3.v[:, sl], st)
        d = norm_back(g6.v[:, sl], x, live, st, back_rows(tot, c), cnt[0]).astype(BF16)
        ge2.v[:, sl] = dot_tn(w.v[...], d).astype(BF16)
        ge2.put(c)
        we2.get(c)
        part = dot_nt(d, we2.v[:, sl])
        acc = part if acc is None else acc + part
    mixed.get()
    x, u = normalize(mixed.v[...], stats_of(total_of(s5), cnt[0], gb5[...]))
    g = acc * live * silu_grad(u)
    g5.v[...] = g
    g5.put()
    spread_rows(so[0], pack_sums(g * x, g))


def run_last_back(n, cnt, t6, s6, gb6, mask, s5, gb5, g6, b3, w, we2, mixed):
    return plain_call(
        last_back, (cnt,), (t6, s6, gb6, mask, s5, gb5),
        [(g6, 4, 1), (b3, 4, 1), (w, 1, 0), (we2, 4, 1), (mixed, 1, 0)],
        [((MID, C_OUT), BF16, 4, 1), ((R, MID), F32, 1, 0)], [like((n, 8, 128))],
    )


def mix_backward(s, m, ins, outs, so, extra):
    (cnt,) = s
    (t5, s5, gb5, mask, sig, pooled, wnext, wup, kern, scale, table_t, spread, wdown, s4, gb4) = m
    (g5, mixed, imt, wmix_t, z, zl, b1), (g4, gmix) = ins, outs
    gkern_ref, gdown_ref, gup_ref, sums_ref = so
    gim, gzg = extra
    live = mask[...]
    count = cnt[0]
    st = stats_of(total_of(s5), count, gb5[...])
    tot = back_rows(total_of(t5))
    g5.get()
    mixed.get()
    carried = None
    gsig = []
    for c in (3, 2, 1, 0):
        sl = slice(c * 128, (c + 1) * 128)
        stc = cols(st, c)
        x, _ = normalize(mixed.v[:, sl], stc)
        gm = norm_back(g5.v[:, sl], x, live, stc, cols(tot, c), count)
        if carried is not None:
            gm = gm + carried
        if c > 0:
            low = (live * gm).astype(BF16)
            imt.get(c - 1)
            gmix.v[c - 1] = dot_tn(imt.v[c - 1], low).astype(BF16)
            gmix.put(c - 1)
            low = low.astype(F32)
            for dx in (-1, 0, 1):
                moved = kshift_cols(low, -dx)
                for dy in (-1, 0, 1):
                    t = (dy + 1) * 3 + dx + 1
                    gim[:, t * 128 : (t + 1) * 128] = shift_rows(moved, -dy).astype(BF16)
            if c == 3:
                wmix_t.get()
                z.get()
            gm = ktime_shift(dot(gim[...], wmix_t.v[c - 1]), True)
            carried = gm
        gzg[:, sl] = gm
        gsig.insert(0, frame_sums(gm * z.v[:, sl]))
    sg = sig[...]
    ge = jnp.concatenate(gsig, axis=1) * sg * (1.0 - sg)
    gup_ref[...] = lax.dot_general(
        pooled[...], ge, (((0,), (0,)), ((), ())), precision=HIGHEST, preferred_element_type=F32
    )
    q = scale[...] * lax.dot_general(
        ge, wup[...], (((1,), (1,)), ((), ())), precision=HIGHEST, preferred_element_type=F32
    )
    coef = []
    gk = []
    for t in range(9):
        gk.append(jnp.sum(q * wnext[t * 16 : (t + 1) * 16], axis=0, keepdims=True))
        coef.append(kern[t : t + 1, :] * q)
    gk = jnp.concatenate(gk + [jnp.zeros((7, SQUEEZE), F32)], axis=0)
    gkern_ref[...] = jnp.concatenate([gk, jnp.zeros((16, 128 - SQUEEZE), F32)], axis=1)
    coef = jnp.concatenate(coef + [-q], axis=0)
    gr = exact_dot(table_t[...], coef).astype(BF16)
    zl.get()
    gdown_ref[...] = dot_tn(zl.v[...], gr)
    gates = jnp.concatenate(three(0.5 + sg), axis=0)
    st = stats_of(total_of(s4), count, gb4[...])
    b1.get()
    sums = []
    for c in range(4):
        sl = slice(c * 128, (c + 1) * 128)
        gz = gzg[:, sl] * dot(spread[...], gates[:, sl]) + dot_nt(gr, wdown[sl, :])
        x, u = normalize(b1.v[:, sl], cols(st, c))
        g = gz * live * silu_grad(u)
        g4.v[:, sl] = g
        sums.append((jnp.sum(g * x, axis=0, keepdims=True), jnp.sum(g, axis=0, keepdims=True)))
    g4.put()
    spread_rows(sums_ref, jnp.concatenate([v[0] for v in sums] + [v[1] for v in sums], axis=0))


def run_mix_backward(n, cnt, small, g5, mixed, im, wmix_t, z, zl, b1):
    return plain_call(
        mix_backward, (cnt,), small,
        [(g5, 1, 0), (mixed, 1, 0), (im, 3, 0), (wmix_t, 1, 0), (z, 1, 0), (zl, 1, 0), (b1, 1, 0)],
        [((R, MID), F32, 1, 0), ((3, 9 * GROUP, GROUP), BF16, 3, 0)],
        [like((16, 128)), like((MID, SQUEEZE)), like((SQUEEZE, MID)), like((n, 8, 128))],
        [pltpu.VMEM((R, 9 * GROUP), BF16), pltpu.VMEM((R, MID), F32)],
    )


def spatial_grad(s, m, ins, outs, so, extra):
    (cnt,), (t1, s1, gb1, mask), (g1, a2, im), (d1, gsp) = s, m, ins, outs
    live = tiled(mask[...], MID)
    st = stats_of(total_of(s1), cnt[0], gb1[...])
    g1.get()
    a2.get()
    x, _ = normalize(a2.v[...], st)
    d = norm_back(g1.v[...], x, live, st, back_rows(total_of(t1)), cnt[0]).astype(BF16)
    d1.v[...] = d
    d1.put()
    for t in range(9):
        sl = slice(t * MID, (t + 1) * MID)
        im.get(t)
        gsp.v[sl, :] = dot_tn(im.v[:, sl], d1.v[...]).astype(BF16)
        gsp.put(t)


def run_spatial_grad(cnt, small, g1, a2, im):
    return plain_call(
        spatial_grad, (cnt,), small, [(g1, 1, 0), (a2, 1, 0), (im, 9, 1)],
        [((R, MID), BF16, 1, 0), ((9 * MID, MID), BF16, 9, 0)],
    )


def conv_back(s, m, ins, outs, so, extra):
    (cnt,), (s0, gb0, mask), (d1, w, a1), (g0,), (moved_ref,) = s, m, ins, outs, extra
    live = mask[...]
    d1.get()
    for c in range(4):
        sl = slice(c * 128, (c + 1) * 128)
        d = d1.v[:, sl].astype(F32)
        for dx in (0, 1):
            moved = kshift_cols(d, dx)
            for dy in (0, 1):
                moved_ref[dy * 2 + dx, :, sl] = shift_rows(moved, dy).astype(BF16)
    st = stats_of(total_of(s0), 4.0 * cnt[0], gb0[...])
    w.get()
    total = jnp.zeros((8, 128), F32)
    for ph in range(4):
        gh = None
        for p, dy, dx, t in TAPS2:
            if p == ph:
                part = dot_nt(moved_ref[-dy * 2 - dx], w.v[t * MID : (t + 1) * MID, :])
                gh = part if gh is None else gh + part
        a1.get(ph)
        sums = []
        for c in range(4):
            sl = slice(c * 128, (c + 1) * 128)
            x, u = normalize(a1.v[ph, :, sl], cols(st, c))
            g = gh[:, sl] * live * silu_grad(u)
            g0.v[ph, :, sl] = g
            sums.append((jnp.sum(g * x, axis=0, keepdims=True), jnp.sum(g, axis=0, keepdims=True)))
        g0.put(ph)
        total = total + jnp.concatenate([v[0] for v in sums] + [v[1] for v in sums], axis=0)
    spread_rows(so[0], total)


def run_conv_back(n, cnt, small, d1, w, a1):
    return plain_call(
        conv_back, (cnt,), small, [(d1, 1, 0), (w, 1, 0), (a1, 4, 0)],
        [((4, R, MID), F32, 4, 0)], [like((n, 8, 128))], [pltpu.VMEM((4, R, MID), BF16)],
    )


def first_grads(s, m, ins, outs, so, extra):
    (cnt,), (t0, s0, gb0, mask), (g0, a1, x), (d0, gr1) = s, m, ins, outs
    live = mask[...]
    count = 4.0 * cnt[0]
    st = stats_of(total_of(s0), count, gb0[...])
    tot = back_rows(total_of(t0))
    acc = None
    for ph in range(4):
        g0.get(ph)
        a1.get(ph)
        for c in range(4):
            sl = slice(c * 128, (c + 1) * 128)
            stc = cols(st, c)
            xh, _ = normalize(a1.v[ph, :, sl], stc)
            d = norm_back(g0.v[ph, :, sl], xh, live, stc, cols(tot, c), count)
            d0.v[ph, :, sl] = d.astype(BF16)
        d0.put(ph)
        x.get(ph)
        part = dot_tn(x.v[ph], d0.v[ph])
        acc = part if acc is None else acc + part
    gr1.v[...] = acc.astype(BF16)
    gr1.put()


def run_first_grads(cnt, small, g0, a1, xph):
    return flow_call(
        first_grads, (cnt,), small, [(g0, 4, 0), (a1, 4, 0), (xph, 4, 0)],
        [((4, R, MID), BF16, 4, 0), ((xph.shape[-1], MID), BF16, 1, 0)], cost=LONG,
    )


def wide_grid(kernel, outs, out_specs, ins, in_specs, scratch=(), steps=4):
    return pl.pallas_call(
        kernel,
        grid=(steps,),
        out_shape=outs,
        in_specs=in_specs,
        out_specs=out_specs,
        scratch_shapes=list(scratch),
        compiler_params=LIMIT,
        cost_estimate=FREE,
    )(*ins)


def fixed(shape):
    return pl.BlockSpec(shape, lambda c: (0,) * len(shape))


def column(rows, lanes):
    return pl.BlockSpec((rows, lanes), lambda c: (0, c))


def row_block(rows, width):
    return pl.BlockSpec((rows, width), lambda c: (c, 0))


CHUNK = pl.BlockSpec((1, 16, 128), lambda c: (c, 0, 0))


def accumulate(ref, part):
    first = pl.program_id(0) == 0

    @pl.when(first)
    def _():
        ref[...] = part

    @pl.when(jnp.logical_not(first))
    def _():
        ref[...] = ref[...] + part


def expand_pair(cnt, a2, s1, gb1, mask, w, x, wsk, h_ref, a3_ref, ap_ref, s_ref):
    @pl.when(pl.program_id(0) == 0)
    def _():
        m = tiled(mask[...], MID)
        h = m * silu(normalize(a2[...], stats_of(total_of(s1), cnt[0], gb1[...]))[1])
        h_ref[...] = h.astype(BF16)

    a = dot(h_ref[...], w[...])
    a3_ref[...] = a
    b = dot(x[0], wsk[...])
    ap_ref[...] = b
    s_ref[0] = jnp.concatenate([pack_sums(a, a * a), pack_sums(b, b * b)], axis=0)


def run_expand_pair(cnt, s1, gb1, mask, a2, we1, xph, wsk):
    c_in = xph.shape[-1]
    wide = column(R, MID)
    return wide_grid(
        expand_pair,
        [like((R, MID), BF16), like((R, C_OUT)), like((R, C_OUT)), like((4, 16, 128))],
        [fixed((R, MID)), wide, wide, CHUNK],
        (cnt, a2, s1, gb1, mask, we1, xph, wsk),
        [SMEM, fixed((R, MID)), fixed(s1.shape), fixed((2, MID)), fixed((R, 128)),
         column(MID, MID), pl.BlockSpec((1, R, c_in), lambda c: (0, 0, 0)), column(c_in, MID)],
    )


def joint_back(cnt, t4, s4, gb4, s23, gb2, gb3, mask, gk, g4, b1, yl, w2, g6, a3, ap,
               gr2_ref, gj_ref, pj_ref, d4_ref):
    m = tiled(mask[...], MID)

    @pl.when(pl.program_id(0) == 0)
    def _():
        st = stats_of(total_of(s4), cnt[0], gb4[...])
        x, _ = normalize(b1[...], st)
        d4_ref[...] = norm_back(g4[...], x, m, st, back_rows(total_of(t4)), cnt[0]).astype(BF16)

    d = d4_ref[...]
    gr2_ref[...] = dot_tn(yl[...], d).astype(BF16)
    gy = g6[...] + dot_nt(d, w2[...])
    got = s23[0]
    x2, u2 = normalize(a3[...], stats_of(got, cnt[0], gb2[...]))
    x3, u3 = normalize(ap[...], stats_of(got, cnt[0], gb3[...], 8, 12))
    g = gy * m * silu_grad(u2 + u3)
    gj_ref[...] = g
    pj_ref[0] = jnp.concatenate(
        [pack_sums(g * x2, g * x3), pack_sums(g, g)[:4], gk[0]], axis=0
    )


def run_joint_back(cnt, small, g4, b1, yl, w2, g6, a3, ap):
    t4, s4, gb4, s23, gb2, gb3, mask, gk = small
    wide, pair = column(R, MID), column(2, MID)
    one = fixed((R, MID))
    return wide_grid(
        joint_back,
        [like((C_OUT, MID), BF16), like((R, C_OUT)), like((4, 16, 128))],
        [row_block(MID, MID), wide, CHUNK],
        (cnt, t4, s4, gb4, s23, gb2, gb3, mask, gk.reshape(4, 4, 128), g4, b1, yl, w2, g6, a3, ap),
        [SMEM, fixed(t4.shape), fixed(s4.shape), fixed((2, MID)), CHUNK, pair, pair,
         fixed((R, 128)), pl.BlockSpec((1, 4, 128), lambda c: (c, 0, 0)), one, one, wide,
         row_block(MID, MID), wide, wide, wide],
        [pltpu.VMEM((R, MID), BF16)],
    )


def expand_back(cnt, tj, s23, gb2, gb3, mask, s1, gb1, gj, a3, ap, h2, x0, we1, a2,
                ge1_ref, gsk_ref, d3_ref, g1_ref, p1_ref):
    m = tiled(mask[...], MID)
    g = gj[...]
    tot, got = tj[0], s23[0]
    sum2, sum3, sumg = (get_rows(tot, 4 * k, MID) for k in range(3))
    st = stats_of(got, cnt[0], gb2[...])
    x, _ = normalize(a3[...], st)
    d = norm_back(g, x, m, st, (sum2, sumg), cnt[0]).astype(BF16)
    ge1_ref[...] = dot_tn(h2[...], d).astype(BF16)
    accumulate(g1_ref, dot_nt(d, we1[...]))
    st = stats_of(got, cnt[0], gb3[...], 8, 12)
    x, _ = normalize(ap[...], st)
    d = norm_back(g, x, m, st, (sum3, sumg), cnt[0]).astype(BF16)
    d3_ref[...] = d
    gsk_ref[...] = dot_tn(x0[0], d).astype(BF16)

    @pl.when(pl.program_id(0) == pl.num_programs(0) - 1)
    def _():
        x1, u1 = normalize(a2[...], stats_of(total_of(s1), cnt[0], gb1[...]))
        v = g1_ref[...] * m * silu_grad(u1)
        g1_ref[...] = v
        spread_rows(p1_ref, pack_sums(v * x1, v))


def run_expand_back(n, cnt, small, gj, a3, ap, h2, xph, we1, a2):
    tj, s23, gb2, gb3, mask, s1, gb1 = small
    wide, pair = column(R, MID), column(2, MID)
    one = fixed((R, MID))
    c_in = xph.shape[-1]
    return wide_grid(
        expand_back,
        [like((MID, C_OUT), BF16), like((c_in, C_OUT), BF16), like((R, C_OUT), BF16),
         like((R, MID)), like((n, 8, 128))],
        [column(MID, MID), column(c_in, MID), wide, one, fixed((n, 8, 128))],
        (cnt, tj, s23, gb2, gb3, mask, s1, gb1, gj, a3, ap, h2, xph, we1, a2),
        [SMEM, CHUNK, CHUNK, pair, pair, fixed((R, 128)), fixed(s1.shape), fixed((2, MID)),
         wide, wide, wide, one, pl.BlockSpec((1, R, c_in), lambda c: (0, 0, 0)),
         column(MID, MID), one],
    )


def input_grads(mask, tc, tm, tf, d0, d3, w1, wsk, oc, om, of):
    lanes = oc.shape[-1]
    m = tiled(mask[...], lanes)
    groups = []
    for ph in range(4):
        v = dot_nt(d0[ph], w1[...])
        if ph == 0:
            v = v + dot_nt(d3[...], wsk[...])
        groups.append(m * v)
    for g, (out, table) in enumerate(((oc, tc), (om, tm), (of, tf))):
        pairs = 2 if g == 0 else 1
        side = 2 * SIDES[g]
        step = ROWS[g] // (FRAMES // pairs)
        for f in range(0, FRAMES, pairs):
            at = CUTS[g] + (f // pairs) * step
            rows = jnp.concatenate([v[at : at + step] for v in groups], axis=0).astype(BF16)
            y = dot(table[...], rows).reshape(pairs, side, 16, lanes)
            for p in range(pairs):
                out[f + p] = y[p, :, 0:side, :].astype(BF16)


def run_input_grads(mask, tables, d0, d3, w1, wsk):
    lanes = 256
    c_in = w1.shape[0]
    return wide_grid(
        input_grads,
        [like((FRAMES, 2 * q, 2 * q, c_in), BF16) for q in SIDES],
        clip_blocks(lanes),
        (mask, *tables, d0, d3, w1, wsk),
        [fixed((R, 128))] + [fixed(t.shape) for t in tables]
        + [fixed(d0.shape), fixed(d3.shape), row_block(lanes, MID), row_block(lanes, C_OUT)],
        steps=c_in // lanes,
    )


def tie(*arrays):
    return lax.optimization_barrier(arrays)


def axes_bits(n, fsdp):
    bits = n.bit_length() - 1
    core = fsdp.bit_length() - 1
    return list(range(core)), core, core + 1, list(range(core + 2, bits))


def swap(v, d, n):
    return lax.ppermute(v, AXES, [(i, i ^ d) for i in range(n)])


def exchange(spread):
    return lax.all_to_all(spread, AXES, 0, 0, tiled=True)


def exchange_wide(rows, n, fsdp):
    core = axes_bits(n, fsdp)[1]
    half = rows.shape[0] // 2
    mine = ((lax.axis_index(AXES) >> core) & 1) == 0
    low, high = rows[:half], rows[half:]
    part = jnp.where(mine, low, high) + swap(jnp.where(mine, high, low), 1 << core, n)
    groups = [[i for i in range(n) if (i >> core) & 1 == k] for k in range(2)]
    got = lax.all_to_all(
        jnp.broadcast_to(part[None], (n // 2,) + part.shape), AXES, 0, 0,
        axis_index_groups=groups, tiled=True,
    )
    part = jnp.sum(got, axis=0)
    other = swap(part, 1 << core, n)
    return jnp.where(
        mine, jnp.concatenate([part, other], axis=0), jnp.concatenate([other, part], axis=0)
    )


def allsum_wide(rows, n, fsdp, beside=()):
    near, core, mid, far = axes_bits(n, fsdp)
    bits = near + [mid] + far
    for r in [[core]] + [bits[i : i + 2] for i in range(0, len(bits), 2)]:
        got = [
            swap(rows, sum(1 << b for j, b in enumerate(r) if m >> j & 1), n)
            for m in range(1, 1 << len(r))
        ]
        rows = sum(got, rows)
        if r == [core]:
            rows, *beside = tie(rows, *beside)
    return (rows, *beside) if beside else rows


def rows16(v):
    return jnp.pad(v, ((0, 0),) * (v.ndim - 2) + ((0, -v.shape[-2] % 16), (0, 0)))


def place_blocks(n, orders, core, heights, width):
    part = width // len(orders)

    def kernel(me_ref, *refs):
        srcs = refs[: 2 * len(orders)]
        outs = refs[2 * len(orders) : -1]
        sem = refs[-1]
        me = me_ref[0]
        for rel in range(n):
            for k, order in enumerate(orders):
                at = sum((rel >> b & 1) << j for j, b in enumerate(order))
                src = srcs[2 * k + (rel >> core & 1)]
                row = 0
                for i, (h, out) in enumerate(zip(heights, outs)):
                    pltpu.make_async_copy(
                        src.at[at, pl.ds(row, h)],
                        out.at[me ^ rel, :, pl.ds(k * part, part)],
                        sem.at[i],
                    ).start()
                    row += h
        for i, out in enumerate(outs):
            pltpu.make_async_copy(out, out, sem.at[i]).wait()

    return pl.pallas_call(
        kernel,
        out_shape=[jax.ShapeDtypeStruct((n, h, width), BF16) for h in heights],
        in_specs=[SMEM] + [pl.BlockSpec(memory_space=pl.ANY)] * (2 * len(orders)),
        out_specs=[VMEM] * len(heights),
        scratch_shapes=[pltpu.SemaphoreType.DMA((len(heights),))],
        compiler_params=LIMIT,
        cost_estimate=FREE,
    )


class Gather:
    def __init__(self, shards, n, fsdp):
        self.n = n
        self.near, self.core, self.mid, self.far = axes_bits(n, fsdp)
        self.shards = shards
        padded = [rows16(v.astype(BF16)) for v in shards]
        self.heights = [v.shape[0] for v in padded]
        self.x = jnp.concatenate(padded, axis=0) if len(padded) > 1 else padded[0]

    def first(self):
        got = []
        for m in range(1, 1 << len(self.far)):
            got.append(swap(self.x, sum(1 << b for j, b in enumerate(self.far) if m >> j & 1), self.n))
        self.hops = [self.x] + got

    def second(self):
        n = self.n
        bits = self.near + [self.mid]
        v = jnp.stack(self.hops)
        got = [v]
        for m in range(1, 1 << len(bits)):
            got.append(swap(v, sum(1 << b for j, b in enumerate(bits) if m >> j & 1), n))
        self.planes = [jnp.concatenate(got, axis=0)]
        self.orders = [self.far + bits]

    def split(self):
        width = self.x.shape[1]
        bits = self.near + [self.mid]
        self.paths = [bits, bits[::-1]]
        self.orders = [self.far + path for path in self.paths]
        v = jnp.stack(self.hops)
        self.planes = [v[..., : width // 2], v[..., width // 2 :]]

    def hop(self, k):
        self.got = [swap(v, 1 << p[k], self.n) for v, p in zip(self.planes, self.paths)]

    def land(self):
        self.planes = [jnp.concatenate([v, g], axis=0) for v, g in zip(self.planes, self.got)]

    def third(self):
        self.other = [swap(v, 1 << self.core, self.n) for v in self.planes]

    def finish(self, me):
        width = self.x.shape[1]
        planes = [v for pair in zip(self.planes, self.other) for v in pair]
        outs = place_blocks(self.n, self.orders, self.core, self.heights, width)(me, *planes)
        return [
            o.reshape(self.n * h, width)
            if h == v.shape[0]
            else o[:, : v.shape[0]].reshape(-1, width)
            for o, h, v in zip(outs, self.heights, self.shards)
        ]


def order_blocks(n, orders, pieces, width, arrays):
    heights = [arrays[i].shape[1] for i, _ in pieces]
    total = sum(heights)
    half = width // 2

    def kernel(me_ref, *refs):
        srcs = refs[: len(arrays)]
        outs = refs[len(arrays) : len(arrays) + 2]
        sem = refs[-1]
        me = me_ref[0]
        for rel in range(n):
            for k, order in enumerate(orders):
                at = 0
                for b in order:
                    at = at * 2 + (rel >> b & 1)
                side = at * 2 // n
                row = 0
                for (i, col), h in zip(pieces, heights):
                    pltpu.make_async_copy(
                        srcs[i].at[me ^ rel, :, pl.ds(col + k * half, half)],
                        outs[side].at[k, at % (n // 2), pl.ds(row, h)],
                        sem.at[side],
                    ).start()
                    row += h
        for k, out in enumerate(outs):
            pltpu.make_async_copy(out, out, sem.at[k]).wait()

    return pl.pallas_call(
        kernel,
        out_shape=[jax.ShapeDtypeStruct((2, n // 2, total, half), BF16)] * 2,
        in_specs=[SMEM] + [pl.BlockSpec(memory_space=pl.ANY)] * len(arrays),
        out_specs=[VMEM] * 2,
        scratch_shapes=[pltpu.SemaphoreType.DMA((2,))],
        compiler_params=LIMIT,
        cost_estimate=FREE,
    )


def add_blocks(keep, got, joined):
    m, rows, half = keep[0].shape[-3:]
    k_in = len(keep)

    if m == 1:
        outs = [like((rows, 2 * half))]
    elif joined:
        outs = [like((2, m // 2, rows, half), BF16)] * 2
    else:
        outs = [like((m // 2, rows, half), BF16)] * 4
    given = [*keep, *got]

    def kernel(*refs):
        k = 2 * k_in
        far_in, far_out = refs[:k], refs[k : k + len(outs)]
        ins, near_out = refs[k + len(outs) : 2 * k + len(outs)], refs[2 * k + len(outs) : -1]
        sem = refs[-1]
        moves = [
            pltpu.make_async_copy(f, v, sem.at[i]) for i, (f, v) in enumerate(zip(far_in, ins))
        ]
        for c in moves:
            c.start()
        for c in moves:
            c.wait()

        def total(k, i):
            if k_in == 1:
                return ins[0][k, i].astype(F32) + ins[1][k, i].astype(F32)
            return ins[k][i].astype(F32) + ins[2 + k][i].astype(F32)

        if m == 1:
            for k in range(2):
                near_out[0][:, k * half : (k + 1) * half] = total(k, 0)
        else:

            @pl.loop(0, m // 2)
            def _(i):
                for k in range(2):
                    for side in range(2):
                        v = total(k, i + side * (m // 2)).astype(BF16)
                        if joined:
                            near_out[side][k, i] = v
                        else:
                            near_out[2 * side + k][i] = v

        moves = [
            pltpu.make_async_copy(v, f, sem.at[2 * k_in + i])
            for i, (f, v) in enumerate(zip(far_out, near_out))
        ]
        for c in moves:
            c.start()
        for c in moves:
            c.wait()

    any_space = pl.BlockSpec(memory_space=pl.ANY)
    need = 2 * sum(v.size * v.dtype.itemsize for v in given) + 4 * 2**20
    return pl.pallas_call(
        kernel,
        out_shape=outs,
        in_specs=[any_space] * len(given),
        out_specs=[any_space] * len(outs),
        scratch_shapes=[pltpu.VMEM(v.shape, v.dtype) for v in given + outs]
        + [pltpu.SemaphoreType.DMA((len(given) + len(outs),))],
        compiler_params=pltpu.CompilerParams(vmem_limit_bytes=min(need, 56 * 2**20)),
        cost_estimate=FREE,
    )(*given)


class Scatter:
    def __init__(self, me, arrays, pieces, width, n, fsdp):
        self.n = n
        near, core, mid, self.far = axes_bits(n, fsdp)
        bits = near + [mid]
        self.paths = [bits, bits[::-1]]
        self.heights = [arrays[i].shape[1] for i, _ in pieces]
        orders = [[core] + path + self.far for path in self.paths]
        send, keep = order_blocks(n, orders, pieces, width, arrays)(me, *arrays)[::-1]
        self.send, self.keep = [send], [keep]
        self.hops = [[core]] + list(zip(*self.paths)) + [[b] for b in self.far]
        self.at = 0

    def start(self):
        self.got = [swap(v, 1 << b, self.n) for v, b in zip(self.send, self.hops[self.at])]
        self.at += 1

    def add(self):
        after = self.hops[self.at : self.at + 1]
        got = add_blocks(self.keep, self.got, bool(after) and len(after[0]) == 1)
        if not after:
            self.total = got[0]
        else:
            k = len(got) // 2
            self.keep, self.send = got[:k], got[k:]

    def end(self, x):
        x, *self.got = tie(x, *self.got)
        return x

    def ready(self, x):
        x, *self.send = tie(x, *self.send)
        self.start()
        return x

    def rest(self):
        self.add()
        while self.at < len(self.hops):
            self.start()
            self.add()
        out = []
        at = 0
        for h in self.heights:
            out.append(self.total[at : at + h])
            at += h
        return out


def body(n, fsdp, *args):
    (coarse, medium, fine, clip_counts, frame_counts, reduce_one, spatial_one, expand_one,
     shortcut_one, reduce_two, excite_down, excite_up, temporal_mix, expand_two, norm_params,
     motion_kernel, cot_c, cot_m, cot_f) = args
    near, core, mid, far = axes_bits(n, fsdp)

    def gather(w):
        return lax.all_gather(w.astype(BF16), AXES, axis=0, tiled=True)

    def flat(w):
        v = w.reshape(-1)
        return jnp.pad(v, (0, -v.size % MID)).reshape(-1, MID)

    def flat_back(got, w):
        return got.reshape(n, -1)[:, : w.size].reshape((n,) + w.shape)

    alive = (jnp.arange(4)[None, :] < frame_counts[0][:, None]) & (clip_counts[0][:, None] > 0)
    alive = alive.astype(F32)
    later = jnp.pad(alive[:, 1:], ((0, 0), (0, 1)))
    alive_slots = alive.reshape(12)
    later_slots = later.reshape(12)
    mask = (jnp.asarray(SPREAD) @ alive_slots)[:, None]
    per_group = jnp.sum(alive, axis=1)
    tables = [jnp.asarray(t, BF16) for t in PHASES]
    tables_t = [jnp.asarray(t.T, BF16) for t in PHASES]
    clips = [coarse, medium, fine]

    m128 = jnp.broadcast_to(mask, (R, 128))
    scale = later_slots / jnp.asarray(NPIX)
    scale = jnp.broadcast_to(jnp.pad(scale, (0, 4))[:, None], (16, SQUEEZE))
    table = jnp.asarray(TABLE, BF16)
    table_t = jnp.asarray(TABLE.T, BF16)
    spread = jnp.asarray(SPREAD3, BF16)
    me = lax.axis_index(AXES).astype(jnp.int32).reshape(1)
    small = jnp.concatenate([flat(norm_params), jnp.pad(per_group, (0, MID - 3))[None]], axis=0)
    ga = Gather([reduce_one, small], n, fsdp)
    gb_ = Gather([spatial_one], n, fsdp)
    gc_ = Gather([shortcut_one, expand_one], n, fsdp)
    narrow = [reduce_two, flat(excite_down), flat(excite_up), flat(temporal_mix)]
    rows = [v.shape[0] for v in narrow]
    narrow = jnp.concatenate(narrow, axis=0)
    got = gather(jnp.pad(narrow, ((0, -narrow.shape[0] % 16), (0, 0))))
    we2 = gather(expand_two)
    ga.first()
    *ga.hops, gb_.x, clips[0], clips[1], clips[2] = tie(*ga.hops, gb_.x, *clips)
    ga.second()
    gb_.first()
    xph = run_split(alive_slots, clips, tables)
    ga.planes[0], xph = tie(ga.planes[0], xph)
    ga.third()
    w1, norms = ga.finish(me)
    norms = norms.reshape(n, -1, MID)
    counts = jnp.sum(norms[:, -1, :3].astype(F32), axis=0)
    cnt = jnp.sum(counts * np.array([q * q for q in SIDES], np.float32)).reshape(1)
    norms = flat_back(norms[:, :-1], norm_params).transpose(1, 0, 2).reshape(2, -1).astype(F32)
    edges = [0, 512, 1024, 3072, 5120, 5632, 6144, 8192]
    gb = [norms[:, edges[k] : edges[k + 1]] for k in range(7)]

    w1, gc_.x, *gb_.hops = tie(w1, gc_.x, *gb_.hops)
    gb_.split()
    w1, *gb_.planes = tie(w1, *gb_.planes)
    gb_.hop(0)
    gc_.first()
    a1, p0 = run_enter(n, xph, w1)
    for k in range(1, len(gb_.paths[0])):
        p0, *gb_.got = tie(p0, *gb_.got)
        gb_.land()
        p0, *gb_.planes = tie(p0, *gb_.planes)
        gb_.hop(k)
    s0 = exchange(p0)
    s0, *rest = tie(s0, *gb_.got, *gc_.hops)
    gb_.got, gc_.hops = rest[:2], rest[2:]
    gb_.land()
    gb_.third()
    gc_.split()
    gc_.hop(0)
    wsp, = gb_.finish(me)
    for k in range(1, len(gc_.paths[0])):
        wsp, *gc_.got = tie(wsp, *gc_.got)
        gc_.land()
        wsp, *gc_.planes = tie(wsp, *gc_.planes)
        gc_.hop(k)
    im, a2, p1 = run_conv_forward(n, cnt, s0, gb[0], m128, a1, wsp)
    s1 = exchange(p1)
    s1, *gc_.got = tie(s1, *gc_.got)
    gc_.land()
    gc_.third()
    wsk, we1 = gc_.finish(me)
    h2, a3, ap, p2 = run_expand_pair(cnt, s1, gb[1], m128, a2, we1, xph, wsk)
    s23, got = allsum_wide(p2, n, fsdp, (got,))
    got = got.reshape(n, -1, MID)
    w2 = got[:, : rows[0]].reshape(C_OUT, MID)
    at = rows[0]
    wdown = flat_back(got[:, at : at + rows[1]], excite_down).reshape(MID, SQUEEZE)
    at += rows[1]
    wup = flat_back(got[:, at : at + rows[2]], excite_up)
    wup = wup.transpose(1, 0, 2).reshape(SQUEEZE, MID).astype(F32)
    at += rows[2]
    wmix = flat_back(got[:, at : at + rows[3]], temporal_mix)
    wmix = wmix.transpose(1, 0, 2).reshape(3, 9 * GROUP, GROUP)
    wmix_t = wmix.reshape(3, 9, GROUP, GROUP).transpose(0, 1, 3, 2).reshape(3, 9 * GROUP, GROUP)
    y1, y1_low, b1, p4 = run_joint_norm(n, cnt, s23, gb[2], gb[3], m128, a3, ap, w2)
    s4 = exchange(p4)
    z, z_low, mixed, mix_im, sig, pooled, wnext, p5 = run_mix_forward(
        n, cnt, s4, gb[4], m128, wdown, wup, motion_kernel, scale, table, spread, b1, wmix
    )
    s5 = exchange(p5)
    w, b3, p6 = run_expand_last(cnt, s5, gb[5], m128, mixed, we2)
    s6 = exchange_wide(p6, n, fsdp)
    o_c, o_m, o_f, g6, p6 = run_last_norm(cnt, s6, gb[6], m128, b3, y1, (cot_c, cot_m, cot_f))

    t6 = exchange_wide(p6, n, fsdp)
    ge2, g5, p5 = run_last_back(n, cnt, t6, s6, gb[6], m128, s5, gb[5], g6, b3, w, we2, mixed)
    t5 = exchange(p5)
    g4, gmix, gkernel, gdown, gup, p4 = run_mix_backward(
        n, cnt,
        (t5, s5, gb[5], m128, sig, pooled, wnext, wup, motion_kernel, scale, table_t, spread,
         wdown, s4, gb[4]),
        g5, mixed, mix_im, wmix_t, z, z_low, b1,
    )
    t4 = exchange(p4)
    gr2, gj, pj = run_joint_back(
        cnt, (t4, s4, gb[4], s23, gb[2], gb[3], m128, gkernel), g4, b1, y1_low, w2, g6, a3, ap
    )

    gmix = gmix.reshape(27, n, GROUP * GROUP // n).transpose(1, 0, 2).reshape(n, -1)
    gup = gup.reshape(SQUEEZE, n, MID // n).transpose(1, 0, 2).reshape(n, -1)
    thin = jnp.concatenate([gmix, gdown.reshape(n, -1).astype(BF16), gup.astype(BF16)], axis=1)
    thin = jnp.pad(thin, ((0, 0), (0, -thin.shape[1] % (16 * MID)))).reshape(n, -1, MID)

    def blocks(v):
        return rows16(v.reshape(n, -1, v.shape[-1]))

    starts = list(range(0, C_OUT, MID))
    tj, gr2, ge2, thin = allsum_wide(pj, n, fsdp, (gr2, ge2, thin))
    ra = Scatter(
        me, [blocks(gr2), thin, blocks(ge2)], [(0, 0), (1, 0)] + [(2, c) for c in starts], MID,
        n, fsdp,
    )
    ra.start()
    ra.add()
    tj = ra.ready(tj)
    ge1, gsk, d3, g1, p1 = run_expand_back(
        n, cnt, (tj, s23, gb[2], gb[3], m128, s1, gb[1]), gj, a3, ap, h2, xph, we1, a2
    )
    p1 = ra.end(p1)
    p1, ge1, gsk = tie(p1, ge1, gsk)
    t1 = exchange(p1)
    ra.add()
    rb = Scatter(
        me, [blocks(ge1), blocks(gsk)], [(i, c) for i in range(2) for c in starts], MID, n, fsdp
    )
    t1 = rb.ready(ra.ready(t1))
    d1, gsp = run_spatial_grad(cnt, (t1, s1, gb[1], m128), g1, a2, im)
    d1 = rb.end(ra.end(d1))
    rb.add()
    d1 = rb.ready(d1)
    gsp, d1 = tie(gsp, d1)
    rc = Scatter(me, [blocks(gsp)], [(0, 0)], MID, n, fsdp)
    d1 = rc.ready(d1)
    ra.add()
    d1 = ra.ready(d1)
    g0, p0 = run_conv_back(n, cnt, (s0, gb[0], m128), d1, wsp, a1)
    p0 = rc.end(rb.end(ra.end(p0)))
    t0 = exchange(p0)
    rc.add()
    rb.add()
    ra.add()
    t0 = rb.ready(rc.ready(t0))
    d0, gr1 = run_first_grads(cnt, (t0, s0, gb[0], m128), g0, a1, xph)
    gr1 = blocks(gr1)
    gr1 = gr1.reshape(n // (2 * fsdp), 2, fsdp, -1, MID)
    side = (me[0] >> core) & 1
    kept = lax.dynamic_index_in_dim(gr1, side, 1, keepdims=False)
    sent = lax.dynamic_index_in_dim(gr1, 1 - side, 1, keepdims=False)
    gr1 = (kept.astype(F32) + swap(sent, 1 << core, n).astype(F32)).astype(BF16)
    groups = [[i for i in range(n) if (i >> core) & 1 == k] for k in range(2)]
    got = lax.all_to_all(
        gr1.reshape(n // 2, -1, MID), AXES, 0, 0, axis_index_groups=groups, tiled=True
    )
    gin = list(run_input_grads(m128, tables_t, d0, d3, w1, wsk))
    gin[0] = rc.end(rb.end(gin[0]))
    gin[0], got, *rest = tie(gin[0], got, *rb.got, *rc.got)
    rb.got, rc.got = rest[:2], rest[2:]
    rc.add()
    rb.add()
    gin[0] = ra.ready(rb.ready(rc.ready(gin[0])))
    *rc.got, t0, t1, t4, t5, t6, tj = tie(*rc.got, t0, t1, t4, t5, t6, tj)
    rc.add()
    rc.start()
    rb.add()
    rb.start()
    *rc.got, o_m, o_f, got = tie(*rc.got, o_m, o_f, got)
    gr1 = jnp.sum(got.astype(F32), axis=0)[: reduce_one.shape[0]]
    second = ra.rest()
    gsp = rc.rest()[0][: spatial_one.shape[0]]
    first = rb.rest()

    def wide_back(parts, like_):
        return jnp.concatenate([p[: like_.shape[0]] for p in parts], axis=1)

    thin = second[1].reshape(-1)
    s1_ = temporal_mix.size
    s2_ = s1_ + excite_down.size
    s3_ = s2_ + excite_up.size

    def split_rows(t, k):
        t = jnp.sum(t, axis=0) if t.ndim == 3 else t
        return t.reshape(k, -1)

    t0, t1, t4, t5 = (split_rows(t, 2) for t in (t0, t1, t4, t5))
    t6 = split_rows(t6, 2)
    gkernel = tj[:, 12:].reshape(16, 128)[:9, :SQUEEZE]
    tj = jnp.stack([tj[:, 4 * k : 4 * k + 4].reshape(-1) for k in range(3)])
    gain = jnp.concatenate([t0[0], t1[0], tj[0], tj[1], t4[0], t5[0], t6[0]])
    bias = jnp.concatenate([t0[1], t1[1], tj[2], tj[2], t4[1], t5[1], t6[1]])
    gnorm = lax.dynamic_slice_in_dim(jnp.stack([gain, bias]), me[0] * (8192 // n), 8192 // n, 1)
    return (
        o_c, o_m, o_f, gin[0], gin[1], gin[2],
        gr1,
        gsp,
        wide_back(first[:4], expand_one),
        wide_back(first[4:], shortcut_one),
        second[0][: reduce_two.shape[0]],
        thin[s1_:s2_].reshape(excite_down.shape),
        thin[s2_:s3_].reshape(excite_up.shape),
        thin[:s1_].reshape(temporal_mix.shape),
        wide_back(second[2:], expand_two),
        gnorm,
        gkernel,
    )


def solution(mesh):
    n = mesh.shape["dp"] * mesh.shape["fsdp"]
    rows = P(AXES, None)
    cols = P(None, AXES)
    image = P(AXES, None, None, None)
    return jax.shard_map(
        partial(body, n, mesh.shape["fsdp"]),
        mesh=mesh,
        in_specs=(image, image, image, rows, rows, rows, rows, rows, rows, rows, rows, cols, cols,
                  rows, cols, P(), image, image, image),
        out_specs=(image, image, image, image, image, image, rows, rows, rows, rows, rows, rows,
                   cols, cols, rows, cols, P()),
        check_vma=False,
    )
```

```python
from functools import partial

import jax
import jax.numpy as jnp
from jax import lax
from jax.experimental import pallas as pl
from jax.experimental.pallas import tpu as pltpu
from jax.sharding import PartitionSpec as P
import numpy as np

MID = 512
C_OUT = 2048
FRAMES = 4
GROUP = 128
SHIFT = 16
SQUEEZE = 32
SIDES = (4, 6, 7)
AXES = ("dp", "fsdp")
EPS = 1e-05
HIGHEST = lax.Precision.HIGHEST
F32 = jnp.float32
BF16 = jnp.bfloat16

ROWS = (64, 192, 224)
CUTS = (0, 64, 256, 480)
R = 480


def row_tables():
    frame = np.zeros(R, np.int32)
    row = np.zeros(R, np.int32)
    col = np.zeros(R, np.int32)
    group = np.zeros(R, np.int32)
    at = 0
    for a in range(2):
        for i in range(4):
            for p in range(2):
                for j in range(4):
                    frame[at], row[at], col[at], group[at] = 2 * a + p, i, j, 0
                    at += 1
    for g in (1, 2):
        for f in range(4):
            for i in range(SIDES[g]):
                for j in range(8):
                    frame[at], row[at], col[at], group[at] = f, i, j, g
                    at += 1
    side = np.array(SIDES)[group]
    return group, frame, row, col, (col < side), side


GROUP_OF, FRAME_OF, ROW_OF, COL_OF, VALID, SIDE_OF = row_tables()
SLOT_OF = GROUP_OF * FRAMES + FRAME_OF


def window_table():
    table = np.zeros((12, 9, R), np.float32)
    for r in range(R):
        if not VALID[r]:
            continue
        for t in range(9):
            dy, dx = t // 3 - 1, t % 3 - 1
            i, j = ROW_OF[r] - dy, COL_OF[r] - dx
            if 0 <= i < SIDE_OF[r] and 0 <= j < SIDE_OF[r]:
                table[SLOT_OF[r], t, r] = 1.0
    return table.reshape(108, R)


WINDOWS = window_table()
SPREAD = ((SLOT_OF[:, None] == np.arange(12)[None]) & VALID[:, None]).astype(np.float32)
NPIX = np.repeat(np.array([s * s for s in SIDES], np.float32), FRAMES)


def split(v):
    c = v.shape[-1]
    return (
        v[0:64].reshape(2, 4, 8, c),
        v[64:256].reshape(4, 6, 8, c),
        v[256:480].reshape(4, 7, 8, c),
    )


def join(parts):
    return jnp.concatenate([p.reshape(-1, p.shape[-1]) for p in parts], axis=0)


def shift_rows(v, dy):
    if dy == 0:
        return v
    out = []
    for p in split(v):
        zero = jnp.zeros_like(p[:, :1])
        out.append(
            jnp.concatenate([p[:, 1:], zero] if dy > 0 else [zero, p[:, :-1]], axis=1)
        )
    return join(out)


def dot(a, b):
    return jnp.dot(a, b, preferred_element_type=F32)


def dot_nt(a, b):
    return lax.dot_general(a, b, (((1,), (1,)), ((), ())), preferred_element_type=F32)


def dot_tn(a, b):
    return lax.dot_general(a, b, (((0,), (0,)), ((), ())), preferred_element_type=F32)


def normalize(a, st):
    mean, rstd, gain, bias = st
    xhat = (a - mean) * rstd
    return xhat, xhat * gain + bias


def silu(u):
    return u * jax.nn.sigmoid(u)


def silu_grad(u):
    s = jax.nn.sigmoid(u)
    return s * (1.0 + u * (1.0 - s))


def norm_back(g, xhat, mask, st, tot, count):
    mean, rstd, gain, bias = st
    return gain * rstd * (g - mask * (tot[1] + xhat * tot[0]) / count)


TAPS2 = []
for kh in range(3):
    for kw in range(3):
        pr, dy = (1, -1) if kh == 0 else ((0, 0) if kh == 1 else (1, 0))
        pc, dx = (1, -1) if kw == 0 else ((0, 0) if kw == 1 else (1, 0))
        TAPS2.append((pr * 2 + pc, dy, dx, kh * 3 + kw))


FREE = pl.CostEstimate(flops=0, bytes_accessed=0, transcendentals=0)
LONG = pl.CostEstimate(flops=20 * 10**9, bytes_accessed=60 * 10**6, transcendentals=0)
VMEM = pl.BlockSpec(memory_space=pltpu.VMEM)
SMEM = pl.BlockSpec(memory_space=pltpu.SMEM)


def call(kernel, outs, n_in, scratch=(), scalars=1):
    return pl.pallas_call(
        kernel,
        out_shape=outs,
        in_specs=[SMEM] * scalars + [VMEM] * n_in,
        out_specs=[VMEM] * len(outs),
        scratch_shapes=list(scratch),
        compiler_params=LIMIT,
        cost_estimate=FREE,
    )


def like(shape, dtype=F32):
    return jax.ShapeDtypeStruct(shape, dtype)


def kshift_cols(v, dx):
    if dx == 0:
        return v
    c = v.shape[-1]
    rolled = pltpu.roll(v.reshape(R // 8, 8, c), 1 if dx < 0 else 7, 1).reshape(R, c)
    top = rolled[:64]
    place = lax.broadcasted_iota(jnp.int32, (64, c), 0) & 3
    top = jnp.where(place == (0 if dx < 0 else 3), 0.0, top)
    return jnp.concatenate([top, rolled[64:]], axis=0)


def kshift_frame(v, df):
    c = v.shape[-1]
    pc, pm, pf = split(v)
    half = pltpu.roll(pc.reshape(8, 8, c), 4, 1).reshape(2, 4, 8, c)
    zero = jnp.zeros_like(half[:1])
    first = lax.broadcasted_iota(jnp.int32, (2, 4, 8, c), 2) < 4
    if df < 0:
        oc = jnp.where(first, jnp.concatenate([zero, half[:-1]], axis=0), half)
    else:
        oc = jnp.where(first, half, jnp.concatenate([half[1:], zero], axis=0))
    out = [oc]
    for p in (pm, pf):
        zero = jnp.zeros_like(p[:1])
        out.append(jnp.concatenate([p[1:], zero] if df > 0 else [zero, p[:-1]], axis=0))
    return join(out)


def ktime_shift(v, back):
    lane = lax.broadcasted_iota(jnp.int32, v.shape, 1)
    a = kshift_frame(v, 1 if back else -1)
    b = kshift_frame(v, -1 if back else 1)
    return jnp.where(lane < SHIFT, a, jnp.where(lane < 2 * SHIFT, b, v))


def cols(st, c, w=128):
    return tuple(v[:, c * w : (c + 1) * w] for v in st)


def three(v):
    a = v.astype(BF16)
    rest = v - a.astype(F32)
    b = rest.astype(BF16)
    c = (rest - b.astype(F32)).astype(BF16)
    return a, b, c


def exact_dot(table, v):
    return sum(dot(table, part) for part in three(v))


def frame_sums(v):
    pc, pm, pf = split(v)
    first = lax.broadcasted_iota(jnp.int32, (2, 4, 8, v.shape[-1]), 2) < 4
    even = jnp.sum(jnp.where(first, pc, 0.0), axis=(1, 2))
    odd = jnp.sum(jnp.where(first, 0.0, pc), axis=(1, 2))
    pm = jnp.sum(pm, axis=(1, 2))
    pf = jnp.sum(pf, axis=(1, 2))
    rows = [even[0:1], odd[0:1], even[1:2], odd[1:2]]
    rows += [pm[f : f + 1] for f in range(4)] + [pf[f : f + 1] for f in range(4)]
    return jnp.concatenate(rows + [jnp.zeros((4, v.shape[-1]), F32)], axis=0)


def window_tables():
    pixel = WINDOWS.reshape(12, 9, R)
    table = np.zeros((160, R), np.float32)
    for slot in range(12):
        if slot % 4 < 3:
            for t in range(9):
                table[t * 16 + slot] = pixel[slot + 1, t]
        table[144 + slot] = pixel[slot, 4]
    spread = np.zeros((R, 16), np.float32)
    spread[:, :12] = SPREAD
    return table, np.concatenate([spread] * 3, axis=1)


TABLE, SPREAD3 = window_tables()


def phase_tables():
    out = []
    for side, pairs in zip(SIDES, (2, 1, 1)):
        high = 2 * side
        wide = 4 if side == 4 else 8
        count = side * wide * pairs
        t = np.zeros((4 * count, pairs * high * 16), np.float32)
        for ph in range(4):
            for p in range(pairs):
                for i in range(side):
                    for j in range(side):
                        row = ph * count + (i * pairs + p) * wide + j
                        at = (p * high + 2 * i + ph // 2) * 16 + 2 * j + ph % 2
                        t[row, at] = 1.0
        out.append(t)
    return out


PHASES = phase_tables()


def split_phases(alive, xc, xm, xf, tc, tm, tf, out_ref, bc, bm, bf):
    @pl.when(pl.program_id(0) == 0)
    def _():
        for b in (bc, bm, bf):
            b[...] = jnp.zeros_like(b)

    pieces = [[], [], [], []]
    lanes = out_ref.shape[-1]
    for g, (x, table, buf) in enumerate(((xc, tc, bc), (xm, tm, bm), (xf, tf, bf))):
        pairs = buf.shape[0]
        side = 2 * SIDES[g]
        for f in range(0, FRAMES, pairs):
            for p in range(pairs):
                live = alive[g * FRAMES + f + p] > 0.0
                buf[p, :, 0:side, :] = jnp.where(live, x[f + p], jnp.zeros_like(x[f + p]))
            y = dot(table[...], buf[...].reshape(-1, lanes))
            step = y.shape[0] // 4
            for ph in range(4):
                pieces[ph].append(y[ph * step : (ph + 1) * step])
    for ph in range(4):
        out_ref[ph] = jnp.concatenate(pieces[ph], axis=0).astype(BF16)


def clip_blocks(lanes):
    return [
        pl.BlockSpec((FRAMES, 2 * s, 2 * s, lanes), lambda c: (0, 0, 0, c)) for s in SIDES
    ]


def whole(v):
    return pl.BlockSpec(v.shape, lambda c: (0,) * v.ndim)


LIMIT = pltpu.CompilerParams(vmem_limit_bytes=60 * 2**20)


def run_split(alive, clips, tables):
    lanes = 256
    c_in = clips[0].shape[-1]
    return pl.pallas_call(
        split_phases,
        grid=(c_in // lanes,),
        out_shape=like((4, R, c_in), BF16),
        in_specs=[SMEM] + clip_blocks(lanes) + [whole(t) for t in tables],
        out_specs=pl.BlockSpec((4, R, lanes), lambda c: (0, 0, c)),
        scratch_shapes=[
            pltpu.VMEM((2 if s == 4 else 1, 2 * s, 16, lanes), BF16) for s in SIDES
        ],
        compiler_params=LIMIT,
        cost_estimate=FREE,
    )(alive, *clips, *tables)


def tiled(m, lanes):
    return jnp.concatenate([m] * (lanes // 128), axis=1)


class Flow:
    def __init__(self, far, near, sem, parts, axis, out):
        self.far, self.v, self.sem = far, near, sem
        self.parts, self.axis, self.out = parts, axis, out

    def copy(self, c):
        size = self.v.shape[self.axis] // self.parts
        at = [slice(None)] * len(self.v.shape)
        at[self.axis] = pl.ds(c * size, size)
        a, b = self.far.at[tuple(at)], self.v.at[tuple(at)]
        return pltpu.make_async_copy(*((b, a) if self.out else (a, b)), self.sem.at[c])

    def get(self, c=0):
        self.copy(c).wait()

    def put(self, c=0):
        self.copy(c).start()


class Plain:
    def __init__(self, ref):
        self.v = ref

    def get(self, c=0):
        pass

    def put(self, c=0):
        pass


def plain_call(body, scalars, small, ins, outs, small_outs=(), scratch=(), only=()):
    n_s, n_m, n_i, n_o, n_p = len(scalars), len(small), len(ins), len(outs), len(small_outs)

    def kernel(*refs):
        at = 0

        def take(k):
            nonlocal at
            at += k
            return refs[at - k : at]

        s, m, fi, fo, so = take(n_s), take(n_m), take(n_i), take(n_o), take(n_p)
        body(s, m, [Plain(r) for r in fi], [Plain(r) for r in fo], so, take(len(scratch)))

    return pl.pallas_call(
        kernel,
        out_shape=[like(o[0], o[1]) for o in outs] + list(small_outs),
        in_specs=[SMEM] * n_s + [VMEM] * (n_m + n_i),
        out_specs=[VMEM] * (n_o + n_p),
        scratch_shapes=list(scratch),
        compiler_params=LIMIT,
        cost_estimate=FREE,
    )(*scalars, *small, *[v for v, _, _ in ins])


def flow_call(body, scalars, small, ins, outs, small_outs=(), scratch=(), only=(), cost=FREE):
    n_s, n_m, n_i, n_o, n_p = len(scalars), len(small), len(ins), len(outs), len(small_outs)

    def kernel(*refs):
        at = 0

        def take(k):
            nonlocal at
            at += k
            return refs[at - k : at]

        s, m, far_in, far_out, so = take(n_s), take(n_m), take(n_i), take(n_o), take(n_p)
        near_in, near_out, extra = take(n_i), take(n_o), take(len(scratch))
        sem_in, sem_out = take(n_i), take(n_o)
        fi = [
            Flow(f, v, q, p, a, False)
            for f, v, q, (_, p, a) in zip(far_in, near_in, sem_in, ins)
        ]
        fo = [
            Flow(f, v, q, p, a, True)
            for f, v, q, (_, _, p, a) in zip(far_out, near_out, sem_out, outs)
        ]
        for c in range(max([f.parts for f in fi])):
            for i, f in enumerate(fi):
                if c < f.parts and (c == 0 or i not in only):
                    f.put(c)
        body(s, m, fi, fo, so, extra)
        for f in fo:
            for c in range(f.parts):
                f.get(c)

    any_space = pl.BlockSpec(memory_space=pl.ANY)
    return pl.pallas_call(
        kernel,
        out_shape=[like(o[0], o[1]) for o in outs] + list(small_outs),
        in_specs=[SMEM] * n_s + [VMEM] * n_m + [any_space] * n_i,
        out_specs=[any_space] * n_o + [VMEM] * n_p,
        scratch_shapes=[pltpu.VMEM(v.shape, v.dtype) for v, _, _ in ins]
        + [pltpu.VMEM(o[0], o[1]) for o in outs]
        + list(scratch)
        + [pltpu.SemaphoreType.DMA((p,)) for _, p, _ in ins]
        + [pltpu.SemaphoreType.DMA((o[2],)) for o in outs],
        compiler_params=LIMIT,
        cost_estimate=cost,
    )(*scalars, *small, *[v for v, _, _ in ins])


def put_rows(ref, row, vec):
    for j in range(vec.shape[1] // 128):
        ref[row + j : row + j + 1, :] = vec[:, j * 128 : (j + 1) * 128]


def get_rows(t, row, width):
    return jnp.concatenate([t[row + j : row + j + 1, :] for j in range(width // 128)], axis=1)


def spread_rows(ref, rows):
    @pl.loop(0, ref.shape[0])
    def _(i):
        ref[i] = rows


def pack_sums(a, b):
    out = []
    for v in (a, b):
        v = jnp.sum(v, axis=0, keepdims=True)
        out += [v[:, j * 128 : (j + 1) * 128] for j in range(v.shape[1] // 128)]
    return jnp.concatenate(out, axis=0)


def stats_of(got, count, gb, row=0, second=4, width=MID, lane=0):
    mean = get_rows(got, row, width) / count
    var = get_rows(got, second, width) / count - mean * mean
    sl = slice(lane, lane + width)
    return mean, lax.rsqrt(var + EPS), gb[0:1, sl], gb[1:2, sl]


def total_of(ref):
    return jnp.sum(ref[...], axis=0) if len(ref.shape) == 3 else ref[...]


def wide_stats(got, count, gb, c, base=0):
    return stats_of(got, count, gb, base + 4 * c, base + 16 + 4 * c, MID, c * MID)


def enter(s, m, ins, outs, so, extra):
    (x, w), (a1,) = ins, outs
    w.get()
    total = jnp.zeros((8, 128), F32)
    for ph in range(4):
        x.get(ph)
        a = dot(x.v[ph], w.v[...])
        a1.v[ph] = a
        a1.put(ph)
        total = total + pack_sums(a, a * a)
    spread_rows(so[0], total)


def run_enter(n, xph, w1):
    return flow_call(
        enter, (), (), [(w1, 1, 0), (xph, 4, 0)][::-1], [((4, R, MID), F32, 4, 0)],
        [like((n, 8, 128))],
    )


def conv_forward(s, m, ins, outs, so, extra):
    (cnt,), (s0, gb0, mask), (a1, w), (im, a2) = s, m, ins, outs
    live = mask[...]
    st = stats_of(total_of(s0), 4.0 * cnt[0], gb0[...])
    acc = None
    for ph in range(4):
        a1.get(ph)
        taps = [q for q in TAPS2 if q[0] == ph]
        for c in range(4):
            sl = slice(c * 128, (c + 1) * 128)
            stc = cols(st, c)
            h = live * silu(normalize(a1.v[ph, :, sl], stc)[1])
            h = h.astype(BF16).astype(F32)
            for dx in (0, -1):
                if dx and not ph & 1:
                    continue
                moved = kshift_cols(h, dx)
                for _, dy, dx2, t in taps:
                    if dx2 == dx:
                        at = t * MID + c * 128
                        im.v[:, at : at + 128] = shift_rows(moved, dy).astype(BF16)
        for _, _, _, t in taps:
            im.put(t)
        if ph == 0:
            w.get()
        for _, _, _, t in taps:
            sl = slice(t * MID, (t + 1) * MID)
            part = dot(im.v[:, sl], w.v[sl, :])
            acc = part if acc is None else acc + part
    acc = acc * tiled(live, MID)
    a2.v[...] = acc
    a2.put()
    spread_rows(so[0], pack_sums(acc, acc * acc))


def run_conv_forward(n, cnt, s0, gb0, mask, a1, w):
    return flow_call(
        conv_forward, (cnt,), (s0, gb0, mask), [(a1, 4, 0), (w, 1, 0)],
        [((R, 9 * MID), BF16, 9, 1), ((R, MID), F32, 1, 0)], [like((n, 8, 128))],
    )


def joint_norm(s, m, ins, outs, so, extra):
    (cnt,), (s23, gb2, gb3, mask), (a3, ap, w2), (y1, yl, b1) = s, m, ins, outs
    live = tiled(mask[...], MID)
    got = s23[...]
    acc = None
    for c in range(4):
        sl = slice(c * MID, (c + 1) * MID)
        a3.get(c)
        ap.get(c)
        gbs = [b[:, sl] for b in (gb2, gb3)]
        _, u2 = normalize(a3.v[:, sl], stats_of(got[c], cnt[0], gbs[0]))
        _, u3 = normalize(ap.v[:, sl], stats_of(got[c], cnt[0], gbs[1], 8, 12))
        y = live * silu(u2 + u3)
        y1.v[:, sl] = y
        y1.put(c)
        low = y.astype(BF16)
        yl.v[:, sl] = low
        yl.put(c)
        w2.get(c)
        part = dot(low, w2.v[sl, :])
        acc = part if acc is None else acc + part
    b1.v[...] = acc
    b1.put()
    spread_rows(so[0], pack_sums(acc, acc * acc))


def run_joint_norm(n, cnt, s23, gb2, gb3, mask, a3, ap, w2):
    return flow_call(
        joint_norm, (cnt,), (s23, gb2, gb3, mask), [(a3, 4, 1), (ap, 4, 1), (w2, 4, 0)],
        [((R, C_OUT), F32, 4, 1), ((R, C_OUT), BF16, 4, 1), ((R, MID), F32, 1, 0)],
        [like((n, 8, 128))],
    )


def mix_forward(s, m, ins, outs, so, extra):
    (cnt,) = s
    s4, gb4, mask, wdown, wup, kern, scale, table, spread = m
    (b1, wmix), (z, zl, mixed, im) = ins, outs
    sig_ref, pooled_ref, wnext_ref, sums_ref = so
    live = mask[...]
    st = stats_of(total_of(s4), cnt[0], gb4[...])
    b1.get()
    for c in range(4):
        sl = slice(c * 128, (c + 1) * 128)
        v = live * silu(normalize(b1.v[:, sl], cols(st, c))[1])
        z.v[:, sl] = v
        zl.v[:, sl] = v.astype(BF16)
    z.put()
    zl.put()
    r = dot(zl.v[...], wdown[...])
    ws = exact_dot(table[...], r)
    wnext_ref[...] = ws[:144]
    pooled = -ws[144:160]
    for t in range(9):
        pooled = pooled + kern[t : t + 1, :] * ws[t * 16 : (t + 1) * 16]
    pooled = scale[...] * pooled
    pooled_ref[...] = pooled
    sig = jax.nn.sigmoid(jnp.dot(pooled, wup[...], precision=HIGHEST))
    sig_ref[...] = sig
    gates = jnp.concatenate(three(0.5 + sig), axis=0)
    prev = None
    sums = []
    for c in range(4):
        sl = slice(c * 128, (c + 1) * 128)
        v = z.v[:, sl] * dot(spread[...], gates[:, sl])
        if c > 0:
            low = ktime_shift(v + prev, False).astype(BF16).astype(F32)
            for dx in (-1, 0, 1):
                moved = kshift_cols(low, dx)
                for dy in (-1, 0, 1):
                    t = (dy + 1) * 3 + dx + 1
                    im.v[c - 1, :, t * 128 : (t + 1) * 128] = shift_rows(moved, dy).astype(BF16)
            im.put(c - 1)
            if c == 1:
                wmix.get()
            v = live * dot(im.v[c - 1], wmix.v[c - 1])
        prev = v
        mixed.v[:, sl] = v
        sums.append((jnp.sum(v, axis=0, keepdims=True), jnp.sum(v * v, axis=0, keepdims=True)))
    mixed.put()
    spread_rows(sums_ref, jnp.concatenate([q[0] for q in sums] + [q[1] for q in sums], axis=0))


def run_mix_forward(n, cnt, s4, gb4, mask, wdown, wup, kern, scale, table, spread, b1, wmix):
    return flow_call(
        mix_forward, (cnt,), (s4, gb4, mask, wdown, wup, kern, scale, table, spread),
        [(b1, 1, 0), (wmix, 1, 0)],
        [((R, MID), F32, 1, 0), ((R, MID), BF16, 1, 0), ((R, MID), F32, 1, 0),
         ((3, R, 9 * GROUP), BF16, 3, 0)],
        [like((16, MID)), like((16, SQUEEZE)), like((144, SQUEEZE)), like((n, 8, 128))],
    )


def expand_last(s, m, ins, outs, so, extra):
    (cnt,), (s5, gb5, mask), (mixed, we2), (w, b3), (rows,) = s, m, ins, outs, extra
    live = tiled(mask[...], MID)
    mixed.get()
    h = live * silu(normalize(mixed.v[...], stats_of(total_of(s5), cnt[0], gb5[...]))[1])
    w.v[...] = h.astype(BF16)
    w.put()
    for c in range(4):
        sl = slice(c * MID, (c + 1) * MID)
        we2.get(c)
        a = dot(w.v[...], we2.v[:, sl])
        b3.v[:, sl] = a
        b3.put(c)
        put_rows(rows, 4 * c, jnp.sum(a, axis=0, keepdims=True))
        put_rows(rows, 16 + 4 * c, jnp.sum(a * a, axis=0, keepdims=True))
    so[0][...] = rows[...]


def run_expand_last(cnt, s5, gb5, mask, mixed, we2):
    return plain_call(
        expand_last, (cnt,), (s5, gb5, mask), [(mixed, 1, 0), (we2, 4, 1)],
        [((R, MID), BF16, 1, 0), ((R, C_OUT), F32, 4, 1)], [like((32, 128))],
        [pltpu.VMEM((32, 128), F32)],
    )


def last_norm(s, m, ins, outs, so, extra):
    (cnt,), (s6, gb6, mask), (b3, y1, cc, cm, cf), (oc, om, of, g6) = s, m, ins, outs
    bc, bm, bf, rows = extra
    for b in (bc, bm, bf):
        b[...] = jnp.zeros_like(b)
    live = tiled(mask[...], MID)
    got = total_of(s6)
    for c in range(4):
        sl = slice(c * MID, (c + 1) * MID)
        for f in ins:
            f.get(c)
        for f in range(FRAMES):
            p = f % 2
            bc[f // 2, :, p * 4 : p * 4 + 4, :] = cc.v[f, :, :, sl].astype(F32)
        bm[:, :, 0:6, :] = cm.v[..., sl].astype(F32)
        bf[:, :, 0:7, :] = cf.v[..., sl].astype(F32)
        cot = join((bc[...], bm[...], bf[...]))
        x, u = normalize(b3.v[:, sl], wide_stats(got, cnt[0], gb6[...], c))
        u = u + y1.v[:, sl]
        sg = jax.nn.sigmoid(u)
        pc, pm, pf = split(live * u * sg)
        for f in range(FRAMES):
            p = f % 2
            oc.v[f, :, :, sl] = pc[f // 2, :, p * 4 : p * 4 + 4, :].astype(BF16)
        om.v[..., sl] = pm[:, :, 0:6, :].astype(BF16)
        of.v[..., sl] = pf[:, :, 0:7, :].astype(BF16)
        g = cot * live * (sg * (1.0 + u * (1.0 - sg)))
        g6.v[:, sl] = g
        for f in outs:
            f.put(c)
        put_rows(rows, 4 * c, jnp.sum(g * x, axis=0, keepdims=True))
        put_rows(rows, 16 + 4 * c, jnp.sum(g, axis=0, keepdims=True))
    so[0][...] = rows[...]


def run_last_norm(cnt, s6, gb6, mask, b3, y1, cots):
    return flow_call(
        last_norm, (cnt,), (s6, gb6, mask), [(b3, 4, 1), (y1, 4, 1)] + [(v, 4, 3) for v in cots],
        [((FRAMES, q, q, C_OUT), BF16, 4, 3) for q in SIDES] + [((R, C_OUT), F32, 4, 1)],
        [like((32, 128))],
        [pltpu.VMEM((2 if q == 4 else 4, q, 8, MID), F32) for q in SIDES]
        + [pltpu.VMEM((32, 128), F32)],
    )


def back_rows(tot, c=None):
    if c is None:
        return get_rows(tot, 0, MID), get_rows(tot, 4, MID)
    return get_rows(tot, 4 * c, MID), get_rows(tot, 16 + 4 * c, MID)


def last_back(s, m, ins, outs, so, extra):
    (cnt,), (t6, s6, gb6, mask, s5, gb5), (g6, b3, w, we2, mixed), (ge2, g5) = s, m, ins, outs
    live = tiled(mask[...], MID)
    tot, got = total_of(t6), total_of(s6)
    w.get()
    acc = None
    for c in range(4):
        sl = slice(c * MID, (c + 1) * MID)
        g6.get(c)
        b3.get(c)
        st = wide_stats(got, cnt[0], gb6[...], c)
        x, _ = normalize(b3.v[:, sl], st)
        d = norm_back(g6.v[:, sl], x, live, st, back_rows(tot, c), cnt[0]).astype(BF16)
        ge2.v[:, sl] = dot_tn(w.v[...], d).astype(BF16)
        ge2.put(c)
        we2.get(c)
        part = dot_nt(d, we2.v[:, sl])
        acc = part if acc is None else acc + part
    mixed.get()
    x, u = normalize(mixed.v[...], stats_of(total_of(s5), cnt[0], gb5[...]))
    g = acc * live * silu_grad(u)
    g5.v[...] = g
    g5.put()
    spread_rows(so[0], pack_sums(g * x, g))


def run_last_back(n, cnt, t6, s6, gb6, mask, s5, gb5, g6, b3, w, we2, mixed):
    return plain_call(
        last_back, (cnt,), (t6, s6, gb6, mask, s5, gb5),
        [(g6, 4, 1), (b3, 4, 1), (w, 1, 0), (we2, 4, 1), (mixed, 1, 0)],
        [((MID, C_OUT), BF16, 4, 1), ((R, MID), F32, 1, 0)], [like((n, 8, 128))],
    )


def mix_backward(s, m, ins, outs, so, extra):
    (cnt,) = s
    (t5, s5, gb5, mask, sig, pooled, wnext, wup, kern, scale, table_t, spread, wdown, s4, gb4) = m
    (g5, mixed, imt, wmix_t, z, zl, b1), (g4, gmix) = ins, outs
    gkern_ref, gdown_ref, gup_ref, sums_ref = so
    gim, gzg = extra
    live = mask[...]
    count = cnt[0]
    st = stats_of(total_of(s5), count, gb5[...])
    tot = back_rows(total_of(t5))
    g5.get()
    mixed.get()
    carried = None
    gsig = []
    for c in (3, 2, 1, 0):
        sl = slice(c * 128, (c + 1) * 128)
        stc = cols(st, c)
        x, _ = normalize(mixed.v[:, sl], stc)
        gm = norm_back(g5.v[:, sl], x, live, stc, cols(tot, c), count)
        if carried is not None:
            gm = gm + carried
        if c > 0:
            low = (live * gm).astype(BF16)
            imt.get(c - 1)
            gmix.v[c - 1] = dot_tn(imt.v[c - 1], low).astype(BF16)
            gmix.put(c - 1)
            low = low.astype(F32)
            for dx in (-1, 0, 1):
                moved = kshift_cols(low, -dx)
                for dy in (-1, 0, 1):
                    t = (dy + 1) * 3 + dx + 1
                    gim[:, t * 128 : (t + 1) * 128] = shift_rows(moved, -dy).astype(BF16)
            if c == 3:
                wmix_t.get()
                z.get()
            gm = ktime_shift(dot(gim[...], wmix_t.v[c - 1]), True)
            carried = gm
        gzg[:, sl] = gm
        gsig.insert(0, frame_sums(gm * z.v[:, sl]))
    sg = sig[...]
    ge = jnp.concatenate(gsig, axis=1) * sg * (1.0 - sg)
    gup_ref[...] = lax.dot_general(
        pooled[...], ge, (((0,), (0,)), ((), ())), precision=HIGHEST, preferred_element_type=F32
    )
    q = scale[...] * lax.dot_general(
        ge, wup[...], (((1,), (1,)), ((), ())), precision=HIGHEST, preferred_element_type=F32
    )
    coef = []
    gk = []
    for t in range(9):
        gk.append(jnp.sum(q * wnext[t * 16 : (t + 1) * 16], axis=0, keepdims=True))
        coef.append(kern[t : t + 1, :] * q)
    gk = jnp.concatenate(gk + [jnp.zeros((7, SQUEEZE), F32)], axis=0)
    gkern_ref[...] = jnp.concatenate([gk, jnp.zeros((16, 128 - SQUEEZE), F32)], axis=1)
    coef = jnp.concatenate(coef + [-q], axis=0)
    gr = exact_dot(table_t[...], coef).astype(BF16)
    zl.get()
    gdown_ref[...] = dot_tn(zl.v[...], gr)
    gates = jnp.concatenate(three(0.5 + sg), axis=0)
    st = stats_of(total_of(s4), count, gb4[...])
    b1.get()
    sums = []
    for c in range(4):
        sl = slice(c * 128, (c + 1) * 128)
        gz = gzg[:, sl] * dot(spread[...], gates[:, sl]) + dot_nt(gr, wdown[sl, :])
        x, u = normalize(b1.v[:, sl], cols(st, c))
        g = gz * live * silu_grad(u)
        g4.v[:, sl] = g
        sums.append((jnp.sum(g * x, axis=0, keepdims=True), jnp.sum(g, axis=0, keepdims=True)))
    g4.put()
    spread_rows(sums_ref, jnp.concatenate([v[0] for v in sums] + [v[1] for v in sums], axis=0))


def run_mix_backward(n, cnt, small, g5, mixed, im, wmix_t, z, zl, b1):
    return plain_call(
        mix_backward, (cnt,), small,
        [(g5, 1, 0), (mixed, 1, 0), (im, 3, 0), (wmix_t, 1, 0), (z, 1, 0), (zl, 1, 0), (b1, 1, 0)],
        [((R, MID), F32, 1, 0), ((3, 9 * GROUP, GROUP), BF16, 3, 0)],
        [like((16, 128)), like((MID, SQUEEZE)), like((SQUEEZE, MID)), like((n, 8, 128))],
        [pltpu.VMEM((R, 9 * GROUP), BF16), pltpu.VMEM((R, MID), F32)],
    )


def spatial_grad(s, m, ins, outs, so, extra):
    (d1, im), (gsp,) = ins, outs
    for t in range(9):
        sl = slice(t * MID, (t + 1) * MID)
        gsp.v[sl, :] = dot_tn(im.v[:, sl], d1.v[...]).astype(BF16)


def run_spatial_grad(d1, im):
    return plain_call(
        spatial_grad, (), (), [(d1, 1, 0), (im, 9, 1)], [((9 * MID, MID), BF16, 9, 0)],
    )[0]


def conv_back(s, m, ins, outs, so, extra):
    (cnt,), (t1, s1, gb1, s0, gb0, mask), (moved_ref,) = s, m, extra
    (g1, a2, w, a1), (d1, g0) = ins, outs
    live = mask[...]
    st = stats_of(total_of(s1), cnt[0], gb1[...])
    tot = back_rows(total_of(t1))
    for c in range(4):
        sl = slice(c * 128, (c + 1) * 128)
        stc = cols(st, c)
        x, _ = normalize(a2.v[:, sl], stc)
        d = norm_back(g1.v[:, sl], x, live, stc, cols(tot, c), cnt[0]).astype(BF16)
        d1.v[:, sl] = d
        d = d.astype(F32)
        for dx in (0, 1):
            moved = kshift_cols(d, dx)
            for dy in (0, 1):
                moved_ref[dy * 2 + dx, :, sl] = shift_rows(moved, dy).astype(BF16)
    st = stats_of(total_of(s0), 4.0 * cnt[0], gb0[...])
    total = jnp.zeros((8, 128), F32)
    for ph in range(4):
        gh = None
        for p, dy, dx, t in TAPS2:
            if p == ph:
                part = dot_nt(moved_ref[-dy * 2 - dx], w.v[t * MID : (t + 1) * MID, :])
                gh = part if gh is None else gh + part
        sums = []
        for c in range(4):
            sl = slice(c * 128, (c + 1) * 128)
            x, u = normalize(a1.v[ph, :, sl], cols(st, c))
            g = gh[:, sl] * live * silu_grad(u)
            g0.v[ph, :, sl] = g
            sums.append((jnp.sum(g * x, axis=0, keepdims=True), jnp.sum(g, axis=0, keepdims=True)))
        total = total + jnp.concatenate([v[0] for v in sums] + [v[1] for v in sums], axis=0)
    spread_rows(so[0], total)


def run_conv_back(n, cnt, small, g1, a2, w, a1):
    return plain_call(
        conv_back, (cnt,), small, [(g1, 1, 0), (a2, 1, 0), (w, 1, 0), (a1, 4, 0)],
        [((R, MID), BF16, 1, 0), ((4, R, MID), F32, 4, 0)], [like((n, 8, 128))],
        [pltpu.VMEM((4, R, MID), BF16)],
    )


def first_grads(s, m, ins, outs, so, extra):
    (cnt,), (t0, s0, gb0, mask), (g0, a1, x), (d0, gr1) = s, m, ins, outs
    live = mask[...]
    count = 4.0 * cnt[0]
    st = stats_of(total_of(s0), count, gb0[...])
    tot = back_rows(total_of(t0))
    acc = None
    for ph in range(4):
        g0.get(ph)
        a1.get(ph)
        for c in range(4):
            sl = slice(c * 128, (c + 1) * 128)
            stc = cols(st, c)
            xh, _ = normalize(a1.v[ph, :, sl], stc)
            d = norm_back(g0.v[ph, :, sl], xh, live, stc, cols(tot, c), count)
            d0.v[ph, :, sl] = d.astype(BF16)
        d0.put(ph)
        x.get(ph)
        part = dot_tn(x.v[ph], d0.v[ph])
        acc = part if acc is None else acc + part
    gr1.v[...] = acc.astype(BF16)
    gr1.put()


def run_first_grads(cnt, small, g0, a1, xph):
    return flow_call(
        first_grads, (cnt,), small, [(g0, 4, 0), (a1, 4, 0), (xph, 4, 0)],
        [((4, R, MID), BF16, 4, 0), ((xph.shape[-1], MID), BF16, 1, 0)], cost=LONG,
    )


def wide_grid(kernel, outs, out_specs, ins, in_specs, scratch=(), steps=4):
    return pl.pallas_call(
        kernel,
        grid=(steps,),
        out_shape=outs,
        in_specs=in_specs,
        out_specs=out_specs,
        scratch_shapes=list(scratch),
        compiler_params=LIMIT,
        cost_estimate=FREE,
    )(*ins)


def fixed(shape):
    return pl.BlockSpec(shape, lambda c: (0,) * len(shape))


def column(rows, lanes):
    return pl.BlockSpec((rows, lanes), lambda c: (0, c))


def row_block(rows, width):
    return pl.BlockSpec((rows, width), lambda c: (c, 0))


CHUNK = pl.BlockSpec((1, 16, 128), lambda c: (c, 0, 0))


def accumulate(ref, part):
    first = pl.program_id(0) == 0

    @pl.when(first)
    def _():
        ref[...] = part

    @pl.when(jnp.logical_not(first))
    def _():
        ref[...] = ref[...] + part


def expand_pair(cnt, a2, s1, gb1, mask, w, x, wsk, h_ref, a3_ref, ap_ref, s_ref):
    @pl.when(pl.program_id(0) == 0)
    def _():
        m = tiled(mask[...], MID)
        h = m * silu(normalize(a2[...], stats_of(total_of(s1), cnt[0], gb1[...]))[1])
        h_ref[...] = h.astype(BF16)

    a = dot(h_ref[...], w[...])
    a3_ref[...] = a
    b = dot(x[0], wsk[...])
    ap_ref[...] = b
    s_ref[0] = jnp.concatenate([pack_sums(a, a * a), pack_sums(b, b * b)], axis=0)


def run_expand_pair(cnt, s1, gb1, mask, a2, we1, xph, wsk):
    c_in = xph.shape[-1]
    wide = column(R, MID)
    return wide_grid(
        expand_pair,
        [like((R, MID), BF16), like((R, C_OUT)), like((R, C_OUT)), like((4, 16, 128))],
        [fixed((R, MID)), wide, wide, CHUNK],
        (cnt, a2, s1, gb1, mask, we1, xph, wsk),
        [SMEM, fixed((R, MID)), fixed(s1.shape), fixed((2, MID)), fixed((R, 128)),
         column(MID, MID), pl.BlockSpec((1, R, c_in), lambda c: (0, 0, 0)), column(c_in, MID)],
    )


def joint_back(cnt, t4, s4, gb4, s23, gb2, gb3, mask, gk, g4, b1, yl, w2, g6, a3, ap,
               gr2_ref, gj_ref, pj_ref, d4_ref):
    m = tiled(mask[...], MID)

    @pl.when(pl.program_id(0) == 0)
    def _():
        st = stats_of(total_of(s4), cnt[0], gb4[...])
        x, _ = normalize(b1[...], st)
        d4_ref[...] = norm_back(g4[...], x, m, st, back_rows(total_of(t4)), cnt[0]).astype(BF16)

    d = d4_ref[...]
    gr2_ref[...] = dot_tn(yl[...], d).astype(BF16)
    gy = g6[...] + dot_nt(d, w2[...])
    got = s23[0]
    x2, u2 = normalize(a3[...], stats_of(got, cnt[0], gb2[...]))
    x3, u3 = normalize(ap[...], stats_of(got, cnt[0], gb3[...], 8, 12))
    g = gy * m * silu_grad(u2 + u3)
    gj_ref[...] = g
    pj_ref[0] = jnp.concatenate(
        [pack_sums(g * x2, g * x3), pack_sums(g, g)[:4], gk[0]], axis=0
    )


def run_joint_back(cnt, small, g4, b1, yl, w2, g6, a3, ap):
    t4, s4, gb4, s23, gb2, gb3, mask, gk = small
    wide, pair = column(R, MID), column(2, MID)
    one = fixed((R, MID))
    return wide_grid(
        joint_back,
        [like((C_OUT, MID), BF16), like((R, C_OUT)), like((4, 16, 128))],
        [row_block(MID, MID), wide, CHUNK],
        (cnt, t4, s4, gb4, s23, gb2, gb3, mask, gk.reshape(4, 4, 128), g4, b1, yl, w2, g6, a3, ap),
        [SMEM, fixed(t4.shape), fixed(s4.shape), fixed((2, MID)), CHUNK, pair, pair,
         fixed((R, 128)), pl.BlockSpec((1, 4, 128), lambda c: (c, 0, 0)), one, one, wide,
         row_block(MID, MID), wide, wide, wide],
        [pltpu.VMEM((R, MID), BF16)],
    )


def expand_back(cnt, tj, s23, gb2, gb3, mask, s1, gb1, gj, a3, ap, h2, x0, we1, a2,
                ge1_ref, gsk_ref, d3_ref, g1_ref, p1_ref):
    m = tiled(mask[...], MID)
    g = gj[...]
    tot, got = tj[0], s23[0]
    sum2, sum3, sumg = (get_rows(tot, 4 * k, MID) for k in range(3))
    st = stats_of(got, cnt[0], gb2[...])
    x, _ = normalize(a3[...], st)
    d = norm_back(g, x, m, st, (sum2, sumg), cnt[0]).astype(BF16)
    ge1_ref[...] = dot_tn(h2[...], d).astype(BF16)
    accumulate(g1_ref, dot_nt(d, we1[...]))
    st = stats_of(got, cnt[0], gb3[...], 8, 12)
    x, _ = normalize(ap[...], st)
    d = norm_back(g, x, m, st, (sum3, sumg), cnt[0]).astype(BF16)
    d3_ref[...] = d
    gsk_ref[...] = dot_tn(x0[0], d).astype(BF16)

    @pl.when(pl.program_id(0) == pl.num_programs(0) - 1)
    def _():
        x1, u1 = normalize(a2[...], stats_of(total_of(s1), cnt[0], gb1[...]))
        v = g1_ref[...] * m * silu_grad(u1)
        g1_ref[...] = v
        spread_rows(p1_ref, pack_sums(v * x1, v))


def run_expand_back(n, cnt, small, gj, a3, ap, h2, xph, we1, a2):
    tj, s23, gb2, gb3, mask, s1, gb1 = small
    wide, pair = column(R, MID), column(2, MID)
    one = fixed((R, MID))
    c_in = xph.shape[-1]
    return wide_grid(
        expand_back,
        [like((MID, C_OUT), BF16), like((c_in, C_OUT), BF16), like((R, C_OUT), BF16),
         like((R, MID)), like((n, 8, 128))],
        [column(MID, MID), column(c_in, MID), wide, one, fixed((n, 8, 128))],
        (cnt, tj, s23, gb2, gb3, mask, s1, gb1, gj, a3, ap, h2, xph, we1, a2),
        [SMEM, CHUNK, CHUNK, pair, pair, fixed((R, 128)), fixed(s1.shape), fixed((2, MID)),
         wide, wide, wide, one, pl.BlockSpec((1, R, c_in), lambda c: (0, 0, 0)),
         column(MID, MID), one],
    )


def input_grads(mask, tc, tm, tf, d0, d3, w1, wsk, oc, om, of):
    lanes = oc.shape[-1]
    m = tiled(mask[...], lanes)
    groups = []
    for ph in range(4):
        v = dot_nt(d0[ph], w1[...])
        if ph == 0:
            v = v + dot_nt(d3[...], wsk[...])
        groups.append(m * v)
    for g, (out, table) in enumerate(((oc, tc), (om, tm), (of, tf))):
        pairs = 2 if g == 0 else 1
        side = 2 * SIDES[g]
        step = ROWS[g] // (FRAMES // pairs)
        for f in range(0, FRAMES, pairs):
            at = CUTS[g] + (f // pairs) * step
            rows = jnp.concatenate([v[at : at + step] for v in groups], axis=0).astype(BF16)
            y = dot(table[...], rows).reshape(pairs, side, 16, lanes)
            for p in range(pairs):
                out[f + p] = y[p, :, 0:side, :].astype(BF16)


def run_input_grads(mask, tables, d0, d3, w1, wsk):
    lanes = 256
    c_in = w1.shape[0]
    return wide_grid(
        input_grads,
        [like((FRAMES, 2 * q, 2 * q, c_in), BF16) for q in SIDES],
        clip_blocks(lanes),
        (mask, *tables, d0, d3, w1, wsk),
        [fixed((R, 128))] + [fixed(t.shape) for t in tables]
        + [fixed(d0.shape), fixed(d3.shape), row_block(lanes, MID), row_block(lanes, C_OUT)],
        steps=c_in // lanes,
    )


def tie(*arrays):
    return lax.optimization_barrier(arrays)


def axes_bits(n, fsdp):
    bits = n.bit_length() - 1
    core = fsdp.bit_length() - 1
    return list(range(core)), core, core + 1, list(range(core + 2, bits))


def swap(v, d, n):
    return lax.ppermute(v, AXES, [(i, i ^ d) for i in range(n)])


def exchange(spread):
    return lax.all_to_all(spread, AXES, 0, 0, tiled=True)


def exchange_wide(rows, n, fsdp):
    core = axes_bits(n, fsdp)[1]
    half = rows.shape[0] // 2
    mine = ((lax.axis_index(AXES) >> core) & 1) == 0
    low, high = rows[:half], rows[half:]
    part = jnp.where(mine, low, high) + swap(jnp.where(mine, high, low), 1 << core, n)
    groups = [[i for i in range(n) if (i >> core) & 1 == k] for k in range(2)]
    got = lax.all_to_all(
        jnp.broadcast_to(part[None], (n // 2,) + part.shape), AXES, 0, 0,
        axis_index_groups=groups, tiled=True,
    )
    part = jnp.sum(got, axis=0)
    other = swap(part, 1 << core, n)
    return jnp.where(
        mine, jnp.concatenate([part, other], axis=0), jnp.concatenate([other, part], axis=0)
    )


def allsum_wide(rows, n, fsdp, beside=()):
    near, core, mid, far = axes_bits(n, fsdp)
    bits = near + [mid] + far
    for r in [[core]] + [bits[i : i + 2] for i in range(0, len(bits), 2)]:
        got = [
            swap(rows, sum(1 << b for j, b in enumerate(r) if m >> j & 1), n)
            for m in range(1, 1 << len(r))
        ]
        rows = sum(got, rows)
        if r == [core]:
            rows, *beside = tie(rows, *beside)
    return (rows, *beside) if beside else rows


def rows16(v):
    return jnp.pad(v, ((0, 0),) * (v.ndim - 2) + ((0, -v.shape[-2] % 16), (0, 0)))


def place_blocks(n, orders, core, heights, width):
    part = width // len(orders)

    def kernel(me_ref, *refs):
        srcs = refs[: 2 * len(orders)]
        outs = refs[2 * len(orders) : -1]
        sem = refs[-1]
        me = me_ref[0]
        for rel in range(n):
            for k, order in enumerate(orders):
                at = sum((rel >> b & 1) << j for j, b in enumerate(order))
                src = srcs[2 * k + (rel >> core & 1)]
                row = 0
                for i, (h, out) in enumerate(zip(heights, outs)):
                    pltpu.make_async_copy(
                        src.at[at, pl.ds(row, h)],
                        out.at[me ^ rel, :, pl.ds(k * part, part)],
                        sem.at[i],
                    ).start()
                    row += h
        for i, out in enumerate(outs):
            pltpu.make_async_copy(out, out, sem.at[i]).wait()

    return pl.pallas_call(
        kernel,
        out_shape=[jax.ShapeDtypeStruct((n, h, width), BF16) for h in heights],
        in_specs=[SMEM] + [pl.BlockSpec(memory_space=pl.ANY)] * (2 * len(orders)),
        out_specs=[VMEM] * len(heights),
        scratch_shapes=[pltpu.SemaphoreType.DMA((len(heights),))],
        compiler_params=LIMIT,
        cost_estimate=FREE,
    )


class Gather:
    def __init__(self, shards, n, fsdp):
        self.n = n
        self.near, self.core, self.mid, self.far = axes_bits(n, fsdp)
        self.shards = shards
        padded = [rows16(v.astype(BF16)) for v in shards]
        self.heights = [v.shape[0] for v in padded]
        self.x = jnp.concatenate(padded, axis=0) if len(padded) > 1 else padded[0]

    def first(self):
        got = []
        for m in range(1, 1 << len(self.far)):
            got.append(swap(self.x, sum(1 << b for j, b in enumerate(self.far) if m >> j & 1), self.n))
        self.hops = [self.x] + got

    def second(self):
        n = self.n
        bits = self.near + [self.mid]
        v = jnp.stack(self.hops)
        got = [v]
        for m in range(1, 1 << len(bits)):
            got.append(swap(v, sum(1 << b for j, b in enumerate(bits) if m >> j & 1), n))
        self.planes = [jnp.concatenate(got, axis=0)]
        self.orders = [self.far + bits]

    def split(self):
        width = self.x.shape[1]
        bits = self.near + [self.mid]
        self.paths = [bits, bits[::-1]]
        self.orders = [self.far + path for path in self.paths]
        v = jnp.stack(self.hops)
        self.planes = [v[..., : width // 2], v[..., width // 2 :]]

    def hop(self, k):
        self.got = [swap(v, 1 << p[k], self.n) for v, p in zip(self.planes, self.paths)]

    def land(self):
        self.planes = [jnp.concatenate([v, g], axis=0) for v, g in zip(self.planes, self.got)]

    def third(self):
        self.other = [swap(v, 1 << self.core, self.n) for v in self.planes]

    def finish(self, me):
        width = self.x.shape[1]
        planes = [v for pair in zip(self.planes, self.other) for v in pair]
        outs = place_blocks(self.n, self.orders, self.core, self.heights, width)(me, *planes)
        return [
            o.reshape(self.n * h, width)
            if h == v.shape[0]
            else o[:, : v.shape[0]].reshape(-1, width)
            for o, h, v in zip(outs, self.heights, self.shards)
        ]


def order_blocks(n, orders, pieces, width, arrays):
    heights = [arrays[i].shape[1] for i, _ in pieces]
    total = sum(heights)
    half = width // 2

    def kernel(me_ref, *refs):
        srcs = refs[: len(arrays)]
        outs = refs[len(arrays) : len(arrays) + 2]
        sem = refs[-1]
        me = me_ref[0]
        for rel in range(n):
            for k, order in enumerate(orders):
                at = 0
                for b in order:
                    at = at * 2 + (rel >> b & 1)
                side = at * 2 // n
                row = 0
                for (i, col), h in zip(pieces, heights):
                    pltpu.make_async_copy(
                        srcs[i].at[me ^ rel, :, pl.ds(col + k * half, half)],
                        outs[side].at[k, at % (n // 2), pl.ds(row, h)],
                        sem.at[side],
                    ).start()
                    row += h
        for k, out in enumerate(outs):
            pltpu.make_async_copy(out, out, sem.at[k]).wait()

    return pl.pallas_call(
        kernel,
        out_shape=[jax.ShapeDtypeStruct((2, n // 2, total, half), BF16)] * 2,
        in_specs=[SMEM] + [pl.BlockSpec(memory_space=pl.ANY)] * len(arrays),
        out_specs=[VMEM] * 2,
        scratch_shapes=[pltpu.SemaphoreType.DMA((2,))],
        compiler_params=LIMIT,
        cost_estimate=FREE,
    )


def add_blocks(keep, got, joined):
    m, rows, half = keep[0].shape[-3:]
    k_in = len(keep)

    if m == 1:
        outs = [like((rows, 2 * half))]
    elif joined:
        outs = [like((2, m // 2, rows, half), BF16)] * 2
    else:
        outs = [like((m // 2, rows, half), BF16)] * 4
    given = [*keep, *got]

    def kernel(*refs):
        k = 2 * k_in
        far_in, far_out = refs[:k], refs[k : k + len(outs)]
        ins, near_out = refs[k + len(outs) : 2 * k + len(outs)], refs[2 * k + len(outs) : -1]
        sem = refs[-1]
        moves = [
            pltpu.make_async_copy(f, v, sem.at[i]) for i, (f, v) in enumerate(zip(far_in, ins))
        ]
        for c in moves:
            c.start()
        for c in moves:
            c.wait()

        def total(k, i):
            if k_in == 1:
                return ins[0][k, i].astype(F32) + ins[1][k, i].astype(F32)
            return ins[k][i].astype(F32) + ins[2 + k][i].astype(F32)

        if m == 1:
            for k in range(2):
                near_out[0][:, k * half : (k + 1) * half] = total(k, 0)
        else:

            @pl.loop(0, m // 2)
            def _(i):
                for k in range(2):
                    for side in range(2):
                        v = total(k, i + side * (m // 2)).astype(BF16)
                        if joined:
                            near_out[side][k, i] = v
                        else:
                            near_out[2 * side + k][i] = v

        moves = [
            pltpu.make_async_copy(v, f, sem.at[2 * k_in + i])
            for i, (f, v) in enumerate(zip(far_out, near_out))
        ]
        for c in moves:
            c.start()
        for c in moves:
            c.wait()

    any_space = pl.BlockSpec(memory_space=pl.ANY)
    need = 2 * sum(v.size * v.dtype.itemsize for v in given) + 4 * 2**20
    return pl.pallas_call(
        kernel,
        out_shape=outs,
        in_specs=[any_space] * len(given),
        out_specs=[any_space] * len(outs),
        scratch_shapes=[pltpu.VMEM(v.shape, v.dtype) for v in given + outs]
        + [pltpu.SemaphoreType.DMA((len(given) + len(outs),))],
        compiler_params=pltpu.CompilerParams(vmem_limit_bytes=min(need, 56 * 2**20)),
        cost_estimate=FREE,
    )(*given)


def norm_rows(t0, t1, tj, t4, t5, t6, out):
    for half in range(2):
        row = 64 * half
        short = slice(4 * half, 4 * half + 4)
        out[row : row + 4, :] = total_of(t0)[short]
        out[row + 4 : row + 8, :] = total_of(t1)[short]
        for k in range(2):
            at = 8 if half else 4 * k
            for c in range(4):
                base = row + 8 + 16 * k + 4 * c
                out[base : base + 4, :] = tj[c, at : at + 4, :]
        out[row + 40 : row + 44, :] = total_of(t4)[short]
        out[row + 44 : row + 48, :] = total_of(t5)[short]
        out[row + 48 : row + 64, :] = t6[16 * half : 16 * half + 16, :]


class Scatter:
    def __init__(self, me, arrays, pieces, width, n, fsdp):
        self.n = n
        near, core, mid, self.far = axes_bits(n, fsdp)
        bits = near + [mid]
        self.paths = [bits, bits[::-1]]
        self.heights = [arrays[i].shape[1] for i, _ in pieces]
        orders = [[core] + path + self.far for path in self.paths]
        send, keep = order_blocks(n, orders, pieces, width, arrays)(me, *arrays)[::-1]
        self.send, self.keep = [send], [keep]
        self.hops = [[core]] + list(zip(*self.paths)) + [[b] for b in self.far]
        self.at = 0

    def start(self):
        self.got = [swap(v, 1 << b, self.n) for v, b in zip(self.send, self.hops[self.at])]
        self.at += 1

    def add(self):
        after = self.hops[self.at : self.at + 1]
        got = add_blocks(self.keep, self.got, bool(after) and len(after[0]) == 1)
        if not after:
            self.total = got[0]
        else:
            k = len(got) // 2
            self.keep, self.send = got[:k], got[k:]

    def end(self, x):
        x, *self.got = tie(x, *self.got)
        return x

    def ready(self, x):
        x, *self.send = tie(x, *self.send)
        self.start()
        return x

    def rest(self):
        self.add()
        while self.at < len(self.hops):
            self.start()
            self.add()
        out = []
        at = 0
        for h in self.heights:
            out.append(self.total[at : at + h])
            at += h
        return out


def body(n, fsdp, *args):
    (coarse, medium, fine, clip_counts, frame_counts, reduce_one, spatial_one, expand_one,
     shortcut_one, reduce_two, excite_down, excite_up, temporal_mix, expand_two, norm_params,
     motion_kernel, cot_c, cot_m, cot_f) = args
    near, core, mid, far = axes_bits(n, fsdp)

    def gather(w):
        return lax.all_gather(w.astype(BF16), AXES, axis=0, tiled=True)

    def flat(w):
        v = w.reshape(-1)
        return jnp.pad(v, (0, -v.size % MID)).reshape(-1, MID)

    def flat_back(got, w):
        return got.reshape(n, -1)[:, : w.size].reshape((n,) + w.shape)

    alive = (jnp.arange(4)[None, :] < frame_counts[0][:, None]) & (clip_counts[0][:, None] > 0)
    alive = alive.astype(F32)
    later = jnp.pad(alive[:, 1:], ((0, 0), (0, 1)))
    alive_slots = alive.reshape(12)
    later_slots = later.reshape(12)
    mask = (jnp.asarray(SPREAD) @ alive_slots)[:, None]
    per_group = jnp.sum(alive, axis=1)
    tables = [jnp.asarray(t, BF16) for t in PHASES]
    tables_t = [jnp.asarray(t.T, BF16) for t in PHASES]
    clips = [coarse, medium, fine]

    m128 = jnp.broadcast_to(mask, (R, 128))
    scale = later_slots / jnp.asarray(NPIX)
    scale = jnp.broadcast_to(jnp.pad(scale, (0, 4))[:, None], (16, SQUEEZE))
    table = jnp.asarray(TABLE, BF16)
    table_t = jnp.asarray(TABLE.T, BF16)
    spread = jnp.asarray(SPREAD3, BF16)
    me = lax.axis_index(AXES).astype(jnp.int32).reshape(1)
    small = jnp.concatenate([flat(norm_params), jnp.pad(per_group, (0, MID - 3))[None]], axis=0)
    ga = Gather([reduce_one, small], n, fsdp)
    gb_ = Gather([spatial_one], n, fsdp)
    gc_ = Gather([shortcut_one, expand_one], n, fsdp)
    tall = ga.x.shape[0]
    both = Gather([jnp.concatenate([ga.x, gb_.x], axis=0)], n, fsdp)
    both.first()
    xph = run_split(alive_slots, clips, tables)
    *both.hops, xph = tie(*both.hops, xph)
    xph, *late = tie(xph, reduce_two, excite_down, excite_up, temporal_mix, expand_two)
    narrow = [late[0], flat(late[1]), flat(late[2]), flat(late[3])]
    rows = [v.shape[0] for v in narrow]
    narrow = jnp.concatenate(narrow, axis=0)
    got = gather(jnp.pad(narrow, ((0, -narrow.shape[0] % 16), (0, 0))))
    we2 = gather(late[4])
    ga.hops = [v[:tall] for v in both.hops]
    gb_.hops = [v[tall:] for v in both.hops]
    ga.second()
    gb_.split()
    gb_.hop(0)
    ga.third()
    w1, norms = ga.finish(me)
    norms = norms.reshape(n, -1, MID)
    counts = jnp.sum(norms[:, -1, :3].astype(F32), axis=0)
    cnt = jnp.sum(counts * np.array([q * q for q in SIDES], np.float32)).reshape(1)
    norms = flat_back(norms[:, :-1], norm_params).transpose(1, 0, 2).reshape(2, -1).astype(F32)
    edges = [0, 512, 1024, 3072, 5120, 5632, 6144, 8192]
    gb = [norms[:, edges[k] : edges[k + 1]] for k in range(7)]

    for k in range(1, len(gb_.paths[0])):
        w1, *gb_.got = tie(w1, *gb_.got)
        gb_.land()
        w1, *gb_.planes = tie(w1, *gb_.planes)
        gb_.hop(k)
    w1, gc_.x = tie(w1, gc_.x)
    gc_.first()
    a1, p0 = run_enter(n, xph, w1)
    s0 = exchange(p0)
    s0, *rest = tie(s0, *gb_.got, *gc_.hops)
    gb_.got, gc_.hops = rest[:2], rest[2:]
    gb_.land()
    gb_.third()
    gc_.split()
    gc_.hop(0)
    wsp, = gb_.finish(me)
    for k in range(1, len(gc_.paths[0])):
        wsp, *gc_.got = tie(wsp, *gc_.got)
        gc_.land()
        wsp, *gc_.planes = tie(wsp, *gc_.planes)
        gc_.hop(k)
    im, a2, p1 = run_conv_forward(n, cnt, s0, gb[0], m128, a1, wsp)
    s1 = exchange(p1)
    s1, *gc_.got = tie(s1, *gc_.got)
    gc_.land()
    gc_.third()
    wsk, we1 = gc_.finish(me)
    h2, a3, ap, p2 = run_expand_pair(cnt, s1, gb[1], m128, a2, we1, xph, wsk)
    s23, got = allsum_wide(p2, n, fsdp, (got,))
    got = got.reshape(n, -1, MID)
    w2 = got[:, : rows[0]].reshape(C_OUT, MID)
    at = rows[0]
    wdown = flat_back(got[:, at : at + rows[1]], excite_down).reshape(MID, SQUEEZE)
    at += rows[1]
    wup = flat_back(got[:, at : at + rows[2]], excite_up)
    wup = wup.transpose(1, 0, 2).reshape(SQUEEZE, MID).astype(F32)
    at += rows[2]
    wmix = flat_back(got[:, at : at + rows[3]], temporal_mix)
    wmix = wmix.transpose(1, 0, 2).reshape(3, 9 * GROUP, GROUP)
    wmix_t = wmix.reshape(3, 9, GROUP, GROUP).transpose(0, 1, 3, 2).reshape(3, 9 * GROUP, GROUP)
    y1, y1_low, b1, p4 = run_joint_norm(n, cnt, s23, gb[2], gb[3], m128, a3, ap, w2)
    s4 = exchange(p4)
    z, z_low, mixed, mix_im, sig, pooled, wnext, p5 = run_mix_forward(
        n, cnt, s4, gb[4], m128, wdown, wup, motion_kernel, scale, table, spread, b1, wmix
    )
    s5 = exchange(p5)
    w, b3, p6 = run_expand_last(cnt, s5, gb[5], m128, mixed, we2)
    s6 = exchange_wide(p6, n, fsdp)
    o_c, o_m, o_f, g6, p6 = run_last_norm(cnt, s6, gb[6], m128, b3, y1, (cot_c, cot_m, cot_f))

    t6 = exchange_wide(p6, n, fsdp)
    ge2, g5, p5 = run_last_back(n, cnt, t6, s6, gb[6], m128, s5, gb[5], g6, b3, w, we2, mixed)
    t5 = exchange(p5)
    g4, gmix, gkernel, gdown, gup, p4 = run_mix_backward(
        n, cnt,
        (t5, s5, gb[5], m128, sig, pooled, wnext, wup, motion_kernel, scale, table_t, spread,
         wdown, s4, gb[4]),
        g5, mixed, mix_im, wmix_t, z, z_low, b1,
    )
    t4 = exchange(p4)
    gr2, gj, pj = run_joint_back(
        cnt, (t4, s4, gb[4], s23, gb[2], gb[3], m128, gkernel), g4, b1, y1_low, w2, g6, a3, ap
    )

    gmix = gmix.reshape(27, n, GROUP * GROUP // n).transpose(1, 0, 2).reshape(n, -1)
    gup = gup.reshape(SQUEEZE, n, MID // n).transpose(1, 0, 2).reshape(n, -1)
    thin = jnp.concatenate([gmix, gdown.reshape(n, -1).astype(BF16), gup.astype(BF16)], axis=1)
    thin = jnp.pad(thin, ((0, 0), (0, -thin.shape[1] % (16 * MID)))).reshape(n, -1, MID)

    def blocks(v):
        return rows16(v.reshape(n, -1, v.shape[-1]))

    starts = list(range(0, C_OUT, MID))
    tj, gr2, ge2, thin = allsum_wide(pj, n, fsdp, (gr2, ge2, thin))
    ra = Scatter(
        me, [blocks(gr2), thin, blocks(ge2)], [(0, 0), (1, 0)] + [(2, c) for c in starts], MID,
        n, fsdp,
    )
    ra.start()
    ra.add()
    tj = ra.ready(tj)
    ge1, gsk, d3, g1, p1 = run_expand_back(
        n, cnt, (tj, s23, gb[2], gb[3], m128, s1, gb[1]), gj, a3, ap, h2, xph, we1, a2
    )
    p1 = ra.end(p1)
    p1, ge1, gsk = tie(p1, ge1, gsk)
    t1 = exchange(p1)
    ra.add()
    rb = Scatter(
        me, [blocks(ge1), blocks(gsk)], [(i, c) for i in range(2) for c in starts], MID, n, fsdp
    )
    t1 = rb.ready(ra.ready(t1))
    d1, g0, p0 = run_conv_back(
        n, cnt, (t1, s1, gb[1], s0, gb[0], m128), g1, a2, wsp, a1
    )
    p0 = rb.end(ra.end(p0))
    p0, d1 = tie(p0, d1)
    t0 = exchange(p0)
    gsp = run_spatial_grad(d1, im)
    rc = Scatter(me, [blocks(gsp)], [(0, 0)], MID, n, fsdp)
    rb.add()
    t0 = rb.ready(rc.ready(t0))
    d0, gr1 = run_first_grads(cnt, (t0, s0, gb[0], m128), g0, a1, xph)
    d0 = rc.end(d0)
    rc.add()
    d0 = rc.ready(d0)
    gr1 = blocks(gr1)
    gr1 = gr1.reshape(n // (2 * fsdp), 2, fsdp, -1, MID)
    side = (me[0] >> core) & 1
    kept = lax.dynamic_index_in_dim(gr1, side, 1, keepdims=False)
    sent = lax.dynamic_index_in_dim(gr1, 1 - side, 1, keepdims=False)
    gr1 = (kept.astype(F32) + swap(sent, 1 << core, n).astype(F32)).astype(BF16)
    groups = [[i for i in range(n) if (i >> core) & 1 == k] for k in range(2)]
    got = lax.all_to_all(
        gr1.reshape(n // 2, -1, MID), AXES, 0, 0, axis_index_groups=groups, tiled=True
    )
    gin = list(run_input_grads(m128, tables_t, d0, d3, w1, wsk))
    gin[0] = rc.end(rb.end(gin[0]))
    rc.add()
    rb.add()
    ra.add()
    gin[0] = ra.ready(rb.ready(rc.ready(gin[0])))
    *rc.got, rb.got[0], ra.got[0] = tie(*rc.got, rb.got[0], ra.got[0])
    rc.add()
    rc.start()
    rb.add()
    rb.start()
    ra.add()
    ra.start()
    *rc.got, t0, t1, t4, t5, t6, tj, o_m, o_f = tie(*rc.got, t0, t1, t4, t5, t6, tj, o_m, o_f)
    rc.add()
    rc.start()
    *rc.got, got = tie(*rc.got, got)
    gr1 = jnp.sum(got.astype(F32), axis=0)[: reduce_one.shape[0]]
    second = ra.rest()
    gsp = rc.rest()[0][: spatial_one.shape[0]]
    first = rb.rest()

    def wide_back(parts, like_):
        return jnp.concatenate([p[: like_.shape[0]] for p in parts], axis=1)

    thin = second[1].reshape(-1)
    s1_ = temporal_mix.size
    s2_ = s1_ + excite_down.size
    s3_ = s2_ + excite_up.size

    gkernel = tj[:, 12:].reshape(16, 128)[:9, :SQUEEZE]
    gnorm = call(norm_rows, [like((128, 128))], 6, scalars=0)(t0, t1, tj, t4, t5, t6)[0]
    gnorm = lax.dynamic_slice_in_dim(gnorm.reshape(2, 8192), me[0] * (8192 // n), 8192 // n, 1)
    return (
        o_c, o_m, o_f, gin[0], gin[1], gin[2],
        gr1,
        gsp,
        wide_back(first[:4], expand_one),
        wide_back(first[4:], shortcut_one),
        second[0][: reduce_two.shape[0]],
        thin[s1_:s2_].reshape(excite_down.shape),
        thin[s2_:s3_].reshape(excite_up.shape),
        thin[:s1_].reshape(temporal_mix.shape),
        wide_back(second[2:], expand_two),
        gnorm,
        gkernel,
    )


def solution(mesh):
    n = mesh.shape["dp"] * mesh.shape["fsdp"]
    rows = P(AXES, None)
    cols = P(None, AXES)
    image = P(AXES, None, None, None)
    return jax.shard_map(
        partial(body, n, mesh.shape["fsdp"]),
        mesh=mesh,
        in_specs=(image, image, image, rows, rows, rows, rows, rows, rows, rows, rows, cols, cols,
                  rows, cols, P(), image, image, image),
        out_specs=(image, image, image, image, image, image, rows, rows, rows, rows, rows, rows,
                   cols, cols, rows, cols, P()),
        check_vma=False,
    )
```

```python
from functools import partial

import jax
import jax.numpy as jnp
from jax import lax
from jax.experimental import pallas as pl
from jax.experimental.pallas import tpu as pltpu
from jax.sharding import PartitionSpec as P
import numpy as np

MID = 512
C_OUT = 2048
FRAMES = 4
GROUP = 128
SHIFT = 16
SQUEEZE = 32
SIDES = (4, 6, 7)
AXES = ("dp", "fsdp")
EPS = 1e-05
HIGHEST = lax.Precision.HIGHEST
F32 = jnp.float32
BF16 = jnp.bfloat16

ROWS = (64, 192, 224)
CUTS = (0, 64, 256, 480)
R = 480


def row_tables():
    frame = np.zeros(R, np.int32)
    row = np.zeros(R, np.int32)
    col = np.zeros(R, np.int32)
    group = np.zeros(R, np.int32)
    at = 0
    for a in range(2):
        for i in range(4):
            for p in range(2):
                for j in range(4):
                    frame[at], row[at], col[at], group[at] = 2 * a + p, i, j, 0
                    at += 1
    for g in (1, 2):
        for f in range(4):
            for i in range(SIDES[g]):
                for j in range(8):
                    frame[at], row[at], col[at], group[at] = f, i, j, g
                    at += 1
    side = np.array(SIDES)[group]
    return group, frame, row, col, (col < side), side


GROUP_OF, FRAME_OF, ROW_OF, COL_OF, VALID, SIDE_OF = row_tables()
SLOT_OF = GROUP_OF * FRAMES + FRAME_OF


def window_table():
    table = np.zeros((12, 9, R), np.float32)
    for r in range(R):
        if not VALID[r]:
            continue
        for t in range(9):
            dy, dx = t // 3 - 1, t % 3 - 1
            i, j = ROW_OF[r] - dy, COL_OF[r] - dx
            if 0 <= i < SIDE_OF[r] and 0 <= j < SIDE_OF[r]:
                table[SLOT_OF[r], t, r] = 1.0
    return table.reshape(108, R)


WINDOWS = window_table()
SPREAD = ((SLOT_OF[:, None] == np.arange(12)[None]) & VALID[:, None]).astype(np.float32)
NPIX = np.repeat(np.array([s * s for s in SIDES], np.float32), FRAMES)


def split(v):
    c = v.shape[-1]
    return (
        v[0:64].reshape(2, 4, 8, c),
        v[64:256].reshape(4, 6, 8, c),
        v[256:480].reshape(4, 7, 8, c),
    )


def join(parts):
    return jnp.concatenate([p.reshape(-1, p.shape[-1]) for p in parts], axis=0)


def shift_rows(v, dy):
    if dy == 0:
        return v
    out = []
    for p in split(v):
        zero = jnp.zeros_like(p[:, :1])
        out.append(
            jnp.concatenate([p[:, 1:], zero] if dy > 0 else [zero, p[:, :-1]], axis=1)
        )
    return join(out)


def dot(a, b):
    return jnp.dot(a, b, preferred_element_type=F32)


def dot_nt(a, b):
    return lax.dot_general(a, b, (((1,), (1,)), ((), ())), preferred_element_type=F32)


def dot_tn(a, b):
    return lax.dot_general(a, b, (((0,), (0,)), ((), ())), preferred_element_type=F32)


def normalize(a, st):
    mean, rstd, gain, bias = st
    xhat = (a - mean) * rstd
    return xhat, xhat * gain + bias


def silu(u):
    return u * jax.nn.sigmoid(u)


def silu_grad(u):
    s = jax.nn.sigmoid(u)
    return s * (1.0 + u * (1.0 - s))


def norm_back(g, xhat, mask, st, tot, count):
    mean, rstd, gain, bias = st
    return gain * rstd * (g - mask * (tot[1] + xhat * tot[0]) / count)


TAPS2 = []
for kh in range(3):
    for kw in range(3):
        pr, dy = (1, -1) if kh == 0 else ((0, 0) if kh == 1 else (1, 0))
        pc, dx = (1, -1) if kw == 0 else ((0, 0) if kw == 1 else (1, 0))
        TAPS2.append((pr * 2 + pc, dy, dx, kh * 3 + kw))


FREE = pl.CostEstimate(flops=0, bytes_accessed=0, transcendentals=0)
LONG = pl.CostEstimate(flops=20 * 10**9, bytes_accessed=60 * 10**6, transcendentals=0)
VMEM = pl.BlockSpec(memory_space=pltpu.VMEM)
SMEM = pl.BlockSpec(memory_space=pltpu.SMEM)


def call(kernel, outs, n_in, scratch=(), scalars=1):
    return pl.pallas_call(
        kernel,
        out_shape=outs,
        in_specs=[SMEM] * scalars + [VMEM] * n_in,
        out_specs=[VMEM] * len(outs),
        scratch_shapes=list(scratch),
        compiler_params=LIMIT,
        cost_estimate=FREE,
    )


def like(shape, dtype=F32):
    return jax.ShapeDtypeStruct(shape, dtype)


def kshift_cols(v, dx):
    if dx == 0:
        return v
    c = v.shape[-1]
    rolled = pltpu.roll(v.reshape(R // 8, 8, c), 1 if dx < 0 else 7, 1).reshape(R, c)
    top = rolled[:64]
    place = lax.broadcasted_iota(jnp.int32, (64, c), 0) & 3
    top = jnp.where(place == (0 if dx < 0 else 3), 0.0, top)
    return jnp.concatenate([top, rolled[64:]], axis=0)


def kshift_frame(v, df):
    c = v.shape[-1]
    pc, pm, pf = split(v)
    half = pltpu.roll(pc.reshape(8, 8, c), 4, 1).reshape(2, 4, 8, c)
    zero = jnp.zeros_like(half[:1])
    first = lax.broadcasted_iota(jnp.int32, (2, 4, 8, c), 2) < 4
    if df < 0:
        oc = jnp.where(first, jnp.concatenate([zero, half[:-1]], axis=0), half)
    else:
        oc = jnp.where(first, half, jnp.concatenate([half[1:], zero], axis=0))
    out = [oc]
    for p in (pm, pf):
        zero = jnp.zeros_like(p[:1])
        out.append(jnp.concatenate([p[1:], zero] if df > 0 else [zero, p[:-1]], axis=0))
    return join(out)


def ktime_shift(v, back):
    lane = lax.broadcasted_iota(jnp.int32, v.shape, 1)
    a = kshift_frame(v, 1 if back else -1)
    b = kshift_frame(v, -1 if back else 1)
    return jnp.where(lane < SHIFT, a, jnp.where(lane < 2 * SHIFT, b, v))


def cols(st, c, w=128):
    return tuple(v[:, c * w : (c + 1) * w] for v in st)


def three(v):
    a = v.astype(BF16)
    rest = v - a.astype(F32)
    b = rest.astype(BF16)
    c = (rest - b.astype(F32)).astype(BF16)
    return a, b, c


def exact_dot(table, v):
    return sum(dot(table, part) for part in three(v))


def frame_sums(v):
    pc, pm, pf = split(v)
    first = lax.broadcasted_iota(jnp.int32, (2, 4, 8, v.shape[-1]), 2) < 4
    even = jnp.sum(jnp.where(first, pc, 0.0), axis=(1, 2))
    odd = jnp.sum(jnp.where(first, 0.0, pc), axis=(1, 2))
    pm = jnp.sum(pm, axis=(1, 2))
    pf = jnp.sum(pf, axis=(1, 2))
    rows = [even[0:1], odd[0:1], even[1:2], odd[1:2]]
    rows += [pm[f : f + 1] for f in range(4)] + [pf[f : f + 1] for f in range(4)]
    return jnp.concatenate(rows + [jnp.zeros((4, v.shape[-1]), F32)], axis=0)


def window_tables():
    pixel = WINDOWS.reshape(12, 9, R)
    table = np.zeros((160, R), np.float32)
    for slot in range(12):
        if slot % 4 < 3:
            for t in range(9):
                table[t * 16 + slot] = pixel[slot + 1, t]
        table[144 + slot] = pixel[slot, 4]
    spread = np.zeros((R, 16), np.float32)
    spread[:, :12] = SPREAD
    return table, np.concatenate([spread] * 3, axis=1)


TABLE, SPREAD3 = window_tables()


def phase_tables():
    out = []
    for side, pairs in zip(SIDES, (2, 1, 1)):
        high = 2 * side
        wide = 4 if side == 4 else 8
        count = side * wide * pairs
        t = np.zeros((4 * count, pairs * high * 16), np.float32)
        for ph in range(4):
            for p in range(pairs):
                for i in range(side):
                    for j in range(side):
                        row = ph * count + (i * pairs + p) * wide + j
                        at = (p * high + 2 * i + ph // 2) * 16 + 2 * j + ph % 2
                        t[row, at] = 1.0
        out.append(t)
    return out


PHASES = phase_tables()


def split_phases(alive, xc, xm, xf, tc, tm, tf, out_ref, bc, bm, bf):
    @pl.when(pl.program_id(0) == 0)
    def _():
        for b in (bc, bm, bf):
            b[...] = jnp.zeros_like(b)

    pieces = [[], [], [], []]
    lanes = out_ref.shape[-1]
    for g, (x, table, buf) in enumerate(((xc, tc, bc), (xm, tm, bm), (xf, tf, bf))):
        pairs = buf.shape[0]
        side = 2 * SIDES[g]
        for f in range(0, FRAMES, pairs):
            for p in range(pairs):
                live = alive[g * FRAMES + f + p] > 0.0
                buf[p, :, 0:side, :] = jnp.where(live, x[f + p], jnp.zeros_like(x[f + p]))
            y = dot(table[...], buf[...].reshape(-1, lanes))
            step = y.shape[0] // 4
            for ph in range(4):
                pieces[ph].append(y[ph * step : (ph + 1) * step])
    for ph in range(4):
        out_ref[ph] = jnp.concatenate(pieces[ph], axis=0).astype(BF16)


def clip_blocks(lanes):
    return [
        pl.BlockSpec((FRAMES, 2 * s, 2 * s, lanes), lambda c: (0, 0, 0, c)) for s in SIDES
    ]


def whole(v):
    return pl.BlockSpec(v.shape, lambda c: (0,) * v.ndim)


LIMIT = pltpu.CompilerParams(vmem_limit_bytes=60 * 2**20)


def run_split(alive, clips, tables):
    lanes = 256
    c_in = clips[0].shape[-1]
    return pl.pallas_call(
        split_phases,
        grid=(c_in // lanes,),
        out_shape=like((4, R, c_in), BF16),
        in_specs=[SMEM] + clip_blocks(lanes) + [whole(t) for t in tables],
        out_specs=pl.BlockSpec((4, R, lanes), lambda c: (0, 0, c)),
        scratch_shapes=[
            pltpu.VMEM((2 if s == 4 else 1, 2 * s, 16, lanes), BF16) for s in SIDES
        ],
        compiler_params=LIMIT,
        cost_estimate=FREE,
    )(alive, *clips, *tables)


def tiled(m, lanes):
    return jnp.concatenate([m] * (lanes // 128), axis=1)


class Flow:
    def __init__(self, far, near, sem, parts, axis, out):
        self.far, self.v, self.sem = far, near, sem
        self.parts, self.axis, self.out = parts, axis, out

    def copy(self, c):
        size = self.v.shape[self.axis] // self.parts
        at = [slice(None)] * len(self.v.shape)
        at[self.axis] = pl.ds(c * size, size)
        a, b = self.far.at[tuple(at)], self.v.at[tuple(at)]
        return pltpu.make_async_copy(*((b, a) if self.out else (a, b)), self.sem.at[c])

    def get(self, c=0):
        self.copy(c).wait()

    def put(self, c=0):
        self.copy(c).start()


class Plain:
    def __init__(self, ref):
        self.v = ref

    def get(self, c=0):
        pass

    def put(self, c=0):
        pass


def plain_call(body, scalars, small, ins, outs, small_outs=(), scratch=(), only=()):
    n_s, n_m, n_i, n_o, n_p = len(scalars), len(small), len(ins), len(outs), len(small_outs)

    def kernel(*refs):
        at = 0

        def take(k):
            nonlocal at
            at += k
            return refs[at - k : at]

        s, m, fi, fo, so = take(n_s), take(n_m), take(n_i), take(n_o), take(n_p)
        body(s, m, [Plain(r) for r in fi], [Plain(r) for r in fo], so, take(len(scratch)))

    return pl.pallas_call(
        kernel,
        out_shape=[like(o[0], o[1]) for o in outs] + list(small_outs),
        in_specs=[SMEM] * n_s + [VMEM] * (n_m + n_i),
        out_specs=[VMEM] * (n_o + n_p),
        scratch_shapes=list(scratch),
        compiler_params=LIMIT,
        cost_estimate=FREE,
    )(*scalars, *small, *[v for v, _, _ in ins])


def flow_call(body, scalars, small, ins, outs, small_outs=(), scratch=(), only=(), cost=FREE):
    n_s, n_m, n_i, n_o, n_p = len(scalars), len(small), len(ins), len(outs), len(small_outs)

    def kernel(*refs):
        at = 0

        def take(k):
            nonlocal at
            at += k
            return refs[at - k : at]

        s, m, far_in, far_out, so = take(n_s), take(n_m), take(n_i), take(n_o), take(n_p)
        near_in, near_out, extra = take(n_i), take(n_o), take(len(scratch))
        sem_in, sem_out = take(n_i), take(n_o)
        fi = [
            Flow(f, v, q, p, a, False)
            for f, v, q, (_, p, a) in zip(far_in, near_in, sem_in, ins)
        ]
        fo = [
            Flow(f, v, q, p, a, True)
            for f, v, q, (_, _, p, a) in zip(far_out, near_out, sem_out, outs)
        ]
        for c in range(max([f.parts for f in fi])):
            for i, f in enumerate(fi):
                if c < f.parts and (c == 0 or i not in only):
                    f.put(c)
        body(s, m, fi, fo, so, extra)
        for f in fo:
            for c in range(f.parts):
                f.get(c)

    any_space = pl.BlockSpec(memory_space=pl.ANY)
    return pl.pallas_call(
        kernel,
        out_shape=[like(o[0], o[1]) for o in outs] + list(small_outs),
        in_specs=[SMEM] * n_s + [VMEM] * n_m + [any_space] * n_i,
        out_specs=[any_space] * n_o + [VMEM] * n_p,
        scratch_shapes=[pltpu.VMEM(v.shape, v.dtype) for v, _, _ in ins]
        + [pltpu.VMEM(o[0], o[1]) for o in outs]
        + list(scratch)
        + [pltpu.SemaphoreType.DMA((p,)) for _, p, _ in ins]
        + [pltpu.SemaphoreType.DMA((o[2],)) for o in outs],
        compiler_params=LIMIT,
        cost_estimate=cost,
    )(*scalars, *small, *[v for v, _, _ in ins])


def put_rows(ref, row, vec):
    for j in range(vec.shape[1] // 128):
        ref[row + j : row + j + 1, :] = vec[:, j * 128 : (j + 1) * 128]


def get_rows(t, row, width):
    return jnp.concatenate([t[row + j : row + j + 1, :] for j in range(width // 128)], axis=1)


def spread_rows(ref, rows):
    @pl.loop(0, ref.shape[0])
    def _(i):
        ref[i] = rows


def pack_sums(a, b):
    out = []
    for v in (a, b):
        v = jnp.sum(v, axis=0, keepdims=True)
        out += [v[:, j * 128 : (j + 1) * 128] for j in range(v.shape[1] // 128)]
    return jnp.concatenate(out, axis=0)


def stats_of(got, count, gb, row=0, second=4, width=MID, lane=0):
    mean = get_rows(got, row, width) / count
    var = get_rows(got, second, width) / count - mean * mean
    sl = slice(lane, lane + width)
    return mean, lax.rsqrt(var + EPS), gb[0:1, sl], gb[1:2, sl]


def total_of(ref):
    return jnp.sum(ref[...], axis=0) if len(ref.shape) == 3 else ref[...]


def wide_stats(got, count, gb, c, base=0):
    return stats_of(got, count, gb, base + 4 * c, base + 16 + 4 * c, MID, c * MID)


def enter(s, m, ins, outs, so, extra):
    (x, w), (a1,) = ins, outs
    w.get()
    total = jnp.zeros((8, 128), F32)
    for ph in range(4):
        x.get(ph)
        a = dot(x.v[ph], w.v[...])
        a1.v[ph] = a
        a1.put(ph)
        total = total + pack_sums(a, a * a)
    spread_rows(so[0], total)


def run_enter(n, xph, w1):
    return flow_call(
        enter, (), (), [(w1, 1, 0), (xph, 4, 0)][::-1], [((4, R, MID), F32, 4, 0)],
        [like((n, 8, 128))],
    )


def conv_forward(s, m, ins, outs, so, extra):
    (cnt,), (s0, gb0, mask), (a1, w), (im, a2) = s, m, ins, outs
    live = mask[...]
    st = stats_of(total_of(s0), 4.0 * cnt[0], gb0[...])
    acc = None
    for ph in range(4):
        a1.get(ph)
        taps = [q for q in TAPS2 if q[0] == ph]
        for c in range(4):
            sl = slice(c * 128, (c + 1) * 128)
            stc = cols(st, c)
            h = live * silu(normalize(a1.v[ph, :, sl], stc)[1])
            h = h.astype(BF16).astype(F32)
            for dx in (0, -1):
                if dx and not ph & 1:
                    continue
                moved = kshift_cols(h, dx)
                for _, dy, dx2, t in taps:
                    if dx2 == dx:
                        at = t * MID + c * 128
                        im.v[:, at : at + 128] = shift_rows(moved, dy).astype(BF16)
        for _, _, _, t in taps:
            im.put(t)
        if ph == 0:
            w.get()
        for _, _, _, t in taps:
            sl = slice(t * MID, (t + 1) * MID)
            part = dot(im.v[:, sl], w.v[sl, :])
            acc = part if acc is None else acc + part
    acc = acc * tiled(live, MID)
    a2.v[...] = acc
    a2.put()
    spread_rows(so[0], pack_sums(acc, acc * acc))


def run_conv_forward(n, cnt, s0, gb0, mask, a1, w):
    return flow_call(
        conv_forward, (cnt,), (s0, gb0, mask), [(a1, 4, 0), (w, 1, 0)],
        [((R, 9 * MID), BF16, 9, 1), ((R, MID), F32, 1, 0)], [like((n, 8, 128))],
    )


def joint_norm(s, m, ins, outs, so, extra):
    (cnt,), (s23, gb2, gb3, mask), (a3, ap, w2), (y1, yl, b1) = s, m, ins, outs
    live = tiled(mask[...], MID)
    got = s23[...]
    acc = None
    for c in range(4):
        sl = slice(c * MID, (c + 1) * MID)
        a3.get(c)
        ap.get(c)
        gbs = [b[:, sl] for b in (gb2, gb3)]
        _, u2 = normalize(a3.v[:, sl], stats_of(got[c], cnt[0], gbs[0]))
        _, u3 = normalize(ap.v[:, sl], stats_of(got[c], cnt[0], gbs[1], 8, 12))
        y = live * silu(u2 + u3)
        y1.v[:, sl] = y
        y1.put(c)
        low = y.astype(BF16)
        yl.v[:, sl] = low
        yl.put(c)
        w2.get(c)
        part = dot(low, w2.v[sl, :])
        acc = part if acc is None else acc + part
    b1.v[...] = acc
    b1.put()
    spread_rows(so[0], pack_sums(acc, acc * acc))


def run_joint_norm(n, cnt, s23, gb2, gb3, mask, a3, ap, w2):
    return flow_call(
        joint_norm, (cnt,), (s23, gb2, gb3, mask), [(a3, 4, 1), (ap, 4, 1), (w2, 4, 0)],
        [((R, C_OUT), F32, 4, 1), ((R, C_OUT), BF16, 4, 1), ((R, MID), F32, 1, 0)],
        [like((n, 8, 128))],
    )


def mix_forward(s, m, ins, outs, so, extra):
    (cnt,) = s
    s4, gb4, mask, wdown, wup, kern, scale, table, spread = m
    (b1, wmix), (z, zl, mixed, im) = ins, outs
    sig_ref, pooled_ref, wnext_ref, sums_ref = so
    live = mask[...]
    st = stats_of(total_of(s4), cnt[0], gb4[...])
    b1.get()
    for c in range(4):
        sl = slice(c * 128, (c + 1) * 128)
        v = live * silu(normalize(b1.v[:, sl], cols(st, c))[1])
        z.v[:, sl] = v
        zl.v[:, sl] = v.astype(BF16)
    z.put()
    zl.put()
    r = dot(zl.v[...], wdown[...])
    ws = exact_dot(table[...], r)
    wnext_ref[...] = ws[:144]
    pooled = -ws[144:160]
    for t in range(9):
        pooled = pooled + kern[t : t + 1, :] * ws[t * 16 : (t + 1) * 16]
    pooled = scale[...] * pooled
    pooled_ref[...] = pooled
    sig = jax.nn.sigmoid(jnp.dot(pooled, wup[...], precision=HIGHEST))
    sig_ref[...] = sig
    gates = jnp.concatenate(three(0.5 + sig), axis=0)
    prev = None
    sums = []
    for c in range(4):
        sl = slice(c * 128, (c + 1) * 128)
        v = z.v[:, sl] * dot(spread[...], gates[:, sl])
        if c > 0:
            low = ktime_shift(v + prev, False).astype(BF16).astype(F32)
            for dx in (-1, 0, 1):
                moved = kshift_cols(low, dx)
                for dy in (-1, 0, 1):
                    t = (dy + 1) * 3 + dx + 1
                    im.v[c - 1, :, t * 128 : (t + 1) * 128] = shift_rows(moved, dy).astype(BF16)
            im.put(c - 1)
            if c == 1:
                wmix.get()
            v = live * dot(im.v[c - 1], wmix.v[c - 1])
        prev = v
        mixed.v[:, sl] = v
        sums.append((jnp.sum(v, axis=0, keepdims=True), jnp.sum(v * v, axis=0, keepdims=True)))
    mixed.put()
    spread_rows(sums_ref, jnp.concatenate([q[0] for q in sums] + [q[1] for q in sums], axis=0))


def run_mix_forward(n, cnt, s4, gb4, mask, wdown, wup, kern, scale, table, spread, b1, wmix):
    return flow_call(
        mix_forward, (cnt,), (s4, gb4, mask, wdown, wup, kern, scale, table, spread),
        [(b1, 1, 0), (wmix, 1, 0)],
        [((R, MID), F32, 1, 0), ((R, MID), BF16, 1, 0), ((R, MID), F32, 1, 0),
         ((3, R, 9 * GROUP), BF16, 3, 0)],
        [like((16, MID)), like((16, SQUEEZE)), like((144, SQUEEZE)), like((n, 8, 128))],
    )


def expand_last(s, m, ins, outs, so, extra):
    (cnt,), (s5, gb5, mask), (mixed, we2), (w, b3), (rows,) = s, m, ins, outs, extra
    live = tiled(mask[...], MID)
    mixed.get()
    h = live * silu(normalize(mixed.v[...], stats_of(total_of(s5), cnt[0], gb5[...]))[1])
    w.v[...] = h.astype(BF16)
    w.put()
    for c in range(4):
        sl = slice(c * MID, (c + 1) * MID)
        we2.get(c)
        a = dot(w.v[...], we2.v[:, sl])
        b3.v[:, sl] = a
        b3.put(c)
        put_rows(rows, 4 * c, jnp.sum(a, axis=0, keepdims=True))
        put_rows(rows, 16 + 4 * c, jnp.sum(a * a, axis=0, keepdims=True))
    so[0][...] = rows[...]


def run_expand_last(cnt, s5, gb5, mask, mixed, we2):
    return plain_call(
        expand_last, (cnt,), (s5, gb5, mask), [(mixed, 1, 0), (we2, 4, 1)],
        [((R, MID), BF16, 1, 0), ((R, C_OUT), F32, 4, 1)], [like((32, 128))],
        [pltpu.VMEM((32, 128), F32)],
    )


def last_norm(s, m, ins, outs, so, extra):
    (cnt,), (s6, gb6, mask), (b3, y1, cc, cm, cf), (oc, om, of, g6) = s, m, ins, outs
    bc, bm, bf, rows = extra
    for b in (bc, bm, bf):
        b[...] = jnp.zeros_like(b)
    live = tiled(mask[...], MID)
    got = total_of(s6)
    for c in range(4):
        sl = slice(c * MID, (c + 1) * MID)
        for f in ins:
            f.get(c)
        for f in range(FRAMES):
            p = f % 2
            bc[f // 2, :, p * 4 : p * 4 + 4, :] = cc.v[f, :, :, sl].astype(F32)
        bm[:, :, 0:6, :] = cm.v[..., sl].astype(F32)
        bf[:, :, 0:7, :] = cf.v[..., sl].astype(F32)
        cot = join((bc[...], bm[...], bf[...]))
        x, u = normalize(b3.v[:, sl], wide_stats(got, cnt[0], gb6[...], c))
        u = u + y1.v[:, sl]
        sg = jax.nn.sigmoid(u)
        pc, pm, pf = split(live * u * sg)
        for f in range(FRAMES):
            p = f % 2
            oc.v[f, :, :, sl] = pc[f // 2, :, p * 4 : p * 4 + 4, :].astype(BF16)
        om.v[..., sl] = pm[:, :, 0:6, :].astype(BF16)
        of.v[..., sl] = pf[:, :, 0:7, :].astype(BF16)
        g = cot * live * (sg * (1.0 + u * (1.0 - sg)))
        g6.v[:, sl] = g
        for f in outs:
            f.put(c)
        put_rows(rows, 4 * c, jnp.sum(g * x, axis=0, keepdims=True))
        put_rows(rows, 16 + 4 * c, jnp.sum(g, axis=0, keepdims=True))
    so[0][...] = rows[...]


def run_last_norm(cnt, s6, gb6, mask, b3, y1, cots):
    return flow_call(
        last_norm, (cnt,), (s6, gb6, mask), [(b3, 4, 1), (y1, 4, 1)] + [(v, 4, 3) for v in cots],
        [((FRAMES, q, q, C_OUT), BF16, 4, 3) for q in SIDES] + [((R, C_OUT), F32, 4, 1)],
        [like((32, 128))],
        [pltpu.VMEM((2 if q == 4 else 4, q, 8, MID), F32) for q in SIDES]
        + [pltpu.VMEM((32, 128), F32)],
    )


def back_rows(tot, c=None):
    if c is None:
        return get_rows(tot, 0, MID), get_rows(tot, 4, MID)
    return get_rows(tot, 4 * c, MID), get_rows(tot, 16 + 4 * c, MID)


def last_back(s, m, ins, outs, so, extra):
    (cnt,), (t6, s6, gb6, mask, s5, gb5), (g6, b3, w, we2, mixed), (ge2, g5) = s, m, ins, outs
    live = tiled(mask[...], MID)
    tot, got = total_of(t6), total_of(s6)
    w.get()
    acc = None
    for c in range(4):
        sl = slice(c * MID, (c + 1) * MID)
        g6.get(c)
        b3.get(c)
        st = wide_stats(got, cnt[0], gb6[...], c)
        x, _ = normalize(b3.v[:, sl], st)
        d = norm_back(g6.v[:, sl], x, live, st, back_rows(tot, c), cnt[0]).astype(BF16)
        ge2.v[:, sl] = dot_tn(w.v[...], d).astype(BF16)
        ge2.put(c)
        we2.get(c)
        part = dot_nt(d, we2.v[:, sl])
        acc = part if acc is None else acc + part
    mixed.get()
    x, u = normalize(mixed.v[...], stats_of(total_of(s5), cnt[0], gb5[...]))
    g = acc * live * silu_grad(u)
    g5.v[...] = g
    g5.put()
    spread_rows(so[0], pack_sums(g * x, g))


def run_last_back(n, cnt, t6, s6, gb6, mask, s5, gb5, g6, b3, w, we2, mixed):
    return plain_call(
        last_back, (cnt,), (t6, s6, gb6, mask, s5, gb5),
        [(g6, 4, 1), (b3, 4, 1), (w, 1, 0), (we2, 4, 1), (mixed, 1, 0)],
        [((MID, C_OUT), BF16, 4, 1), ((R, MID), F32, 1, 0)], [like((n, 8, 128))],
    )


def mix_backward(s, m, ins, outs, so, extra):
    (cnt,) = s
    (t5, s5, gb5, mask, sig, pooled, wnext, wup, kern, scale, table_t, spread, wdown, s4, gb4) = m
    (g5, mixed, imt, wmix_t, z, zl, b1), (g4, gmix) = ins, outs
    gkern_ref, gdown_ref, gup_ref, sums_ref = so
    gim, gzg = extra
    live = mask[...]
    count = cnt[0]
    st = stats_of(total_of(s5), count, gb5[...])
    tot = back_rows(total_of(t5))
    g5.get()
    mixed.get()
    carried = None
    gsig = []
    for c in (3, 2, 1, 0):
        sl = slice(c * 128, (c + 1) * 128)
        stc = cols(st, c)
        x, _ = normalize(mixed.v[:, sl], stc)
        gm = norm_back(g5.v[:, sl], x, live, stc, cols(tot, c), count)
        if carried is not None:
            gm = gm + carried
        if c > 0:
            low = (live * gm).astype(BF16)
            imt.get(c - 1)
            gmix.v[c - 1] = dot_tn(imt.v[c - 1], low).astype(BF16)
            gmix.put(c - 1)
            low = low.astype(F32)
            for dx in (-1, 0, 1):
                moved = kshift_cols(low, -dx)
                for dy in (-1, 0, 1):
                    t = (dy + 1) * 3 + dx + 1
                    gim[:, t * 128 : (t + 1) * 128] = shift_rows(moved, -dy).astype(BF16)
            if c == 3:
                wmix_t.get()
                z.get()
            gm = ktime_shift(dot(gim[...], wmix_t.v[c - 1]), True)
            carried = gm
        gzg[:, sl] = gm
        gsig.insert(0, frame_sums(gm * z.v[:, sl]))
    sg = sig[...]
    ge = jnp.concatenate(gsig, axis=1) * sg * (1.0 - sg)
    gup_ref[...] = lax.dot_general(
        pooled[...], ge, (((0,), (0,)), ((), ())), precision=HIGHEST, preferred_element_type=F32
    )
    q = scale[...] * lax.dot_general(
        ge, wup[...], (((1,), (1,)), ((), ())), precision=HIGHEST, preferred_element_type=F32
    )
    coef = []
    gk = []
    for t in range(9):
        gk.append(jnp.sum(q * wnext[t * 16 : (t + 1) * 16], axis=0, keepdims=True))
        coef.append(kern[t : t + 1, :] * q)
    gk = jnp.concatenate(gk + [jnp.zeros((7, SQUEEZE), F32)], axis=0)
    gkern_ref[...] = jnp.concatenate([gk, jnp.zeros((16, 128 - SQUEEZE), F32)], axis=1)
    coef = jnp.concatenate(coef + [-q], axis=0)
    gr = exact_dot(table_t[...], coef).astype(BF16)
    zl.get()
    gdown_ref[...] = dot_tn(zl.v[...], gr)
    gates = jnp.concatenate(three(0.5 + sg), axis=0)
    st = stats_of(total_of(s4), count, gb4[...])
    b1.get()
    sums = []
    for c in range(4):
        sl = slice(c * 128, (c + 1) * 128)
        gz = gzg[:, sl] * dot(spread[...], gates[:, sl]) + dot_nt(gr, wdown[sl, :])
        x, u = normalize(b1.v[:, sl], cols(st, c))
        g = gz * live * silu_grad(u)
        g4.v[:, sl] = g
        sums.append((jnp.sum(g * x, axis=0, keepdims=True), jnp.sum(g, axis=0, keepdims=True)))
    g4.put()
    spread_rows(sums_ref, jnp.concatenate([v[0] for v in sums] + [v[1] for v in sums], axis=0))


def run_mix_backward(n, cnt, small, g5, mixed, im, wmix_t, z, zl, b1):
    return plain_call(
        mix_backward, (cnt,), small,
        [(g5, 1, 0), (mixed, 1, 0), (im, 3, 0), (wmix_t, 1, 0), (z, 1, 0), (zl, 1, 0), (b1, 1, 0)],
        [((R, MID), F32, 1, 0), ((3, 9 * GROUP, GROUP), BF16, 3, 0)],
        [like((16, 128)), like((MID, SQUEEZE)), like((SQUEEZE, MID)), like((n, 8, 128))],
        [pltpu.VMEM((R, 9 * GROUP), BF16), pltpu.VMEM((R, MID), F32)],
    )


def spatial_grad(s, m, ins, outs, so, extra):
    (d1, im), (gsp,) = ins, outs
    for t in range(9):
        sl = slice(t * MID, (t + 1) * MID)
        gsp.v[sl, :] = dot_tn(im.v[:, sl], d1.v[...]).astype(BF16)


def run_spatial_grad(d1, im):
    return plain_call(
        spatial_grad, (), (), [(d1, 1, 0), (im, 9, 1)], [((9 * MID, MID), BF16, 9, 0)],
    )[0]


def conv_back(s, m, ins, outs, so, extra):
    (cnt,), (t1, s1, gb1, s0, gb0, mask), (moved_ref,) = s, m, extra
    (g1, a2, w, a1), (d1, g0) = ins, outs
    live = mask[...]
    st = stats_of(total_of(s1), cnt[0], gb1[...])
    tot = back_rows(total_of(t1))
    for c in range(4):
        sl = slice(c * 128, (c + 1) * 128)
        stc = cols(st, c)
        x, _ = normalize(a2.v[:, sl], stc)
        d = norm_back(g1.v[:, sl], x, live, stc, cols(tot, c), cnt[0]).astype(BF16)
        d1.v[:, sl] = d
        d = d.astype(F32)
        for dx in (0, 1):
            moved = kshift_cols(d, dx)
            for dy in (0, 1):
                moved_ref[dy * 2 + dx, :, sl] = shift_rows(moved, dy).astype(BF16)
    st = stats_of(total_of(s0), 4.0 * cnt[0], gb0[...])
    total = jnp.zeros((8, 128), F32)
    for ph in range(4):
        gh = None
        for p, dy, dx, t in TAPS2:
            if p == ph:
                part = dot_nt(moved_ref[-dy * 2 - dx], w.v[t * MID : (t + 1) * MID, :])
                gh = part if gh is None else gh + part
        sums = []
        for c in range(4):
            sl = slice(c * 128, (c + 1) * 128)
            x, u = normalize(a1.v[ph, :, sl], cols(st, c))
            g = gh[:, sl] * live * silu_grad(u)
            g0.v[ph, :, sl] = g
            sums.append((jnp.sum(g * x, axis=0, keepdims=True), jnp.sum(g, axis=0, keepdims=True)))
        total = total + jnp.concatenate([v[0] for v in sums] + [v[1] for v in sums], axis=0)
    spread_rows(so[0], total)


def run_conv_back(n, cnt, small, g1, a2, w, a1):
    return plain_call(
        conv_back, (cnt,), small, [(g1, 1, 0), (a2, 1, 0), (w, 1, 0), (a1, 4, 0)],
        [((R, MID), BF16, 1, 0), ((4, R, MID), F32, 4, 0)], [like((n, 8, 128))],
        [pltpu.VMEM((4, R, MID), BF16)],
    )


def first_grads(s, m, ins, outs, so, extra):
    (cnt,), (t0, s0, gb0, mask), (g0, a1, x), (d0, gr1) = s, m, ins, outs
    live = mask[...]
    count = 4.0 * cnt[0]
    st = stats_of(total_of(s0), count, gb0[...])
    tot = back_rows(total_of(t0))
    acc = None
    for ph in range(4):
        g0.get(ph)
        a1.get(ph)
        for c in range(4):
            sl = slice(c * 128, (c + 1) * 128)
            stc = cols(st, c)
            xh, _ = normalize(a1.v[ph, :, sl], stc)
            d = norm_back(g0.v[ph, :, sl], xh, live, stc, cols(tot, c), count)
            d0.v[ph, :, sl] = d.astype(BF16)
        d0.put(ph)
        x.get(ph)
        part = dot_tn(x.v[ph], d0.v[ph])
        acc = part if acc is None else acc + part
    gr1.v[...] = acc.astype(BF16)
    gr1.put()


def run_first_grads(cnt, small, g0, a1, xph):
    return flow_call(
        first_grads, (cnt,), small, [(g0, 4, 0), (a1, 4, 0), (xph, 4, 0)],
        [((4, R, MID), BF16, 4, 0), ((xph.shape[-1], MID), BF16, 1, 0)], cost=LONG,
    )


def wide_grid(kernel, outs, out_specs, ins, in_specs, scratch=(), steps=4):
    return pl.pallas_call(
        kernel,
        grid=(steps,),
        out_shape=outs,
        in_specs=in_specs,
        out_specs=out_specs,
        scratch_shapes=list(scratch),
        compiler_params=LIMIT,
        cost_estimate=FREE,
    )(*ins)


def fixed(shape):
    return pl.BlockSpec(shape, lambda c: (0,) * len(shape))


def column(rows, lanes):
    return pl.BlockSpec((rows, lanes), lambda c: (0, c))


def row_block(rows, width):
    return pl.BlockSpec((rows, width), lambda c: (c, 0))


CHUNK = pl.BlockSpec((1, 16, 128), lambda c: (c, 0, 0))


def accumulate(ref, part):
    first = pl.program_id(0) == 0

    @pl.when(first)
    def _():
        ref[...] = part

    @pl.when(jnp.logical_not(first))
    def _():
        ref[...] = ref[...] + part


def expand_pair(cnt, a2, s1, gb1, mask, w, x, wsk, h_ref, a3_ref, ap_ref, s_ref):
    @pl.when(pl.program_id(0) == 0)
    def _():
        m = tiled(mask[...], MID)
        h = m * silu(normalize(a2[...], stats_of(total_of(s1), cnt[0], gb1[...]))[1])
        h_ref[...] = h.astype(BF16)

    a = dot(h_ref[...], w[...])
    a3_ref[...] = a
    b = dot(x[0], wsk[...])
    ap_ref[...] = b
    s_ref[0] = jnp.concatenate([pack_sums(a, a * a), pack_sums(b, b * b)], axis=0)


def run_expand_pair(cnt, s1, gb1, mask, a2, we1, xph, wsk):
    c_in = xph.shape[-1]
    wide = column(R, MID)
    return wide_grid(
        expand_pair,
        [like((R, MID), BF16), like((R, C_OUT)), like((R, C_OUT)), like((4, 16, 128))],
        [fixed((R, MID)), wide, wide, CHUNK],
        (cnt, a2, s1, gb1, mask, we1, xph, wsk),
        [SMEM, fixed((R, MID)), fixed(s1.shape), fixed((2, MID)), fixed((R, 128)),
         column(MID, MID), pl.BlockSpec((1, R, c_in), lambda c: (0, 0, 0)), column(c_in, MID)],
    )


def joint_back(cnt, t4, s4, gb4, s23, gb2, gb3, mask, gk, g4, b1, yl, w2, g6, a3, ap,
               gr2_ref, gj_ref, pj_ref, d4_ref):
    m = tiled(mask[...], MID)

    @pl.when(pl.program_id(0) == 0)
    def _():
        st = stats_of(total_of(s4), cnt[0], gb4[...])
        x, _ = normalize(b1[...], st)
        d4_ref[...] = norm_back(g4[...], x, m, st, back_rows(total_of(t4)), cnt[0]).astype(BF16)

    d = d4_ref[...]
    gr2_ref[...] = dot_tn(yl[...], d).astype(BF16)
    gy = g6[...] + dot_nt(d, w2[...])
    got = s23[0]
    x2, u2 = normalize(a3[...], stats_of(got, cnt[0], gb2[...]))
    x3, u3 = normalize(ap[...], stats_of(got, cnt[0], gb3[...], 8, 12))
    g = gy * m * silu_grad(u2 + u3)
    gj_ref[...] = g
    pj_ref[0] = jnp.concatenate(
        [pack_sums(g * x2, g * x3), pack_sums(g, g)[:4], gk[0]], axis=0
    )


def run_joint_back(cnt, small, g4, b1, yl, w2, g6, a3, ap):
    t4, s4, gb4, s23, gb2, gb3, mask, gk = small
    wide, pair = column(R, MID), column(2, MID)
    one = fixed((R, MID))
    return wide_grid(
        joint_back,
        [like((C_OUT, MID), BF16), like((R, C_OUT)), like((4, 16, 128))],
        [row_block(MID, MID), wide, CHUNK],
        (cnt, t4, s4, gb4, s23, gb2, gb3, mask, gk.reshape(4, 4, 128), g4, b1, yl, w2, g6, a3, ap),
        [SMEM, fixed(t4.shape), fixed(s4.shape), fixed((2, MID)), CHUNK, pair, pair,
         fixed((R, 128)), pl.BlockSpec((1, 4, 128), lambda c: (c, 0, 0)), one, one, wide,
         row_block(MID, MID), wide, wide, wide],
        [pltpu.VMEM((R, MID), BF16)],
    )


def expand_back(cnt, tj, s23, gb2, gb3, mask, s1, gb1, gj, a3, ap, h2, x0, we1, a2,
                ge1_ref, gsk_ref, d3_ref, g1_ref, p1_ref):
    m = tiled(mask[...], MID)
    g = gj[...]
    tot, got = tj[0], s23[0]
    sum2, sum3, sumg = (get_rows(tot, 4 * k, MID) for k in range(3))
    st = stats_of(got, cnt[0], gb2[...])
    x, _ = normalize(a3[...], st)
    d = norm_back(g, x, m, st, (sum2, sumg), cnt[0]).astype(BF16)
    ge1_ref[...] = dot_tn(h2[...], d).astype(BF16)
    accumulate(g1_ref, dot_nt(d, we1[...]))
    st = stats_of(got, cnt[0], gb3[...], 8, 12)
    x, _ = normalize(ap[...], st)
    d = norm_back(g, x, m, st, (sum3, sumg), cnt[0]).astype(BF16)
    d3_ref[...] = d
    gsk_ref[...] = dot_tn(x0[0], d).astype(BF16)

    @pl.when(pl.program_id(0) == pl.num_programs(0) - 1)
    def _():
        x1, u1 = normalize(a2[...], stats_of(total_of(s1), cnt[0], gb1[...]))
        v = g1_ref[...] * m * silu_grad(u1)
        g1_ref[...] = v
        spread_rows(p1_ref, pack_sums(v * x1, v))


def run_expand_back(n, cnt, small, gj, a3, ap, h2, xph, we1, a2):
    tj, s23, gb2, gb3, mask, s1, gb1 = small
    wide, pair = column(R, MID), column(2, MID)
    one = fixed((R, MID))
    c_in = xph.shape[-1]
    return wide_grid(
        expand_back,
        [like((MID, C_OUT), BF16), like((c_in, C_OUT), BF16), like((R, C_OUT), BF16),
         like((R, MID)), like((n, 8, 128))],
        [column(MID, MID), column(c_in, MID), wide, one, fixed((n, 8, 128))],
        (cnt, tj, s23, gb2, gb3, mask, s1, gb1, gj, a3, ap, h2, xph, we1, a2),
        [SMEM, CHUNK, CHUNK, pair, pair, fixed((R, 128)), fixed(s1.shape), fixed((2, MID)),
         wide, wide, wide, one, pl.BlockSpec((1, R, c_in), lambda c: (0, 0, 0)),
         column(MID, MID), one],
    )


def input_grads(mask, tc, tm, tf, d0, d3, w1, wsk, oc, om, of):
    lanes = oc.shape[-1]
    m = tiled(mask[...], lanes)
    groups = []
    for ph in range(4):
        v = dot_nt(d0[ph], w1[...])
        if ph == 0:
            v = v + dot_nt(d3[...], wsk[...])
        groups.append(m * v)
    for g, (out, table) in enumerate(((oc, tc), (om, tm), (of, tf))):
        pairs = 2 if g == 0 else 1
        side = 2 * SIDES[g]
        step = ROWS[g] // (FRAMES // pairs)
        for f in range(0, FRAMES, pairs):
            at = CUTS[g] + (f // pairs) * step
            rows = jnp.concatenate([v[at : at + step] for v in groups], axis=0).astype(BF16)
            y = dot(table[...], rows).reshape(pairs, side, 16, lanes)
            for p in range(pairs):
                out[f + p] = y[p, :, 0:side, :].astype(BF16)


def run_input_grads(mask, tables, d0, d3, w1, wsk):
    lanes = 256
    c_in = w1.shape[0]
    return wide_grid(
        input_grads,
        [like((FRAMES, 2 * q, 2 * q, c_in), BF16) for q in SIDES],
        clip_blocks(lanes),
        (mask, *tables, d0, d3, w1, wsk),
        [fixed((R, 128))] + [fixed(t.shape) for t in tables]
        + [fixed(d0.shape), fixed(d3.shape), row_block(lanes, MID), row_block(lanes, C_OUT)],
        steps=c_in // lanes,
    )


def tie(*arrays):
    return lax.optimization_barrier(arrays)


def axes_bits(n, fsdp):
    bits = n.bit_length() - 1
    core = fsdp.bit_length() - 1
    return list(range(core)), core, core + 1, list(range(core + 2, bits))


def swap(v, d, n):
    return lax.ppermute(v, AXES, [(i, i ^ d) for i in range(n)])


def exchange(spread):
    return lax.all_to_all(spread, AXES, 0, 0, tiled=True)


def exchange_wide(rows, n, fsdp):
    core = axes_bits(n, fsdp)[1]
    half = rows.shape[0] // 2
    mine = ((lax.axis_index(AXES) >> core) & 1) == 0
    low, high = rows[:half], rows[half:]
    part = jnp.where(mine, low, high) + swap(jnp.where(mine, high, low), 1 << core, n)
    groups = [[i for i in range(n) if (i >> core) & 1 == k] for k in range(2)]
    got = lax.all_to_all(
        jnp.broadcast_to(part[None], (n // 2,) + part.shape), AXES, 0, 0,
        axis_index_groups=groups, tiled=True,
    )
    part = jnp.sum(got, axis=0)
    other = swap(part, 1 << core, n)
    return jnp.where(
        mine, jnp.concatenate([part, other], axis=0), jnp.concatenate([other, part], axis=0)
    )


def allsum_wide(rows, n, fsdp, beside=()):
    near, core, mid, far = axes_bits(n, fsdp)
    bits = near + [mid] + far
    for r in [[core]] + [bits[i : i + 2] for i in range(0, len(bits), 2)]:
        got = [
            swap(rows, sum(1 << b for j, b in enumerate(r) if m >> j & 1), n)
            for m in range(1, 1 << len(r))
        ]
        rows = sum(got, rows)
        if r == [core]:
            rows, *beside = tie(rows, *beside)
    return (rows, *beside) if beside else rows


def rows16(v):
    return jnp.pad(v, ((0, 0),) * (v.ndim - 2) + ((0, -v.shape[-2] % 16), (0, 0)))


def place_blocks(n, orders, core, heights, width):
    part = width // len(orders)

    def kernel(me_ref, *refs):
        srcs = refs[: 2 * len(orders)]
        outs = refs[2 * len(orders) : -1]
        sem = refs[-1]
        me = me_ref[0]
        for rel in range(n):
            for k, order in enumerate(orders):
                at = sum((rel >> b & 1) << j for j, b in enumerate(order))
                src = srcs[2 * k + (rel >> core & 1)]
                row = 0
                for i, (h, out) in enumerate(zip(heights, outs)):
                    pltpu.make_async_copy(
                        src.at[at, pl.ds(row, h)],
                        out.at[me ^ rel, :, pl.ds(k * part, part)],
                        sem.at[i],
                    ).start()
                    row += h
        for i, out in enumerate(outs):
            pltpu.make_async_copy(out, out, sem.at[i]).wait()

    return pl.pallas_call(
        kernel,
        out_shape=[jax.ShapeDtypeStruct((n, h, width), BF16) for h in heights],
        in_specs=[SMEM] + [pl.BlockSpec(memory_space=pl.ANY)] * (2 * len(orders)),
        out_specs=[VMEM] * len(heights),
        scratch_shapes=[pltpu.SemaphoreType.DMA((len(heights),))],
        compiler_params=LIMIT,
        cost_estimate=FREE,
    )


class Gather:
    def __init__(self, shards, n, fsdp):
        self.n = n
        self.near, self.core, self.mid, self.far = axes_bits(n, fsdp)
        self.shards = shards
        padded = [rows16(v.astype(BF16)) for v in shards]
        self.heights = [v.shape[0] for v in padded]
        self.x = jnp.concatenate(padded, axis=0) if len(padded) > 1 else padded[0]

    def first(self):
        got = []
        for m in range(1, 1 << len(self.far)):
            got.append(swap(self.x, sum(1 << b for j, b in enumerate(self.far) if m >> j & 1), self.n))
        self.hops = [self.x] + got

    def second(self):
        n = self.n
        bits = self.near + [self.mid]
        v = jnp.stack(self.hops)
        got = [v]
        for m in range(1, 1 << len(bits)):
            got.append(swap(v, sum(1 << b for j, b in enumerate(bits) if m >> j & 1), n))
        self.planes = [jnp.concatenate(got, axis=0)]
        self.orders = [self.far + bits]

    def split(self):
        width = self.x.shape[1]
        bits = self.near + [self.mid]
        self.paths = [bits, bits[::-1]]
        self.orders = [self.far + path for path in self.paths]
        v = jnp.stack(self.hops)
        self.planes = [v[..., : width // 2], v[..., width // 2 :]]

    def hop(self, k):
        self.got = [swap(v, 1 << p[k], self.n) for v, p in zip(self.planes, self.paths)]

    def land(self):
        self.planes = [jnp.concatenate([v, g], axis=0) for v, g in zip(self.planes, self.got)]

    def third(self):
        self.other = [swap(v, 1 << self.core, self.n) for v in self.planes]

    def finish(self, me):
        width = self.x.shape[1]
        planes = [v for pair in zip(self.planes, self.other) for v in pair]
        outs = place_blocks(self.n, self.orders, self.core, self.heights, width)(me, *planes)
        return [
            o.reshape(self.n * h, width)
            if h == v.shape[0]
            else o[:, : v.shape[0]].reshape(-1, width)
            for o, h, v in zip(outs, self.heights, self.shards)
        ]


def order_blocks(n, orders, pieces, width, arrays):
    heights = [arrays[i].shape[1] for i, _ in pieces]
    total = sum(heights)
    half = width // 2

    def kernel(me_ref, *refs):
        srcs = refs[: len(arrays)]
        outs = refs[len(arrays) : len(arrays) + 2]
        sem = refs[-1]
        me = me_ref[0]
        for rel in range(n):
            for k, order in enumerate(orders):
                at = 0
                for b in order:
                    at = at * 2 + (rel >> b & 1)
                side = at * 2 // n
                row = 0
                for (i, col), h in zip(pieces, heights):
                    pltpu.make_async_copy(
                        srcs[i].at[me ^ rel, :, pl.ds(col + k * half, half)],
                        outs[side].at[k, at % (n // 2), pl.ds(row, h)],
                        sem.at[side],
                    ).start()
                    row += h
        for k, out in enumerate(outs):
            pltpu.make_async_copy(out, out, sem.at[k]).wait()

    return pl.pallas_call(
        kernel,
        out_shape=[jax.ShapeDtypeStruct((2, n // 2, total, half), BF16)] * 2,
        in_specs=[SMEM] + [pl.BlockSpec(memory_space=pl.ANY)] * len(arrays),
        out_specs=[VMEM] * 2,
        scratch_shapes=[pltpu.SemaphoreType.DMA((2,))],
        compiler_params=LIMIT,
        cost_estimate=FREE,
    )


def add_blocks(keep, got, joined):
    m, rows, half = keep[0].shape[-3:]
    k_in = len(keep)

    if m == 1:
        outs = [like((rows, 2 * half))]
    elif joined:
        outs = [like((2, m // 2, rows, half), BF16)] * 2
    else:
        outs = [like((m // 2, rows, half), BF16)] * 4
    given = [*keep, *got]

    def kernel(*refs):
        k = 2 * k_in
        far_in, far_out = refs[:k], refs[k : k + len(outs)]
        ins, near_out = refs[k + len(outs) : 2 * k + len(outs)], refs[2 * k + len(outs) : -1]
        sem = refs[-1]
        moves = [
            pltpu.make_async_copy(f, v, sem.at[i]) for i, (f, v) in enumerate(zip(far_in, ins))
        ]
        for c in moves:
            c.start()
        for c in moves:
            c.wait()

        def total(k, i):
            if k_in == 1:
                return ins[0][k, i].astype(F32) + ins[1][k, i].astype(F32)
            return ins[k][i].astype(F32) + ins[2 + k][i].astype(F32)

        if m == 1:
            for k in range(2):
                near_out[0][:, k * half : (k + 1) * half] = total(k, 0)
        else:

            @pl.loop(0, m // 2)
            def _(i):
                for k in range(2):
                    for side in range(2):
                        v = total(k, i + side * (m // 2)).astype(BF16)
                        if joined:
                            near_out[side][k, i] = v
                        else:
                            near_out[2 * side + k][i] = v

        moves = [
            pltpu.make_async_copy(v, f, sem.at[2 * k_in + i])
            for i, (f, v) in enumerate(zip(far_out, near_out))
        ]
        for c in moves:
            c.start()
        for c in moves:
            c.wait()

    any_space = pl.BlockSpec(memory_space=pl.ANY)
    need = 2 * sum(v.size * v.dtype.itemsize for v in given) + 4 * 2**20
    return pl.pallas_call(
        kernel,
        out_shape=outs,
        in_specs=[any_space] * len(given),
        out_specs=[any_space] * len(outs),
        scratch_shapes=[pltpu.VMEM(v.shape, v.dtype) for v in given + outs]
        + [pltpu.SemaphoreType.DMA((len(given) + len(outs),))],
        compiler_params=pltpu.CompilerParams(vmem_limit_bytes=min(need, 56 * 2**20)),
        cost_estimate=FREE,
    )(*given)


def norm_rows(t0, t1, tj, t4, t5, t6, out):
    for half in range(2):
        row = 64 * half
        short = slice(4 * half, 4 * half + 4)
        out[row : row + 4, :] = total_of(t0)[short]
        out[row + 4 : row + 8, :] = total_of(t1)[short]
        for k in range(2):
            at = 8 if half else 4 * k
            for c in range(4):
                base = row + 8 + 16 * k + 4 * c
                out[base : base + 4, :] = tj[c, at : at + 4, :]
        out[row + 40 : row + 44, :] = total_of(t4)[short]
        out[row + 44 : row + 48, :] = total_of(t5)[short]
        out[row + 48 : row + 64, :] = t6[16 * half : 16 * half + 16, :]


class Scatter:
    def __init__(self, me, arrays, pieces, width, n, fsdp):
        self.n = n
        near, core, mid, self.far = axes_bits(n, fsdp)
        bits = near + [mid]
        self.paths = [bits, bits[::-1]]
        self.heights = [arrays[i].shape[1] for i, _ in pieces]
        orders = [[core] + path + self.far for path in self.paths]
        send, keep = order_blocks(n, orders, pieces, width, arrays)(me, *arrays)[::-1]
        self.send, self.keep = [send], [keep]
        self.hops = [[core]] + list(zip(*self.paths)) + [[b] for b in self.far]
        self.at = 0

    def start(self):
        self.got = [swap(v, 1 << b, self.n) for v, b in zip(self.send, self.hops[self.at])]
        self.at += 1

    def add(self):
        after = self.hops[self.at : self.at + 1]
        got = add_blocks(self.keep, self.got, bool(after) and len(after[0]) == 1)
        if not after:
            self.total = got[0]
        else:
            k = len(got) // 2
            self.keep, self.send = got[:k], got[k:]

    def end(self, x):
        x, *self.got = tie(x, *self.got)
        return x

    def ready(self, x):
        x, *self.send = tie(x, *self.send)
        self.start()
        return x

    def rest(self):
        self.add()
        while self.at < len(self.hops):
            self.start()
            self.add()
        out = []
        at = 0
        for h in self.heights:
            out.append(self.total[at : at + h])
            at += h
        return out


def body(n, fsdp, *args):
    (coarse, medium, fine, clip_counts, frame_counts, reduce_one, spatial_one, expand_one,
     shortcut_one, reduce_two, excite_down, excite_up, temporal_mix, expand_two, norm_params,
     motion_kernel, cot_c, cot_m, cot_f) = args
    near, core, mid, far = axes_bits(n, fsdp)

    def gather(w):
        return lax.all_gather(w.astype(BF16), AXES, axis=0, tiled=True)

    def flat(w):
        v = w.reshape(-1)
        return jnp.pad(v, (0, -v.size % MID)).reshape(-1, MID)

    def flat_back(got, w):
        return got.reshape(n, -1)[:, : w.size].reshape((n,) + w.shape)

    alive = (jnp.arange(4)[None, :] < frame_counts[0][:, None]) & (clip_counts[0][:, None] > 0)
    alive = alive.astype(F32)
    later = jnp.pad(alive[:, 1:], ((0, 0), (0, 1)))
    alive_slots = alive.reshape(12)
    later_slots = later.reshape(12)
    mask = (jnp.asarray(SPREAD) @ alive_slots)[:, None]
    per_group = jnp.sum(alive, axis=1)
    tables = [jnp.asarray(t, BF16) for t in PHASES]
    tables_t = [jnp.asarray(t.T, BF16) for t in PHASES]
    clips = [coarse, medium, fine]

    m128 = jnp.broadcast_to(mask, (R, 128))
    scale = later_slots / jnp.asarray(NPIX)
    scale = jnp.broadcast_to(jnp.pad(scale, (0, 4))[:, None], (16, SQUEEZE))
    table = jnp.asarray(TABLE, BF16)
    table_t = jnp.asarray(TABLE.T, BF16)
    spread = jnp.asarray(SPREAD3, BF16)
    me = lax.axis_index(AXES).astype(jnp.int32).reshape(1)
    small = jnp.concatenate([flat(norm_params), jnp.pad(per_group, (0, MID - 3))[None]], axis=0)
    ga = Gather([reduce_one, small], n, fsdp)
    gb_ = Gather([spatial_one], n, fsdp)
    gc_ = Gather([shortcut_one, expand_one], n, fsdp)
    tall = ga.x.shape[0]
    both = Gather([jnp.concatenate([ga.x, gb_.x], axis=0)], n, fsdp)
    both.first()
    xph = run_split(alive_slots, clips, tables)
    *both.hops, xph = tie(*both.hops, xph)
    xph, *late = tie(xph, reduce_two, excite_down, excite_up, temporal_mix, expand_two)
    narrow = [late[0], flat(late[1]), flat(late[2]), flat(late[3])]
    rows = [v.shape[0] for v in narrow]
    narrow = jnp.concatenate(narrow, axis=0)
    got = gather(jnp.pad(narrow, ((0, -narrow.shape[0] % 16), (0, 0))))
    we2 = gather(late[4])
    ga.hops = [v[:tall] for v in both.hops]
    gb_.hops = [v[tall:] for v in both.hops]
    ga.second()
    gb_.split()
    gb_.hop(0)
    ga.third()
    w1, norms = ga.finish(me)
    norms = norms.reshape(n, -1, MID)
    counts = jnp.sum(norms[:, -1, :3].astype(F32), axis=0)
    cnt = jnp.sum(counts * np.array([q * q for q in SIDES], np.float32)).reshape(1)
    norms = flat_back(norms[:, :-1], norm_params).transpose(1, 0, 2).reshape(2, -1).astype(F32)
    edges = [0, 512, 1024, 3072, 5120, 5632, 6144, 8192]
    gb = [norms[:, edges[k] : edges[k + 1]] for k in range(7)]

    for k in range(1, len(gb_.paths[0])):
        w1, *gb_.got = tie(w1, *gb_.got)
        gb_.land()
        w1, *gb_.planes = tie(w1, *gb_.planes)
        gb_.hop(k)
    w1, gc_.x = tie(w1, gc_.x)
    gc_.first()
    a1, p0 = run_enter(n, xph, w1)
    p0, *rest = tie(p0, *gb_.got, *gc_.hops)
    gb_.got, gc_.hops = rest[:2], rest[2:]
    gb_.land()
    gc_.split()
    p0, *rest = tie(p0, *gb_.planes, *gc_.planes)
    gb_.planes, gc_.planes = rest[:2], rest[2:]
    gb_.third()
    gc_.hop(0)
    s0 = exchange(p0)
    wsp, = gb_.finish(me)
    s0, wsp, cnt, gb[0], *gc_.got = tie(s0, wsp, cnt, gb[0], *gc_.got)
    for k in range(1, len(gc_.paths[0])):
        wsp, *gc_.got = tie(wsp, *gc_.got)
        gc_.land()
        wsp, *gc_.planes = tie(wsp, *gc_.planes)
        gc_.hop(k)
    im, a2, p1 = run_conv_forward(n, cnt, s0, gb[0], m128, a1, wsp)
    s1 = exchange(p1)
    s1, *gc_.got = tie(s1, *gc_.got)
    gc_.land()
    gc_.third()
    wsk, we1 = gc_.finish(me)
    h2, a3, ap, p2 = run_expand_pair(cnt, s1, gb[1], m128, a2, we1, xph, wsk)
    s23, got = allsum_wide(p2, n, fsdp, (got,))
    got = got.reshape(n, -1, MID)
    w2 = got[:, : rows[0]].reshape(C_OUT, MID)
    at = rows[0]
    wdown = flat_back(got[:, at : at + rows[1]], excite_down).reshape(MID, SQUEEZE)
    at += rows[1]
    wup = flat_back(got[:, at : at + rows[2]], excite_up)
    wup = wup.transpose(1, 0, 2).reshape(SQUEEZE, MID).astype(F32)
    at += rows[2]
    wmix = flat_back(got[:, at : at + rows[3]], temporal_mix)
    wmix = wmix.transpose(1, 0, 2).reshape(3, 9 * GROUP, GROUP)
    wmix_t = wmix.reshape(3, 9, GROUP, GROUP).transpose(0, 1, 3, 2).reshape(3, 9 * GROUP, GROUP)
    y1, y1_low, b1, p4 = run_joint_norm(n, cnt, s23, gb[2], gb[3], m128, a3, ap, w2)
    s4 = exchange(p4)
    z, z_low, mixed, mix_im, sig, pooled, wnext, p5 = run_mix_forward(
        n, cnt, s4, gb[4], m128, wdown, wup, motion_kernel, scale, table, spread, b1, wmix
    )
    s5 = exchange(p5)
    w, b3, p6 = run_expand_last(cnt, s5, gb[5], m128, mixed, we2)
    s6 = exchange_wide(p6, n, fsdp)
    o_c, o_m, o_f, g6, p6 = run_last_norm(cnt, s6, gb[6], m128, b3, y1, (cot_c, cot_m, cot_f))

    t6 = exchange_wide(p6, n, fsdp)
    ge2, g5, p5 = run_last_back(n, cnt, t6, s6, gb[6], m128, s5, gb[5], g6, b3, w, we2, mixed)
    t5 = exchange(p5)
    g4, gmix, gkernel, gdown, gup, p4 = run_mix_backward(
        n, cnt,
        (t5, s5, gb[5], m128, sig, pooled, wnext, wup, motion_kernel, scale, table_t, spread,
         wdown, s4, gb[4]),
        g5, mixed, mix_im, wmix_t, z, z_low, b1,
    )
    t4 = exchange(p4)
    gr2, gj, pj = run_joint_back(
        cnt, (t4, s4, gb[4], s23, gb[2], gb[3], m128, gkernel), g4, b1, y1_low, w2, g6, a3, ap
    )

    gmix = gmix.reshape(27, n, GROUP * GROUP // n).transpose(1, 0, 2).reshape(n, -1)
    gup = gup.reshape(SQUEEZE, n, MID // n).transpose(1, 0, 2).reshape(n, -1)
    thin = jnp.concatenate([gmix, gdown.reshape(n, -1).astype(BF16), gup.astype(BF16)], axis=1)
    thin = jnp.pad(thin, ((0, 0), (0, -thin.shape[1] % (16 * MID)))).reshape(n, -1, MID)

    def blocks(v):
        return rows16(v.reshape(n, -1, v.shape[-1]))

    starts = list(range(0, C_OUT, MID))
    tj, gr2, ge2, thin = allsum_wide(pj, n, fsdp, (gr2, ge2, thin))
    ra = Scatter(
        me, [blocks(gr2), thin, blocks(ge2)], [(0, 0), (1, 0)] + [(2, c) for c in starts], MID,
        n, fsdp,
    )
    ra.start()
    ra.add()
    tj = ra.ready(tj)
    ge1, gsk, d3, g1, p1 = run_expand_back(
        n, cnt, (tj, s23, gb[2], gb[3], m128, s1, gb[1]), gj, a3, ap, h2, xph, we1, a2
    )
    p1 = ra.end(p1)
    p1, ge1, gsk = tie(p1, ge1, gsk)
    t1 = exchange(p1)
    ra.add()
    rb = Scatter(
        me, [blocks(ge1), blocks(gsk)], [(i, c) for i in range(2) for c in starts], MID, n, fsdp
    )
    t1 = rb.ready(ra.ready(t1))
    d1, g0, p0 = run_conv_back(
        n, cnt, (t1, s1, gb[1], s0, gb[0], m128), g1, a2, wsp, a1
    )
    p0 = rb.end(ra.end(p0))
    p0, d1 = tie(p0, d1)
    t0 = exchange(p0)
    gsp = run_spatial_grad(d1, im)
    rc = Scatter(me, [blocks(gsp)], [(0, 0)], MID, n, fsdp)
    rb.add()
    t0 = rb.ready(rc.ready(t0))
    d0, gr1 = run_first_grads(cnt, (t0, s0, gb[0], m128), g0, a1, xph)
    d0 = rc.end(d0)
    rc.add()
    d0 = rc.ready(d0)
    gr1 = blocks(gr1)
    gr1 = gr1.reshape(n // (2 * fsdp), 2, fsdp, -1, MID)
    side = (me[0] >> core) & 1
    kept = lax.dynamic_index_in_dim(gr1, side, 1, keepdims=False)
    sent = lax.dynamic_index_in_dim(gr1, 1 - side, 1, keepdims=False)
    gr1 = (kept.astype(F32) + swap(sent, 1 << core, n).astype(F32)).astype(BF16)
    groups = [[i for i in range(n) if (i >> core) & 1 == k] for k in range(2)]
    got = lax.all_to_all(
        gr1.reshape(n // 2, -1, MID), AXES, 0, 0, axis_index_groups=groups, tiled=True
    )
    gin = list(run_input_grads(m128, tables_t, d0, d3, w1, wsk))
    gin[0] = rc.end(rb.end(gin[0]))
    rc.add()
    rb.add()
    ra.add()
    gin[0] = ra.ready(rb.ready(rc.ready(gin[0])))
    *rc.got, rb.got[0], ra.got[0] = tie(*rc.got, rb.got[0], ra.got[0])
    rc.add()
    rc.start()
    rb.add()
    rb.start()
    ra.add()
    ra.start()
    *rc.got, t0, t1, t4, t5, t6, tj, o_m, o_f = tie(*rc.got, t0, t1, t4, t5, t6, tj, o_m, o_f)
    rc.add()
    rc.start()
    *rc.got, got = tie(*rc.got, got)
    gr1 = jnp.sum(got.astype(F32), axis=0)[: reduce_one.shape[0]]
    second = ra.rest()
    gsp = rc.rest()[0][: spatial_one.shape[0]]
    first = rb.rest()

    def wide_back(parts, like_):
        return jnp.concatenate([p[: like_.shape[0]] for p in parts], axis=1)

    thin = second[1].reshape(-1)
    s1_ = temporal_mix.size
    s2_ = s1_ + excite_down.size
    s3_ = s2_ + excite_up.size

    gkernel = tj[:, 12:].reshape(16, 128)[:9, :SQUEEZE]
    gnorm = call(norm_rows, [like((128, 128))], 6, scalars=0)(t0, t1, tj, t4, t5, t6)[0]
    gnorm = lax.dynamic_slice_in_dim(gnorm.reshape(2, 8192), me[0] * (8192 // n), 8192 // n, 1)
    return (
        o_c, o_m, o_f, gin[0], gin[1], gin[2],
        gr1,
        gsp,
        wide_back(first[:4], expand_one),
        wide_back(first[4:], shortcut_one),
        second[0][: reduce_two.shape[0]],
        thin[s1_:s2_].reshape(excite_down.shape),
        thin[s2_:s3_].reshape(excite_up.shape),
        thin[:s1_].reshape(temporal_mix.shape),
        wide_back(second[2:], expand_two),
        gnorm,
        gkernel,
    )


def solution(mesh):
    n = mesh.shape["dp"] * mesh.shape["fsdp"]
    rows = P(AXES, None)
    cols = P(None, AXES)
    image = P(AXES, None, None, None)
    return jax.shard_map(
        partial(body, n, mesh.shape["fsdp"]),
        mesh=mesh,
        in_specs=(image, image, image, rows, rows, rows, rows, rows, rows, rows, rows, cols, cols,
                  rows, cols, P(), image, image, image),
        out_specs=(image, image, image, image, image, image, rows, rows, rows, rows, rows, rows,
                   cols, cols, rows, cols, P()),
        check_vma=False,
    )
```
